32 devices in a mesh: row: 4 (over y, x), col: 8 (over z, core).
Axes of the slice: x: 2, y: 2, z: 4, core: 2. Of those that a mesh axis runs over, the one named last changes fastest.
Arguments:
- front: float32 [16, 4, 128, 8, 8, 128], P(None, 'row', None, None, 'col'), as said below
- block_slots: int32 [64], replicated, may hold values from 0 to 63, as said below
- rows_first: int32 [39], replicated, may hold values from 4 to 63, as said below
- rows_second: int32 [49], replicated, may hold values from 8 to 63, as said below
Outputs:
- factored: float32 [16, 4, 128, 8, 8, 128], P(None, 'row', None, None, 'col')
The draws below stay inside these ranges and needn't reach their ends.
Inputs may be any that keep to these rules, and one draw needn't show every extreme that they name: front is symmetric, and its square on the slots of blocks 0 to 7 is positive definite. `block_slots`: each slot appears once. `rows_second`: 49 distinct block numbers in increasing order; 8 and 63 are always among them. `rows_first`: 4, 5, 6, 7, then 39 - 4 distinct block numbers in increasing order, all of them in rows_second, 63 always among them.
All inputs are finite; a program needn't handle non-finite values.
Results may differ from the reference program's by a relative error of at most 0.00028.
Values sent between devices are 32-bit elements; how exact they have to be, the bound alone decides.
No kernel may reach another device: no remote copies, remote signals or barrier semaphores. Data moves between devices by JAX's collectives and lax.ppermute only.
A program may use at most 128 MiB of HBM per device.

```python
import jax
import jax.numpy as jnp
from jax import lax

BS = 128
PB = 4
NB = 64
RB = 16
CB = 8
R2 = 49
R1 = 39


def block_order(key):
    return jax.random.permutation(jax.random.fold_in(key, 11), NB).astype(jnp.int32)


def row_lists(key):
    interior = jax.random.permutation(jax.random.fold_in(key, 23), NB - 10).astype(jnp.int32) + 9
    ends = jnp.array([8, NB - 1], dtype=jnp.int32)
    second_list = jnp.sort(jnp.concatenate([ends, interior[:R2 - 2]]))
    first_extra = jnp.sort(jnp.concatenate([ends[1:], interior[:R1 - 5]]))
    first_list = jnp.concatenate([jnp.arange(4, 8, dtype=jnp.int32), first_extra])
    return (first_list, second_list)


def draw_block_slots(key, part):
    return block_order(key)


def draw_rows_first(key, part):
    return row_lists(key)[0]


def draw_rows_second(key, part):
    return row_lists(key)[1]


def draw_front(key, part):
    matrix_order = NB * BS
    entries = jax.random.truncated_normal(jax.random.fold_in(key, 31), -4.0, 4.0, (matrix_order, matrix_order), jnp.float32)
    symmetric = (entries + entries.T) * 0.70710678
    order = block_order(key)
    block_ids = jnp.arange(NB, dtype=jnp.int32)
    first_mask = jnp.any(block_ids[:, None] == order[None, :PB], axis=1).astype(jnp.float32)
    second_mask = jnp.any(block_ids[:, None] == order[None, PB:2 * PB], axis=1).astype(jnp.float32)
    first_cells = jnp.repeat(first_mask, BS)
    second_cells = jnp.repeat(second_mask, BS)
    cross = first_cells[:, None] * second_cells[None, :]
    cross = cross + cross.T
    symmetric = symmetric * (1.0 - 0.85 * cross)
    same_panel = first_cells[:, None] * first_cells[None, :] + second_cells[:, None] * second_cells[None, :]
    symmetric = symmetric + 0.03 * same_panel
    diagonal_boost = jax.random.uniform(jax.random.fold_in(key, 37), (matrix_order,), jnp.float32, 56.0, 72.0)
    diagonal_boost = diagonal_boost * (first_cells + second_cells)
    positions = jnp.arange(matrix_order, dtype=jnp.int32)
    matrix = symmetric.at[positions, positions].add(diagonal_boost)
    return matrix.reshape(RB, NB // RB, BS, CB, NB // CB, BS)


def setup_inputs(seed: int = 0) -> dict:
    splits = jax.random.split(jax.random.key(seed), 5)
    return {
        "front": draw_front(jax.random.fold_in(splits[4], 71), 0),
        "block_slots": draw_block_slots(jax.random.fold_in(splits[4], 71), 0),
        "rows_first": draw_rows_first(jax.random.fold_in(splits[4], 71), 0),
        "rows_second": draw_rows_second(jax.random.fold_in(splits[4], 71), 0),
    }


def block_indices(slot_list):
    offsets = jnp.arange(BS, dtype=jnp.int32)
    return (slot_list.astype(jnp.int32)[:, None] * BS + offsets[None, :]).reshape(-1)

def reference(front, block_slots, rows_first, rows_second):
    matrix_order = NB * BS
    matrix = front.reshape(matrix_order, matrix_order)
    identity = jnp.eye(PB * BS, dtype=jnp.float32)
    for panel_index, row_list in ((0, rows_first), (1, rows_second)):
        col_index = block_indices(block_slots[PB * panel_index:PB * (panel_index + 1)])
        row_index = block_indices(block_slots[row_list])
        diag_block = matrix[col_index[:, None], col_index[None, :]]
        lower_factor = jnp.linalg.cholesky(diag_block)
        inverse = lax.linalg.triangular_solve(lower_factor, identity, left_side=True, lower=True)
        row_panel = matrix[row_index[:, None], col_index[None, :]]
        solved = jnp.dot(row_panel, inverse.T, precision=lax.Precision.HIGHEST)
        spread = jnp.zeros((matrix_order, PB * BS), dtype=jnp.float32).at[row_index].set(solved)
        matrix = matrix - jnp.dot(spread, spread.T, precision=lax.Precision.HIGHEST)
        matrix = matrix.at[row_index[:, None], col_index[None, :]].set(solved)
        matrix = matrix.at[col_index[:, None], col_index[None, :]].set(lower_factor)
    return matrix.reshape(front.shape)
```

```python
import jax
import jax.numpy as jnp
from jax import lax
from jax.experimental import pallas as pl
from jax.experimental.pallas import tpu as pltpu
from jax.sharding import PartitionSpec as P

BS = 128
PB = 4
NC = 2 * PB
STEP = 4
HIGHEST = lax.Precision.HIGHEST


def lane_copy(tile, lane):
    return jnp.broadcast_to(tile[:, lane : lane + 1], tile.shape)


def row_copy(tile, row):
    return jnp.broadcast_to(tile[row : row + 1, :], tile.shape)


def factor_block(block):
    tiles = BS // 8
    sub = lax.broadcasted_iota(jnp.int32, (8, BS), 0)
    lanes = lax.broadcasted_iota(jnp.int32, (8, BS), 1)
    left = [block[8 * i : 8 * i + 8, :] for i in range(tiles)]
    right = [jnp.where(lanes == sub + 8 * i, 1.0, 0.0).astype(jnp.float32) for i in range(tiles)]
    upper = []
    inverse = []
    for j in range(0, BS, STEP):
        g, o = divmod(j, 8)
        if o == 0:
            upper_tile = jnp.zeros((8, BS), jnp.float32)
            inverse_tile = jnp.zeros((8, BS), jnp.float32)
        rows = [row_copy(left[g], o + s) for s in range(STEP)]
        extra = [row_copy(right[g], o + s) for s in range(STEP)]
        first = g if o + STEP < 8 else g + 1
        cols = {i: [lane_copy(left[i], j + s) for s in range(STEP)] for i in range(first, tiles)}
        pivot = [[lane_copy(rows[s], j + t) if t >= s else None for t in range(STEP)] for s in range(STEP)]
        ratio = [[None] * STEP for _ in range(STEP)]
        recip = []
        for s in range(STEP):
            inv = 1.0 / pivot[s][s]
            recip.append(inv)
            for t in range(s + 1, STEP):
                ratio[s][t] = pivot[s][t] * inv
            for t in range(s + 1, STEP):
                for u in range(t, STEP):
                    pivot[t][u] = pivot[t][u] - ratio[s][t] * pivot[s][u]
                rows[t] = rows[t] - ratio[s][t] * rows[s]
                extra[t] = extra[t] - ratio[s][t] * extra[s]
        for s in range(STEP):
            scale = lax.rsqrt(pivot[s][s])
            scale = scale * (1.5 - 0.5 * pivot[s][s] * scale * scale)
            here = sub == o + s
            upper_tile = jnp.where(here, rows[s] * scale, upper_tile)
            inverse_tile = jnp.where(here, extra[s] * scale, inverse_tile)
        if o + STEP == 8:
            upper.append(jnp.where(lanes >= sub + 8 * g, upper_tile, 0.0))
            inverse.append(jnp.where(lanes <= sub + 8 * g, inverse_tile, 0.0))
        for s in reversed(range(STEP)):
            rows[s] = rows[s] * recip[s]
            extra[s] = extra[s] * recip[s]
            for t in range(s + 1, STEP):
                rows[s] = rows[s] - ratio[s][t] * rows[t]
                extra[s] = extra[s] - ratio[s][t] * extra[t]
        for i in range(first, tiles):
            less = cols[i][0] * rows[0]
            less_extra = cols[i][0] * extra[0]
            for s in range(1, STEP):
                less = less + cols[i][s] * rows[s]
                less_extra = less_extra + cols[i][s] * extra[s]
            if i == g:
                below = sub >= o + STEP
                left[i] = jnp.where(below, left[i] - less, left[i])
                right[i] = jnp.where(below, right[i] - less_extra, right[i])
            else:
                left[i] = left[i] - less
                right[i] = right[i] - less_extra
    return jnp.concatenate(upper, axis=0), jnp.concatenate(inverse, axis=0)


def lower_index(i, j):
    return i * (i + 1) // 2 + j


def dot_nt(a, b):
    return lax.dot_general(a, b, (((1,), (1,)), ((), ())), precision=HIGHEST, preferred_element_type=jnp.float32)


def dot_nn(a, b):
    return lax.dot_general(a, b, (((1,), (0,)), ((), ())), precision=HIGHEST, preferred_element_type=jnp.float32)


def split(x):
    high = x.astype(jnp.bfloat16)
    return high, (x - high.astype(jnp.float32)).astype(jnp.bfloat16)


def square_kernel(diag_ref, lower_ref, high_ref, low_ref, work, acc, inv, low_blk, inv_blk):
    lower_ref[...] = jnp.zeros_like(lower_ref)
    inv[...] = jnp.zeros_like(inv)
    acc[...] = jnp.zeros_like(acc)
    for i in range(NC):
        for j in range(i + 1):
            work[i * BS : (i + 1) * BS, j * BS : (j + 1) * BS] = diag_ref[lower_index(i, j)]

    @pl.loop(0, NC)
    def _(k):
        at = pl.ds(pl.multiple_of(k * BS, BS), BS)
        upper, inverse = factor_block(work[at, at])
        low_blk[...] = upper.T
        inv_blk[...] = inverse
        lower_ref[at, at] = low_blk[...]
        inv[at, at] = inverse
        for n in range(NC):
            @pl.when(k == n)
            def _(n=n):
                here = slice(n * BS, (n + 1) * BS)
                after = slice((n + 1) * BS, NC * BS)
                if n > 0:
                    inv[here, : n * BS] = dot_nn(inv_blk[...], acc[here, : n * BS])
                if n + 1 < NC:
                    lower_ref[after, here] = dot_nt(work[after, here], inv_blk[...])
                    for i in range(n + 1, NC):
                        rows = slice(i * BS, (i + 1) * BS)
                        cols = slice((n + 1) * BS, (i + 1) * BS)
                        done = slice(0, (n + 1) * BS)
                        panel = lower_ref[rows, here]
                        work[rows, cols] = work[rows, cols] - dot_nt(panel, lower_ref[cols, here])
                        acc[rows, done] = acc[rows, done] - dot_nn(panel, inv[here, done])

    high, low = split(inv[...])
    high_ref[...] = high
    low_ref[...] = low


def factor_square(diag):
    size = NC * BS
    return pl.pallas_call(
        square_kernel,
        out_shape=(
            jax.ShapeDtypeStruct((size, size), jnp.float32),
            jax.ShapeDtypeStruct((size, size), jnp.bfloat16),
            jax.ShapeDtypeStruct((size, size), jnp.bfloat16),
        ),
        in_specs=[pl.BlockSpec(memory_space=pltpu.VMEM)],
        out_specs=(pl.BlockSpec(memory_space=pltpu.VMEM),) * 3,
        scratch_shapes=[
            pltpu.VMEM((size, size), jnp.float32),
            pltpu.VMEM((size, size), jnp.float32),
            pltpu.VMEM((size, size), jnp.float32),
            pltpu.VMEM((BS, BS), jnp.float32),
            pltpu.VMEM((BS, BS), jnp.float32),
        ],
        compiler_params=pltpu.CompilerParams(vmem_limit_bytes=48 * 2**20),
        cost_estimate=pl.CostEstimate(flops=10**10, bytes_accessed=10**7, transcendentals=0),
        name="factor_square",
    )(diag)


def update_kernel(flags, front_ref, rows_ref, cols_ref, lower_ref, high_ref, low_ref, out_ref,
                  panel, col_high, col_low, solved, sol_high, sol_low):
    row_blocks = flags.shape[0]
    size = NC * BS
    half = PB * BS
    width = 2 * BS
    step = pl.program_id(0)
    col_blocks = cols_ref.shape[1]

    def three(dot, a_high, a_low, b_high, b_low):
        kwargs = dict(preferred_element_type=jnp.float32)
        return dot(a_high, b_high, **kwargs) + (dot(a_high, b_low, **kwargs) + dot(a_low, b_high, **kwargs))

    def nt(a, b, **kwargs):
        return lax.dot_general(a, b, (((1,), (1,)), ((), ())), **kwargs)

    def nn(a, b, **kwargs):
        return lax.dot_general(a, b, (((1,), (0,)), ((), ())), **kwargs)

    def masked(tiles, first, second):
        low_part = jnp.concatenate(tiles[:PB], axis=1)
        high_part = jnp.concatenate(tiles[PB:], axis=1)
        zero = jnp.zeros_like(low_part)
        return jnp.concatenate([jnp.where(first, low_part, zero), jnp.where(second, high_part, zero)], axis=1)

    @pl.when(step == 0)
    def _():
        for b in range(col_blocks):
            at = slice(b * BS, (b + 1) * BS)
            raw = masked([cols_ref[c, b] for c in range(NC)], flags[b, 3] != 0, flags[b, 4] != 0)
            high, low = split(raw)
            panel[0, at, :] = high
            panel[1, at, :] = low
        for m in range(0, size, width):
            deep = m + width
            value = three(nt, high_ref[m:deep, :deep], low_ref[m:deep, :deep], panel[0, :, :deep], panel[1, :, :deep])
            if m >= half:
                value = jnp.concatenate(
                    [
                        jnp.where(flags[b, 4] != 0, value[:, b * BS : (b + 1) * BS], 0.0)
                        for b in range(col_blocks)
                    ],
                    axis=1,
                )
            high, low = split(value)
            col_high[m:deep, :] = high
            col_low[m:deep, :] = low

    for k in range(2):
        a = step * 2 + k
        raw = masked([rows_ref[c, k] for c in range(NC)], flags[a, 0] != 0, flags[a, 1] != 0)
        high, low = split(raw)
        sol_high[k * BS : (k + 1) * BS, :] = high
        sol_low[k * BS : (k + 1) * BS, :] = low
    for m in range(0, size, width):
        deep = m + width
        value = three(nt, sol_high[:, :deep], sol_low[:, :deep], high_ref[m:deep, :deep], low_ref[m:deep, :deep])
        if m >= half:
            value = jnp.concatenate(
                [
                    jnp.where(flags[step * 2 + k, 1] != 0, value[k * BS : (k + 1) * BS, :], 0.0)
                    for k in range(2)
                ],
                axis=0,
            )
        solved[:, m:deep] = value
    high, low = split(solved[...])
    sol_high[...] = high
    sol_low[...] = low
    for b in range(0, col_blocks, 2):
        at = slice(b * BS, (b + 2) * BS)
        value = three(nn, sol_high[...], sol_low[...], col_high[:, at], col_low[:, at])
        for s in range(2):
            out_ref[:, b + s, :] = front_ref[:, b + s, :] - value[:, s * BS : (s + 1) * BS]
    for b in range(col_blocks):
        j = flags[b, 5]

        @pl.when(j >= 0)
        def _(b=b, j=j):
            at = pl.ds(pl.multiple_of(j * BS, BS), BS)
            for k in range(2):
                a = step * 2 + k
                rows = slice(k * BS, (k + 1) * BS)
                listed = flags[a, 0] * (j < PB).astype(jnp.int32) + flags[a, 1] * (j >= PB).astype(jnp.int32)
                own = flags[a, 2]

                @pl.when(listed != 0)
                def _():
                    out_ref[rows, b, :] = solved[rows, at]

                @pl.when(jnp.logical_and(own >= 0, own // PB == j // PB))
                def _():
                    source = pl.ds(pl.multiple_of(own * BS, BS), BS)
                    out_ref[rows, b, :] = lower_ref[source, at]


def update_front(flags, front, rows, cols, lower, high, low):
    row_blocks = rows.shape[1]
    col_blocks = cols.shape[1]
    size = NC * BS
    whole = pl.BlockSpec(memory_space=pltpu.VMEM)
    flops = 3 * 2 * row_blocks * BS * size * (col_blocks * BS + size)
    return pl.pallas_call(
        update_kernel,
        out_shape=jax.ShapeDtypeStruct(front.shape, jnp.float32),
        grid_spec=pltpu.PrefetchScalarGridSpec(
            num_scalar_prefetch=1,
            grid=(row_blocks // 2,),
            in_specs=[
                pl.BlockSpec((2 * BS, col_blocks, BS), lambda i, f: (i, 0, 0)),
                pl.BlockSpec((NC, 2, BS, BS), lambda i, f: (0, i, 0, 0)),
                whole,
                whole,
                whole,
                whole,
            ],
            out_specs=pl.BlockSpec((2 * BS, col_blocks, BS), lambda i, f: (i, 0, 0)),
            scratch_shapes=[
                pltpu.VMEM((2, col_blocks * BS, size), jnp.bfloat16),
                pltpu.VMEM((size, col_blocks * BS), jnp.bfloat16),
                pltpu.VMEM((size, col_blocks * BS), jnp.bfloat16),
                pltpu.VMEM((2 * BS, size), jnp.float32),
                pltpu.VMEM((2 * BS, size), jnp.bfloat16),
                pltpu.VMEM((2 * BS, size), jnp.bfloat16),
            ],
        ),
        compiler_params=pltpu.CompilerParams(vmem_limit_bytes=56 * 2**20),
        cost_estimate=pl.CostEstimate(flops=flops, bytes_accessed=4 * 10**7, transcendentals=0),
        name="update_front",
    )(flags, front, rows, cols, lower, high, low)


def exchange(value, grid, flip):
    grid_rows, grid_cols = grid
    pairs = []
    for p in range(grid_rows):
        for q in range(grid_cols):
            to_p, to_q = flip(p, q)
            pairs.append((p * grid_cols + q, to_p * grid_cols + to_q))
    return lax.ppermute(value, ("row", "col"), pairs)


def sum_everywhere(value, grid, own_row, own_col):
    if grid != (4, 8):
        return lax.psum(value, ("row", "col"))
    levels = [
        (lambda p, q: (p, q ^ 1), own_col % 2),
        (lambda p, q: (p ^ 2, q), own_row // 2),
        (lambda p, q: (p ^ 1, q), own_row % 2),
        (lambda p, q: (p, q ^ 2), own_col // 2 % 2),
        (lambda p, q: (p, q ^ 4), own_col // 4),
    ]
    shape = value.shape
    value = value.reshape(-1, shape[-1])
    for flip, bit in levels:
        half = value.shape[0] // 2
        first, second = value[:half], value[half:]
        keep = jnp.where(bit == 0, first, second)
        send = jnp.where(bit == 0, second, first)
        value = keep + exchange(send, grid, flip)
    for flip, bit in reversed(levels):
        other = exchange(value, grid, flip)
        first = jnp.where(bit == 0, value, other)
        second = jnp.where(bit == 0, other, value)
        value = jnp.concatenate([first, second], axis=0)
    return value.reshape(shape)


def column_panel(rows, grid, own_row, own_col):
    grid_rows, grid_cols = grid
    ratio = grid_cols // grid_rows
    shape = rows.shape
    parts = rows.reshape(shape[0], shape[1] // ratio, ratio, shape[2], shape[3])
    mine = lax.dynamic_index_in_dim(parts, own_col // grid_rows, 2, keepdims=False)
    root = own_col % grid_rows
    if grid != (4, 8):
        return lax.psum(jnp.where(own_row == root, mine, jnp.zeros_like(mine)), "row")
    down = [
        ((q % 4) * 8 + q, ((q % 4) ^ 2) * 8 + q) for q in range(8)
    ]
    received = lax.ppermute(mine, ("row", "col"), down)
    mine = jnp.where(own_row == root, mine, received)
    across = []
    for q in range(8):
        for y in range(2):
            x = q % 2
            across.append(((y * 2 + x) * 8 + q, (y * 2 + 1 - x) * 8 + q))
    received = lax.ppermute(mine, ("row", "col"), across)
    return jnp.where(own_row % 2 == own_col % 2, mine, received)


def block_flags(slots, listed_one, listed_two, diag_slots):
    one = jnp.any(slots[:, None] == listed_one[None, :], axis=1).astype(jnp.int32)
    two = jnp.any(slots[:, None] == listed_two[None, :], axis=1).astype(jnp.int32)
    order = jnp.arange(1, NC + 1, dtype=jnp.int32)
    place = jnp.sum(jnp.where(slots[:, None] == diag_slots[None, :], order[None, :], 0), axis=1) - 1
    return jnp.stack([one, two, place], axis=1)


def on_device(front, block_slots, rows_first, rows_second):
    grid_rows = lax.axis_size("row")
    grid_cols = lax.axis_size("col")
    grid = (grid_rows, grid_cols)
    own_row = lax.axis_index("row")
    own_col = lax.axis_index("col")
    row_blocks, col_blocks = front.shape[0], front.shape[3]
    diag_slots = block_slots[:NC]
    listed_one = block_slots[rows_first]
    listed_two = block_slots[rows_second]
    row_slots = jnp.arange(row_blocks, dtype=jnp.int32) * grid_rows + own_row
    col_slots = jnp.arange(col_blocks, dtype=jnp.int32) * grid_cols + own_col
    flags_row = block_flags(row_slots, listed_one, listed_two, diag_slots)
    flags_col = block_flags(col_slots, listed_one, listed_two, diag_slots)
    flags_col = jnp.pad(flags_col, ((0, row_blocks - col_blocks), (0, 0)))
    flags = jnp.concatenate([flags_row, flags_col], axis=1)

    local = front.reshape(row_blocks, BS, col_blocks, BS)
    pieces = []
    for c in range(NC):
        piece = lax.dynamic_index_in_dim(local, diag_slots[c] // grid_cols, 2, keepdims=False)
        pieces.append(jnp.where(diag_slots[c] % grid_cols == own_col, piece, jnp.zeros_like(piece)))
    pieces = jnp.stack(pieces, axis=0)
    blocks = []
    for i in range(NC):
        part = lax.dynamic_index_in_dim(pieces, diag_slots[i] // grid_rows, 1, keepdims=False)[: i + 1]
        blocks.append(jnp.where(diag_slots[i] % grid_rows == own_row, part, jnp.zeros_like(part)))
    diag = sum_everywhere(jnp.concatenate(blocks, axis=0), grid, own_row, own_col)
    lower, high, low = factor_square(diag)
    rows = lax.psum(pieces, "col")
    cols = column_panel(rows, grid, own_row, own_col)
    flat = front.reshape(row_blocks * BS, col_blocks, BS)
    return update_front(flags, flat, rows, cols, lower, high, low).reshape(front.shape)


def solution(mesh):
    placed = (P(None, "row", None, None, "col", None), P(), P(), P())
    return jax.shard_map(
        on_device,
        mesh=mesh,
        in_specs=placed,
        out_specs=P(None, "row", None, None, "col", None),
        check_vma=False,
    )
```

```python
import functools

import jax
import jax.numpy as jnp
from jax import lax
from jax.experimental import pallas as pl
from jax.experimental.pallas import tpu as pltpu
from jax.sharding import PartitionSpec as P

BS = 128
PB = 4
NC = 2 * PB
STEP = 4
SHORT = 8
LONG = 10
HIGHEST = lax.Precision.HIGHEST
ANY = pl.BlockSpec(memory_space=pl.ANY)
VMEM = pl.BlockSpec(memory_space=pltpu.VMEM)
SMEM = pl.BlockSpec(memory_space=pltpu.SMEM)


def lane_copy(tile, lane):
    return jnp.broadcast_to(tile[:, lane : lane + 1], tile.shape)


def row_copy(tile, row):
    return jnp.broadcast_to(tile[row : row + 1, :], tile.shape)


def factor_block(block):
    tiles = BS // 8
    sub = lax.broadcasted_iota(jnp.int32, (8, BS), 0)
    lanes = lax.broadcasted_iota(jnp.int32, (8, BS), 1)
    left = [block[8 * i : 8 * i + 8, :] for i in range(tiles)]
    right = [jnp.where(lanes == sub + 8 * i, 1.0, 0.0).astype(jnp.float32) for i in range(tiles)]
    upper = []
    inverse = []
    for j in range(0, BS, STEP):
        g, o = divmod(j, 8)
        if o == 0:
            upper_tile = jnp.zeros((8, BS), jnp.float32)
            inverse_tile = jnp.zeros((8, BS), jnp.float32)
        rows = [row_copy(left[g], o + s) for s in range(STEP)]
        extra = [row_copy(right[g], o + s) for s in range(STEP)]
        first = g if o + STEP < 8 else g + 1
        cols = {i: [lane_copy(left[i], j + s) for s in range(STEP)] for i in range(first, tiles)}
        pivot = [[lane_copy(rows[s], j + t) if t >= s else None for t in range(STEP)] for s in range(STEP)]
        ratio = [[None] * STEP for _ in range(STEP)]
        recip = []
        for s in range(STEP):
            inv = 1.0 / pivot[s][s]
            recip.append(inv)
            for t in range(s + 1, STEP):
                ratio[s][t] = pivot[s][t] * inv
            for t in range(s + 1, STEP):
                for u in range(t, STEP):
                    pivot[t][u] = pivot[t][u] - ratio[s][t] * pivot[s][u]
                rows[t] = rows[t] - ratio[s][t] * rows[s]
                extra[t] = extra[t] - ratio[s][t] * extra[s]
        for s in range(STEP):
            scale = lax.rsqrt(pivot[s][s])
            scale = scale * (1.5 - 0.5 * pivot[s][s] * scale * scale)
            here = sub == o + s
            upper_tile = jnp.where(here, rows[s] * scale, upper_tile)
            inverse_tile = jnp.where(here, extra[s] * scale, inverse_tile)
        if o + STEP == 8:
            upper.append(jnp.where(lanes >= sub + 8 * g, upper_tile, 0.0))
            inverse.append(jnp.where(lanes <= sub + 8 * g, inverse_tile, 0.0))
        for s in reversed(range(STEP)):
            rows[s] = rows[s] * recip[s]
            extra[s] = extra[s] * recip[s]
            for t in range(s + 1, STEP):
                rows[s] = rows[s] - ratio[s][t] * rows[t]
                extra[s] = extra[s] - ratio[s][t] * extra[t]
        for i in range(first, tiles):
            less = cols[i][0] * rows[0]
            less_extra = cols[i][0] * extra[0]
            for s in range(1, STEP):
                less = less + cols[i][s] * rows[s]
                less_extra = less_extra + cols[i][s] * extra[s]
            if i == g:
                below = sub >= o + STEP
                left[i] = jnp.where(below, left[i] - less, left[i])
                right[i] = jnp.where(below, right[i] - less_extra, right[i])
            else:
                left[i] = left[i] - less
                right[i] = right[i] - less_extra
    return jnp.concatenate(upper, axis=0), jnp.concatenate(inverse, axis=0)


def lower_index(i, j):
    return i * (i + 1) // 2 + j


def dot_nt(a, b):
    return lax.dot_general(a, b, (((1,), (1,)), ((), ())), precision=HIGHEST, preferred_element_type=jnp.float32)


def dot_nn(a, b):
    return lax.dot_general(a, b, (((1,), (0,)), ((), ())), precision=HIGHEST, preferred_element_type=jnp.float32)


def split(x):
    high = x.astype(jnp.bfloat16)
    return high, (x - high.astype(jnp.float32)).astype(jnp.bfloat16)


def place(count, core, block):
    half = count // 2
    return (block // half) == core, block % half


def start_kernel(slots, first, second, front_ref, wide_ref, flags, plan, rows_out, keep_one, send_one, keep_two,
                 send_two, mine, theirs_a, theirs_b, zero, zero_wide, sems):
    row_blocks, _, col_blocks = wide_ref.shape[:3]
    grid_rows, grid_cols, depth = 4, 8, 4
    own_row = lax.axis_index("row")
    own_col = lax.axis_index("col")
    core = own_col % 2
    z = own_col // 2
    zero[...] = jnp.zeros_like(zero)
    zero_wide[...] = jnp.zeros_like(zero_wide)
    slot = [slots[i] for i in range(NC)]
    waits = []
    used = [0]

    def copy(condition, source, target):
        sem = sems.at[used[0]]
        used[0] += 1

        @pl.when(condition)
        def _():
            pltpu.make_async_copy(source, target, sem).start()

        return sem

    one = NC // 2 * (NC // 2 + 1) // 2
    two = NC * (NC + 1) // 2 - one
    chip = [(slot[c] % grid_cols) // 2 for c in range(NC)]
    here = [chip[c] == z for c in range(NC)]
    rank = []
    for c in range(NC):
        count = jnp.int32(0)
        for d in range(c):
            count = count + (chip[d] == chip[c]).astype(jnp.int32)
        rank.append(count)
    for c in range(NC):
        owned = slot[c] % grid_cols == own_col
        b = slot[c] // grid_cols
        source = front_ref.at[:, core, :, b]
        other = front_ref.at[:, 1 - core, :, b]
        sem = copy(owned, source, mine.at[rank[c]])
        waits.append((owned, mine.at[0], sem))
        near = jnp.logical_and(owned, rank[c] < 2)
        sem = copy(near, other, theirs_a.at[jnp.minimum(rank[c], 1)])
        waits.append((near, theirs_a.at[0], sem))
        far = jnp.logical_and(owned, rank[c] >= 2)
        sem = copy(far, other, theirs_b.at[jnp.maximum(rank[c] - 2, 0)])
        waits.append((far, theirs_b.at[0], sem))
    for i in range(NC):
        for j in range(i + 1):
            block = lower_index(i, j)
            if i < PB:
                count, at, keep, send = one, block, keep_one, send_one
            else:
                count, at, keep, send = two, block - one, keep_two, send_two
            half = count // 2
            a = slot[i] // grid_rows
            b = slot[j] // grid_cols
            owned = jnp.logical_and(slot[i] % grid_rows == own_row, slot[j] % grid_cols == own_col)
            stay = core == at // half
            source = front_ref.at[a // 2, a % 2, :, b]
            index = used[0]
            for target, chosen in ((keep.at[at % half], stay), (send.at[at % half], jnp.logical_not(stay))):
                used[0] = index
                copy(jnp.logical_and(chosen, owned), source, target)
                used[0] = index
                copy(jnp.logical_and(chosen, jnp.logical_not(owned)), zero, target)
            waits.append((None, keep.at[0], sems.at[index]))
    for c in range(NC):
        owned = slot[c] % grid_rows == own_row
        index = used[0]
        copy(owned, wide_ref.at[slot[c] // grid_rows], rows_out.at[c])
        used[0] = index
        copy(jnp.logical_not(owned), zero_wide, rows_out.at[c])
        waits.append((None, rows_out.at[0], sems.at[index]))

    for a in range(row_blocks):
        for f in range(8):
            flags[a, f] = jnp.int32(-1 if f in (2, 5) else 0)
    for c in range(NC):
        @pl.when(slot[c] % grid_rows == own_row)
        def _(c=c):
            flags[slot[c] // grid_rows, 2] = jnp.int32(c)

        @pl.when(slot[c] % grid_cols == own_col)
        def _(c=c):
            flags[slot[c] // grid_cols, 5] = jnp.int32(c)

    for listed, f in ((first, 0), (second, 1)):
        @pl.loop(0, listed.shape[0])
        def _(i, listed=listed, f=f):
            s = slots[listed[i]]

            @pl.when(s % grid_rows == own_row)
            def _():
                flags[s // grid_rows, f] = jnp.int32(1)

            @pl.when(s % grid_cols == own_col)
            def _():
                flags[s // grid_cols, 3 + f] = jnp.int32(1)

    for t in range(LONG):
        for f in range(8):
            plan[t, f] = jnp.int32(0)
    counts = []
    for s in range(depth):
        count = jnp.int32(0)
        for c in range(NC):
            count = count + (chip[c] == s).astype(jnp.int32)
        counts.append(count)
    last = jnp.int32(0)
    for way in range(2):
        order = (lambda s: s) if way == 0 else (lambda s: depth - 1 - s)
        begin = [[None] * depth for _ in range(depth)]
        for at in range(depth - 1):
            for s in range(at, -1, -1):
                if s == at:
                    begin[at][s] = jnp.int32(0)
                else:
                    begin[at][s] = jnp.maximum(
                        begin[at][s + 1] + counts[order(s + 1)], begin[at - 1][s] + 1
                    )
        for at in range(depth - 1):
            for s in range(at + 1):
                count = counts[order(s)]
                last = jnp.maximum(last, jnp.where(count > 0, begin[at][s] + count, 0))
        for at in range(depth):
            @pl.when(z == order(at))
            def _(at=at, begin=begin, order=order, way=way):
                for c in range(NC):
                    for s in range(at + 1):
                        source = chip[c] == order(s)
                        if s == at and at < depth - 1:
                            @pl.when(source)
                            def _(c=c):
                                when = begin[at][at] + rank[c]
                                plan[when, 2 * way] = jnp.where(slot[c] % grid_cols == own_col, 1, 2)
                                plan[when, 2 * way + 1] = rank[c]
                        if s < at:
                            @pl.when(source)
                            def _(c=c, s=s):
                                got = begin[at - 1][s] + rank[c]
                                plan[c, 4] = jnp.int32(2 + way)
                                plan[c, 5] = got
                                if at < depth - 1:
                                    when = begin[at][s] + rank[c]
                                    plan[when, 2 * way] = jnp.int32(3)
                                    plan[when, 2 * way + 1] = got
    for c in range(NC):
        @pl.when(here[c])
        def _(c=c):
            plan[c, 4] = jnp.where(slot[c] % grid_cols == own_col, 0, 1)
            plan[c, 5] = rank[c]
    plan[0, 6] = last

    for condition, target, sem in waits:
        if condition is None:
            pltpu.make_async_copy(target, target, sem).wait()
        else:
            @pl.when(condition)
            def _(target=target, sem=sem):
                pltpu.make_async_copy(target, target, sem).wait()


def start(front, block_slots, rows_first, rows_second):
    row_blocks, col_blocks = front.shape[0], front.shape[3]
    half = row_blocks // 2
    one = PB * (PB + 1) // 2
    two = NC * (NC + 1) // 2 - one
    f32 = lambda *shape: jax.ShapeDtypeStruct(shape, jnp.float32)
    outs = pl.pallas_call(
        start_kernel,
        out_shape=(
            jax.ShapeDtypeStruct((row_blocks, 8), jnp.int32),
            jax.ShapeDtypeStruct((LONG, 8), jnp.int32),
            f32(NC, BS, col_blocks, BS),
            f32(one // 2, BS, 1, BS),
            f32(one // 2, BS, 1, BS),
            f32(two // 2, BS, 1, BS),
            f32(two // 2, BS, 1, BS),
            f32(NC, half, BS, 1, BS),
            f32(2, half, BS, 1, BS),
            f32(NC - 2, half, BS, 1, BS),
        ),
        in_specs=[SMEM, SMEM, SMEM, ANY, ANY],
        out_specs=(SMEM, SMEM) + (ANY,) * 8,
        scratch_shapes=[
            pltpu.VMEM((BS, 1, BS), jnp.float32),
            pltpu.VMEM((BS, col_blocks, BS), jnp.float32),
            pltpu.SemaphoreType.DMA((72,)),
        ],
        name="start",
    )(
        block_slots,
        rows_first,
        rows_second,
        front.reshape(half, 2, BS, col_blocks, 1, BS),
        front.reshape(row_blocks, BS, col_blocks, BS),
    )
    flags, plan, rows = outs[:3]
    flat = [x.reshape(-1, BS) for x in outs[3:7]]
    chunks = [x.reshape(x.shape[0], half, BS, BS) for x in outs[7:]]
    return flags, plan, rows, flat, chunks


def choose_kernel(step, plan, mine, extra_a, extra_b, *rest):
    right = rest[:step]
    left = rest[step : 2 * step]
    outs = rest[-3:-1]
    sems = rest[-1]
    for way, got in ((0, right), (1, left)):
        code = plan[step, 2 * way]
        index = plan[step, 2 * way + 1]
        target = outs[way]
        parts = [(mine.at[index], code == 1)]
        parts.append((extra_a.at[jnp.minimum(index, 1)], jnp.logical_and(code == 2, index < 2)))
        parts.append((extra_b.at[jnp.maximum(index - 2, 0)], jnp.logical_and(code == 2, index >= 2)))
        for t in range(step):
            parts.append((got[t], jnp.logical_and(code == 3, index == t)))
        for source, condition in parts:
            @pl.when(condition)
            def _(source=source):
                pltpu.make_async_copy(source, target, sems.at[way]).start()
    for way in range(2):
        @pl.when(plan[step, 2 * way] > 0)
        def _():
            pltpu.make_async_copy(outs[way], outs[way], sems.at[way]).wait()


def choose(step, plan, own, right, left, after):
    chunk = jax.ShapeDtypeStruct(own[0].shape[1:], jnp.float32)
    count = 3 + 2 * step + len(after)
    return pl.pallas_call(
        functools.partial(choose_kernel, step),
        out_shape=(chunk, chunk),
        in_specs=[SMEM] + [ANY] * count,
        out_specs=(ANY, ANY),
        scratch_shapes=[pltpu.SemaphoreType.DMA((2,))],
        name="choose",
    )(plan, *own, *right, *left, *after)


def permute(value, flip):
    pairs = []
    for p in range(4):
        for q in range(8):
            to_p, to_q = flip(p, q)
            if 0 <= to_q < 8:
                pairs.append((p * 8 + q, to_p * 8 + to_q))
    return lax.ppermute(value, ("row", "col"), pairs)


def swap_core(value):
    return permute(value, lambda p, q: (p, q ^ 1))


def quarter_kernel(keep, got, *rest):
    outs, total = rest[-5:-1], rest[-1]
    total[...] = keep[...] + got[...]
    own = lax.axis_index("row")
    for d in range(4):
        outs[d][...] = total[own ^ d]


def quarters(keep, got, after):
    rows = keep.shape[0] // 4
    part = jax.ShapeDtypeStruct((rows, BS), jnp.float32)
    shape = (4, rows, BS)
    return pl.pallas_call(
        quarter_kernel,
        out_shape=(part,) * 4,
        in_specs=[VMEM, VMEM] + [ANY] * len(after),
        out_specs=(VMEM,) * 4,
        scratch_shapes=[pltpu.VMEM(shape, jnp.float32)],
        name="quarters",
    )(keep.reshape(shape), got.reshape(shape), *after)


def collect_kernel(own, one, two, three, out, sems):
    at = lax.axis_index("row")
    copies = [
        pltpu.make_async_copy(source, out.at[at ^ d], sems.at[d]) for d, source in enumerate((own, one, two, three))
    ]
    for copy in copies:
        copy.start()
    for copy in copies:
        copy.wait()


def collect(own, others):
    rows = own.shape[0]
    return pl.pallas_call(
        collect_kernel,
        out_shape=jax.ShapeDtypeStruct((4, rows, BS), jnp.float32),
        in_specs=[ANY] * 4,
        out_specs=ANY,
        scratch_shapes=[pltpu.SemaphoreType.DMA((4,))],
        name="collect",
    )(own, *others)


def join_kernel(own, other, out, sems):
    core = lax.axis_index("col") % 2
    copies = [
        pltpu.make_async_copy(own, out.at[core], sems.at[0]),
        pltpu.make_async_copy(other, out.at[1 - core], sems.at[1]),
    ]
    for copy in copies:
        copy.start()
    for copy in copies:
        copy.wait()


def join(own):
    other = swap_core(own)
    out = pl.pallas_call(
        join_kernel,
        out_shape=jax.ShapeDtypeStruct((2,) + own.shape, jnp.float32),
        in_specs=[ANY] * 2,
        out_specs=ANY,
        scratch_shapes=[pltpu.SemaphoreType.DMA((2,))],
        name="join",
    )(own, other)
    return out.reshape(-1, BS, BS)


def across_square(parts):
    return [permute(parts[d - 1], lambda p, q, d=d: (p ^ d, q)) for d in range(1, 4)]


def along_line(value):
    return [permute(value, lambda p, q, d=d: (p, q ^ (2 * d))) for d in range(1, 4)]


def sum_first(keep, send, after):
    own, *parts = quarters(keep, swap_core(send), after)
    got = across_square(parts)
    return own + got[0] + got[1] + got[2]


def sum_second(value):
    got = along_line(value)
    return value + got[0] + got[1] + got[2]


def sum_third(value):
    return collect(value, across_square([value] * 3))


def piece_kernel(n, diag, *rest):
    lowers = rest[:n]
    inverses = rest[n : 2 * n]
    lower_out, inverse_out = rest[-2:]

    def row(i):
        return jnp.concatenate([lowers[j][(i - j) * BS : (i - j + 1) * BS, :] for j in range(n)], axis=1)

    column = []
    for i in range(n, PB):
        value = diag[lower_index(i, n)]
        if n:
            value = value - dot_nt(row(i), row(n))
        column.append(value)
    upper, inverse = factor_block(column[0])
    lower_out[0:BS, :] = upper.T
    if n + 1 < PB:
        lower_out[BS:, :] = dot_nt(jnp.concatenate(column[1:], axis=0), inverse)
    inverse_out[:, n * BS :] = inverse
    if n:
        before = jnp.concatenate(
            [
                jnp.concatenate([inverses[j][...], jnp.zeros((BS, (n - 1 - j) * BS), jnp.float32)], axis=1)
                if j + 1 < n
                else inverses[j][...]
                for j in range(n)
            ],
            axis=0,
        )
        inverse_out[:, : n * BS] = -dot_nn(inverse, dot_nn(row(n), before))


def piece(n, diag, lowers, inverses, after):
    return pl.pallas_call(
        functools.partial(piece_kernel, n),
        out_shape=(
            jax.ShapeDtypeStruct(((PB - n) * BS, BS), jnp.float32),
            jax.ShapeDtypeStruct((BS, (n + 1) * BS), jnp.float32),
        ),
        in_specs=[VMEM] * (1 + 2 * n) + [ANY] * len(after),
        out_specs=(VMEM, VMEM),
        compiler_params=pltpu.CompilerParams(vmem_limit_bytes=32 * 2**20),
        cost_estimate=pl.CostEstimate(flops=10**10, bytes_accessed=10**6, transcendentals=0),
        name="factor_piece",
    )(diag, *lowers, *inverses, *after)


def inverse_rows(inverses):
    rows = []
    for j in range(PB):
        if j + 1 < PB:
            rows.append(jnp.concatenate([inverses[j][...], jnp.zeros((BS, (PB - 1 - j) * BS), jnp.float32)], axis=1))
        else:
            rows.append(inverses[j][...])
    return jnp.concatenate(rows, axis=0)


def between_kernel(diag, *rest):
    inverses = rest[:PB]
    cross_out, rest_out = rest[-2:]
    inverse = inverse_rows(inverses)
    one = PB * (PB + 1) // 2
    left = [
        jnp.concatenate([diag[lower_index(i, j) - one] for j in range(PB)], axis=1) for i in range(PB, NC)
    ]
    cross = dot_nt(jnp.concatenate(left, axis=0), inverse)
    cross_out[...] = cross
    for i in range(PB):
        here = cross[i * BS : (i + 1) * BS, :]
        product = dot_nt(here, cross[: (i + 1) * BS, :])
        for j in range(i + 1):
            block = diag[lower_index(i + PB, j + PB) - one]
            rest_out[lower_index(i, j)] = block - product[:, j * BS : (j + 1) * BS]


def between(diag, inverses, after):
    return pl.pallas_call(
        between_kernel,
        out_shape=(
            jax.ShapeDtypeStruct((PB * BS, PB * BS), jnp.float32),
            jax.ShapeDtypeStruct((PB * (PB + 1) // 2, BS, BS), jnp.float32),
        ),
        in_specs=[VMEM] * (1 + PB) + [ANY] * len(after),
        out_specs=(VMEM, VMEM),
        compiler_params=pltpu.CompilerParams(vmem_limit_bytes=32 * 2**20),
        cost_estimate=pl.CostEstimate(flops=10**10, bytes_accessed=10**6, transcendentals=0),
        name="between",
    )(diag, *inverses, *after)


def finish_kernel(*refs):
    first = inverse_rows(refs[:PB])
    second = inverse_rows(refs[PB : 2 * PB])
    cross = refs[2 * PB][...]
    lowers = refs[2 * PB + 1 : 4 * PB + 1]
    lower_out, high_out, low_out = refs[-3:]
    size = PB * BS
    lower_out[...] = jnp.zeros_like(lower_out)
    for j in range(PB):
        for half in range(2):
            rows = slice(half * size + j * BS, (half + 1) * size)
            lower_out[rows, j * BS : (j + 1) * BS] = lowers[half * PB + j][...]
    high_out[:size, size:] = jnp.zeros((size, size), jnp.bfloat16)
    low_out[:size, size:] = jnp.zeros((size, size), jnp.bfloat16)
    corner = -dot_nn(second, dot_nn(cross, first))
    for value, rows, cols in (
        (first, slice(0, size), slice(0, size)),
        (corner, slice(size, 2 * size), slice(0, size)),
        (second, slice(size, 2 * size), slice(size, 2 * size)),
    ):
        high, low = split(value)
        high_out[rows, cols] = high
        low_out[rows, cols] = low


def finish(first, second, cross, lowers):
    size = NC * BS
    return pl.pallas_call(
        finish_kernel,
        out_shape=(jax.ShapeDtypeStruct((size, size // 2), jnp.float32),)
        + (jax.ShapeDtypeStruct((size, size), jnp.bfloat16),) * 2,
        in_specs=[VMEM] * (4 * PB + 1),
        out_specs=(VMEM,) * 3,
        compiler_params=pltpu.CompilerParams(vmem_limit_bytes=32 * 2**20),
        cost_estimate=pl.CostEstimate(flops=10**10, bytes_accessed=10**6, transcendentals=0),
        name="finish",
    )(*first, *second, cross, *lowers)


def start_copies(condition, source, target, sem):
    @pl.when(condition)
    def _():
        pltpu.make_async_copy(source, target, sem).start()


def fetch_streams(steps, plan, refs, panel, sems):
    core = lax.axis_index("col") % 2
    mine, extra_a, extra_b, theirs_a, theirs_b, sibling = refs[:6]
    right, left, right_other, left_other = (refs[6 + i * steps : 6 + (i + 1) * steps] for i in range(4))
    for c in range(NC):
        code = plan[c, 4]
        index = plan[c, 5]
        near = index < 2
        low = jnp.minimum(index, 1)
        far = jnp.maximum(index - 2, 0)
        same = (panel.at[c, core], sems.at[c, 0])
        other = (panel.at[c, 1 - core], sems.at[c, 1])
        start_copies(code == 0, mine.at[index], *same)
        start_copies(jnp.logical_and(code == 1, near), extra_a.at[low], *same)
        start_copies(jnp.logical_and(code == 1, index >= 2), extra_b.at[far], *same)
        start_copies(jnp.logical_and(code == 0, near), theirs_a.at[low], *other)
        start_copies(jnp.logical_and(code == 0, index >= 2), theirs_b.at[far], *other)
        start_copies(code == 1, sibling.at[index], *other)
        for t in range(steps):
            start_copies(jnp.logical_and(code == 2, index == t), right[t], *same)
            start_copies(jnp.logical_and(code == 3, index == t), left[t], *same)
            start_copies(jnp.logical_and(code == 2, index == t), right_other[t], *other)
            start_copies(jnp.logical_and(code == 3, index == t), left_other[t], *other)


def fetch_rows(plan, refs, panel, sems):
    for c in range(NC):
        for k in range(2):
            pltpu.make_async_copy(refs[0].at[c, :, k], panel.at[c, k], sems.at[c, k]).start()


def three(dot, a_high, a_low, b_high, b_low):
    kwargs = dict(preferred_element_type=jnp.float32)
    return dot(a_high, b_high, **kwargs) + (dot(a_high, b_low, **kwargs) + dot(a_low, b_high, **kwargs))


def nt(a, b, **kwargs):
    return lax.dot_general(a, b, (((1,), (1,)), ((), ())), **kwargs)


def nn(a, b, **kwargs):
    return lax.dot_general(a, b, (((1,), (0,)), ((), ())), **kwargs)


def masked(tiles, axis, first, second):
    low_part = jnp.concatenate(tiles[:PB], axis=axis)
    high_part = jnp.concatenate(tiles[PB:], axis=axis)
    zero = jnp.zeros_like(low_part)
    return jnp.concatenate([jnp.where(first, low_part, zero), jnp.where(second, high_part, zero)], axis=axis)


def update_kernel(fetch, flags, plan, front_ref, cols_ref, lower_ref, high_ref, low_ref, *rest):
    refs = rest[:-10]
    out_ref, panel, raw_high, raw_low, col_high, col_low, solved, sol_high, sol_low, sems = rest[-10:]
    size = NC * BS
    half = PB * BS
    width = 2 * BS
    step = pl.program_id(0)
    col_blocks = cols_ref.shape[2]

    @pl.when(step == 0)
    def _():
        fetch(plan, refs, panel, sems)
        for b in range(col_blocks):
            at = slice(b * BS, (b + 1) * BS)
            raw = masked([cols_ref[c, :, b, :] for c in range(NC)], 0, flags[b, 3] != 0, flags[b, 4] != 0)
            high, low = split(raw)
            raw_high[:, at] = high
            raw_low[:, at] = low
        for m in range(0, size, width):
            deep = m + width
            value = three(nn, high_ref[m:deep, :deep], low_ref[m:deep, :deep], raw_high[:deep, :], raw_low[:deep, :])
            if m >= half:
                value = jnp.concatenate(
                    [
                        jnp.where(flags[b, 4] != 0, value[:, b * BS : (b + 1) * BS], 0.0)
                        for b in range(col_blocks)
                    ],
                    axis=1,
                )
            high, low = split(value)
            col_high[m:deep, :] = high
            col_low[m:deep, :] = low
        for c in range(NC):
            for k in range(2):
                pltpu.make_async_copy(panel.at[c, k], panel.at[c, k], sems.at[c, k]).wait()

    for k in range(2):
        a = step * 2 + k
        raw = masked([panel[c, k, step] for c in range(NC)], 1, flags[a, 0] != 0, flags[a, 1] != 0)
        high, low = split(raw)
        sol_high[k * BS : (k + 1) * BS, :] = high
        sol_low[k * BS : (k + 1) * BS, :] = low
    for m in range(0, size, width):
        deep = m + width
        value = three(nt, sol_high[:, :deep], sol_low[:, :deep], high_ref[m:deep, :deep], low_ref[m:deep, :deep])
        if m >= half:
            value = jnp.concatenate(
                [
                    jnp.where(flags[step * 2 + k, 1] != 0, value[k * BS : (k + 1) * BS, :], 0.0)
                    for k in range(2)
                ],
                axis=0,
            )
        solved[:, m:deep] = value
    high, low = split(solved[...])
    sol_high[...] = high
    sol_low[...] = low
    for b in range(0, col_blocks, 2):
        at = slice(b * BS, (b + 2) * BS)
        value = three(nn, sol_high[...], sol_low[...], col_high[:, at], col_low[:, at])
        for s in range(2):
            out_ref[:, b + s, :] = front_ref[:, b + s, :] - value[:, s * BS : (s + 1) * BS]
    for b in range(col_blocks):
        j = flags[b, 5]

        @pl.when(j >= 0)
        def _(b=b, j=j):
            at = pl.ds(pl.multiple_of(j * BS, BS), BS)
            for k in range(2):
                a = step * 2 + k
                rows = slice(k * BS, (k + 1) * BS)
                listed = jnp.where(j < PB, flags[a, 0], flags[a, 1])
                own = flags[a, 2]

                @pl.when(listed != 0)
                def _():
                    out_ref[rows, b, :] = solved[rows, at]

                @pl.when(jnp.logical_and(own >= 0, own // PB == j // PB))
                def _():
                    source = pl.ds(pl.multiple_of(own * BS, BS), BS)
                    inside = pl.ds(pl.multiple_of(j % PB * BS, BS), BS)
                    out_ref[rows, b, :] = lower_ref[source, inside]


def update_front(fetch, flags, plan, front, cols, lower, high, low, sources):
    row_blocks, _, col_blocks = front.shape[:3]
    size = NC * BS
    flops = 3 * 2 * row_blocks * BS * size * (col_blocks * BS + size)
    block = pl.BlockSpec((2 * BS, col_blocks, BS), lambda i: (i, 0, 0))
    return pl.pallas_call(
        functools.partial(update_kernel, fetch),
        out_shape=jax.ShapeDtypeStruct((row_blocks * BS, col_blocks, BS), jnp.float32),
        grid=(row_blocks // 2,),
        in_specs=[SMEM, SMEM, block] + [VMEM] * 4 + [ANY] * len(sources),
        out_specs=block,
        scratch_shapes=[
            pltpu.VMEM((NC, 2, row_blocks // 2, BS, BS), jnp.float32),
            pltpu.VMEM((size, col_blocks * BS), jnp.bfloat16),
            pltpu.VMEM((size, col_blocks * BS), jnp.bfloat16),
            pltpu.VMEM((size, col_blocks * BS), jnp.bfloat16),
            pltpu.VMEM((size, col_blocks * BS), jnp.bfloat16),
            pltpu.VMEM((2 * BS, size), jnp.float32),
            pltpu.VMEM((2 * BS, size), jnp.bfloat16),
            pltpu.VMEM((2 * BS, size), jnp.bfloat16),
            pltpu.SemaphoreType.DMA((NC, 2)),
        ],
        compiler_params=pltpu.CompilerParams(vmem_limit_bytes=56 * 2**20),
        cost_estimate=pl.CostEstimate(flops=flops, bytes_accessed=4 * 10**7, transcendentals=0),
        name="update_front",
    )(flags, plan, front.reshape(row_blocks * BS, col_blocks, BS), cols, lower, high, low, *sources)


def block_flags(slots, listed_one, listed_two, diag_slots):
    one = jnp.any(slots[:, None] == listed_one[None, :], axis=1).astype(jnp.int32)
    two = jnp.any(slots[:, None] == listed_two[None, :], axis=1).astype(jnp.int32)
    order = jnp.arange(1, NC + 1, dtype=jnp.int32)
    where = jnp.sum(jnp.where(slots[:, None] == diag_slots[None, :], order[None, :], 0), axis=1) - 1
    return jnp.stack([one, two, where], axis=1)


def gather_summed(front, block_slots, rows_first, rows_second):
    grid_rows, grid_cols = lax.axis_size("row"), lax.axis_size("col")
    own_row, own_col = lax.axis_index("row"), lax.axis_index("col")
    row_blocks, col_blocks = front.shape[0], front.shape[3]
    diag_slots = block_slots[:NC]
    listed_one = block_slots[rows_first]
    listed_two = block_slots[rows_second]
    row_slots = jnp.arange(row_blocks, dtype=jnp.int32) * grid_rows + own_row
    col_slots = jnp.arange(row_blocks, dtype=jnp.int32) * grid_cols + own_col
    flags = jnp.concatenate(
        [block_flags(slots, listed_one, listed_two, diag_slots) for slots in (row_slots, col_slots)], axis=1
    )
    flags = jnp.pad(flags, ((0, 0), (0, 2)))
    local = front.reshape(row_blocks, BS, col_blocks, BS)
    pieces = []
    rows = []
    for c in range(NC):
        piece = lax.dynamic_index_in_dim(local, diag_slots[c] // grid_cols, 2, keepdims=False)
        pieces.append(jnp.where(diag_slots[c] % grid_cols == own_col, piece, jnp.zeros_like(piece)))
        piece = lax.dynamic_index_in_dim(local, diag_slots[c] // grid_rows, 0, keepdims=False)
        rows.append(jnp.where(diag_slots[c] % grid_rows == own_row, piece, jnp.zeros_like(piece)))
    pieces = jnp.stack(pieces, axis=0)
    blocks = []
    for i in range(NC):
        part = lax.dynamic_index_in_dim(pieces, diag_slots[i] // grid_rows, 1, keepdims=False)[: i + 1]
        blocks.append(jnp.where(diag_slots[i] % grid_rows == own_row, part, jnp.zeros_like(part)))
    diag = lax.psum(jnp.concatenate(blocks, axis=0), ("row", "col"))
    panel = lax.psum(pieces, "col").reshape(NC, row_blocks // 2, 2, BS, BS)
    return flags, jnp.stack(rows, axis=0), diag, panel


def factor_panel(diag, hooks):
    lowers, inverses = [], []
    for n in range(PB):
        lower, inverse = piece(n, diag, lowers, inverses, hooks(n, lowers))
        lowers.append(lower)
        inverses.append(inverse)
    return lowers, inverses


def on_device(front, block_slots, rows_first, rows_second):
    if (lax.axis_size("row"), lax.axis_size("col")) != (4, 8):
        flags, rows, diag, panel = gather_summed(front, block_slots, rows_first, rows_second)
        cols = lax.psum(rows, "row")
        one = PB * (PB + 1) // 2
        nothing = lambda n, done: []
        lowers, inverses = factor_panel(diag[:one], nothing)
        cross, corner = between(diag[one:], inverses, [])
        more_lowers, more_inverses = factor_panel(corner, nothing)
        factors = finish(inverses, more_inverses, cross, lowers + more_lowers)
        out = update_front(fetch_rows, flags, flags, local_blocks(front), cols, *factors, [panel])
        return out.reshape(front.shape)

    flags, plan, rows, flat, chunks = start(front, block_slots, rows_first, rows_second)
    cols = lax.psum(rows, "row")
    mine, theirs_a, theirs_b = chunks
    extra_a = swap_core(theirs_a)
    extra_b = swap_core(theirs_b)
    right, left, sent = [], [], []

    def stream(after):
        step = len(right)
        own = (mine, extra_a, extra_b if step >= 2 else extra_a)
        to_right, to_left = choose(step, plan, own, right, left, after)
        right.append(permute(to_right, lambda p, q: (p, q + 2)))
        left.append(permute(to_left, lambda p, q: (p, q - 2)))
        sent.append(to_right)

    def hooks(n, done):
        if n:
            stream([done[-1]])
        return [sent[-1]]

    stream([])
    part = sum_first(flat[0], flat[1], [])
    stream([part])
    diag = join(sum_third(sum_second(part)))
    sibling = swap_core(mine)
    stream([diag])
    second = sum_second(sum_first(flat[2], flat[3], [diag]))
    lowers, inverses = factor_panel(diag, hooks)
    second = join(sum_third(second))
    stream([lowers[-1]])
    cross, corner = between(second, inverses, [sent[-1]])
    more_lowers, more_inverses = factor_panel(corner, lambda n, done: hooks(n, done) if n == 1 else [sent[-1]])
    factors = finish(inverses, more_inverses, cross, lowers + more_lowers)

    def complete():
        sources = [mine, extra_a, extra_b, theirs_a, theirs_b, sibling, *right, *left]
        sources += [swap_core(x) for x in right] + [swap_core(x) for x in left]
        fetch = functools.partial(fetch_streams, len(right))
        return update_front(fetch, flags, plan, local_blocks(front), cols, *factors, sources)

    def longer():
        kept = len(right)
        while len(right) < LONG:
            stream([])
        out = complete()
        del right[kept:], left[kept:]
        return out

    assert len(right) == SHORT
    out = lax.cond(plan[0, 6] > SHORT, longer, complete)
    return out.reshape(front.shape)


def local_blocks(front):
    return front.reshape(front.shape[0], BS, front.shape[3], BS)


def solution(mesh):
    placed = (P(None, "row", None, None, "col", None), P(), P(), P())
    return jax.shard_map(
        on_device,
        mesh=mesh,
        in_specs=placed,
        out_specs=P(None, "row", None, None, "col", None),
        check_vma=False,
    )
```

```python
import functools

import jax
import jax.numpy as jnp
from jax import lax
from jax.experimental import pallas as pl
from jax.experimental.pallas import tpu as pltpu
from jax.sharding import PartitionSpec as P

BS = 128
PB = 4
NC = 2 * PB
STEP = 4
SHORT = 8
LONG = 10
ALMOST_ALL = 63 * 2**20
HIGHEST = lax.Precision.HIGHEST
ANY = pl.BlockSpec(memory_space=pl.ANY)
HBM = pl.BlockSpec(memory_space=pltpu.HBM)
VMEM = pl.BlockSpec(memory_space=pltpu.VMEM)
SMEM = pl.BlockSpec(memory_space=pltpu.SMEM)


def lane_copy(tile, lane):
    return jnp.broadcast_to(tile[:, lane : lane + 1], tile.shape)


def row_copy(tile, row):
    return jnp.broadcast_to(tile[row : row + 1, :], tile.shape)


def factor_block(block):
    tiles = BS // 8
    sub = lax.broadcasted_iota(jnp.int32, (8, BS), 0)
    lanes = lax.broadcasted_iota(jnp.int32, (8, BS), 1)
    left = [block[8 * i : 8 * i + 8, :] for i in range(tiles)]
    right = [jnp.where(lanes == sub + 8 * i, 1.0, 0.0).astype(jnp.float32) for i in range(tiles)]
    upper = []
    inverse = []
    for j in range(0, BS, STEP):
        g, o = divmod(j, 8)
        if o == 0:
            upper_tile = jnp.zeros((8, BS), jnp.float32)
            inverse_tile = jnp.zeros((8, BS), jnp.float32)
        rows = [row_copy(left[g], o + s) for s in range(STEP)]
        extra = [row_copy(right[g], o + s) for s in range(STEP)]
        first = g if o + STEP < 8 else g + 1
        cols = {i: [lane_copy(left[i], j + s) for s in range(STEP)] for i in range(first, tiles)}
        pivot = [[lane_copy(rows[s], j + t) if t >= s else None for t in range(STEP)] for s in range(STEP)]
        ratio = [[None] * STEP for _ in range(STEP)]
        recip = []
        for s in range(STEP):
            inv = 1.0 / pivot[s][s]
            recip.append(inv)
            for t in range(s + 1, STEP):
                ratio[s][t] = pivot[s][t] * inv
            for t in range(s + 1, STEP):
                for u in range(t, STEP):
                    pivot[t][u] = pivot[t][u] - ratio[s][t] * pivot[s][u]
                rows[t] = rows[t] - ratio[s][t] * rows[s]
                extra[t] = extra[t] - ratio[s][t] * extra[s]
        for s in range(STEP):
            scale = lax.rsqrt(pivot[s][s])
            scale = scale * (1.5 - 0.5 * pivot[s][s] * scale * scale)
            here = sub == o + s
            upper_tile = jnp.where(here, rows[s] * scale, upper_tile)
            inverse_tile = jnp.where(here, extra[s] * scale, inverse_tile)
        if o + STEP == 8:
            upper.append(jnp.where(lanes >= sub + 8 * g, upper_tile, 0.0))
            inverse.append(jnp.where(lanes <= sub + 8 * g, inverse_tile, 0.0))
        for s in reversed(range(STEP)):
            rows[s] = rows[s] * recip[s]
            extra[s] = extra[s] * recip[s]
            for t in range(s + 1, STEP):
                rows[s] = rows[s] - ratio[s][t] * rows[t]
                extra[s] = extra[s] - ratio[s][t] * extra[t]
        for i in range(first, tiles):
            less = cols[i][0] * rows[0]
            less_extra = cols[i][0] * extra[0]
            for s in range(1, STEP):
                less = less + cols[i][s] * rows[s]
                less_extra = less_extra + cols[i][s] * extra[s]
            if i == g:
                below = sub >= o + STEP
                left[i] = jnp.where(below, left[i] - less, left[i])
                right[i] = jnp.where(below, right[i] - less_extra, right[i])
            else:
                left[i] = left[i] - less
                right[i] = right[i] - less_extra
    return jnp.concatenate(upper, axis=0), jnp.concatenate(inverse, axis=0)


def lower_index(i, j):
    return i * (i + 1) // 2 + j


def dot_nt(a, b):
    return lax.dot_general(a, b, (((1,), (1,)), ((), ())), precision=HIGHEST, preferred_element_type=jnp.float32)


def dot_nn(a, b):
    return lax.dot_general(a, b, (((1,), (0,)), ((), ())), precision=HIGHEST, preferred_element_type=jnp.float32)


def split(x):
    high = x.astype(jnp.bfloat16)
    return high, (x - high.astype(jnp.float32)).astype(jnp.bfloat16)


def place(count, core, block):
    half = count // 2
    return (block // half) == core, block % half


def start_kernel(slots, first, second, front_ref, wide_ref, flags, plan, rows_out, keep_one, send_one, keep_two,
                 send_two, mine, theirs_a, theirs_b, zero, zero_wide, blocks, columns, lines, sems, out_sems):
    row_blocks, _, col_blocks = wide_ref.shape[:3]
    grid_rows, grid_cols, depth = 4, 8, 4
    own_row = lax.axis_index("row")
    own_col = lax.axis_index("col")
    core = own_col % 2
    z = own_col // 2
    slot = [slots[i] for i in range(NC)]
    one = PB * (PB + 1) // 2
    two = NC * (NC + 1) // 2 - one
    chip = [(slot[c] % grid_cols) // 2 for c in range(NC)]
    here = [chip[c] == z for c in range(NC)]
    rank = []
    for c in range(NC):
        count = jnp.int32(0)
        for d in range(c):
            count = count + (chip[d] == chip[c]).astype(jnp.int32)
        rank.append(count)
    moves = []
    fills = []

    def move(condition, source, middle, targets):
        index = len(moves)

        @pl.when(condition)
        def _():
            pltpu.make_async_copy(source, middle, sems.at[index]).start()

        moves.append((condition, middle, targets, index))

    for i in range(NC):
        for j in range(i + 1):
            block = lower_index(i, j)
            if i < PB:
                count, at, keep, send = one, block, keep_one, send_one
            else:
                count, at, keep, send = two, block - one, keep_two, send_two
            half = count // 2
            a = slot[i] // grid_rows
            b = slot[j] // grid_cols
            owned = jnp.logical_and(slot[i] % grid_rows == own_row, slot[j] % grid_cols == own_col)
            stay = core == at // half
            targets = ((keep.at[at % half], stay), (send.at[at % half], jnp.logical_not(stay)))
            move(owned, front_ref.at[a // 2, a % 2, :, b], blocks.at[block], targets)
            for target, chosen in targets:
                fills.append((jnp.logical_and(chosen, jnp.logical_not(owned)), zero, target, block))
    always = core >= 0
    for c in range(NC):
        owned = slot[c] % grid_cols == own_col
        b = slot[c] // grid_cols
        move(owned, front_ref.at[:, core, :, b], columns.at[c, 0], ((mine.at[rank[c]], always),))
        near = rank[c] < 2
        targets = (
            (theirs_a.at[jnp.minimum(rank[c], 1)], near),
            (theirs_b.at[jnp.maximum(rank[c] - 2, 0)], jnp.logical_not(near)),
        )
        move(owned, front_ref.at[:, 1 - core, :, b], columns.at[c, 1], targets)
    for c in range(NC):
        owned = slot[c] % grid_rows == own_row
        fills.append((jnp.logical_not(owned), zero_wide, rows_out.at[c], len(moves)))
        move(owned, wide_ref.at[slot[c] // grid_rows], lines.at[c], ((rows_out.at[c], always),))

    zero[...] = jnp.zeros_like(zero)
    zero_wide[...] = jnp.zeros_like(zero_wide)
    for condition, source, target, index in fills:
        @pl.when(condition)
        def _(source=source, target=target, index=index):
            pltpu.make_async_copy(source, target, out_sems.at[index]).start()

    def send_out(condition, middle, targets, index):
        @pl.when(condition)
        def _():
            pltpu.make_async_copy(middle, middle, sems.at[index]).wait()
            for target, chosen in targets:
                @pl.when(chosen)
                def _(target=target):
                    pltpu.make_async_copy(middle, target, out_sems.at[index]).start()

    for item in moves[: one + two]:
        send_out(*item)

    for a in range(row_blocks):
        for f in range(8):
            flags[a, f] = jnp.int32(-1 if f in (2, 5) else 0)
    for c in range(NC):
        @pl.when(slot[c] % grid_rows == own_row)
        def _(c=c):
            flags[slot[c] // grid_rows, 2] = jnp.int32(c)

        @pl.when(slot[c] % grid_cols == own_col)
        def _(c=c):
            flags[slot[c] // grid_cols, 5] = jnp.int32(c)

    for listed, f in ((first, 0), (second, 1)):
        @pl.loop(0, listed.shape[0])
        def _(i, listed=listed, f=f):
            s = slots[listed[i]]

            @pl.when(s % grid_rows == own_row)
            def _():
                flags[s // grid_rows, f] = jnp.int32(1)

            @pl.when(s % grid_cols == own_col)
            def _():
                flags[s // grid_cols, 3 + f] = jnp.int32(1)

    for t in range(LONG):
        for f in range(8):
            plan[t, f] = jnp.int32(0)
    counts = []
    for s in range(depth):
        count = jnp.int32(0)
        for c in range(NC):
            count = count + (chip[c] == s).astype(jnp.int32)
        counts.append(count)
    last = jnp.int32(0)
    for way in range(2):
        order = (lambda s: s) if way == 0 else (lambda s: depth - 1 - s)
        begin = [[None] * depth for _ in range(depth)]
        for at in range(depth - 1):
            for s in range(at, -1, -1):
                if s == at:
                    begin[at][s] = jnp.int32(0)
                else:
                    begin[at][s] = jnp.maximum(
                        begin[at][s + 1] + counts[order(s + 1)], begin[at - 1][s] + 1
                    )
        for at in range(depth - 1):
            for s in range(at + 1):
                count = counts[order(s)]
                last = jnp.maximum(last, jnp.where(count > 0, begin[at][s] + count, 0))
        for at in range(depth):
            @pl.when(z == order(at))
            def _(at=at, begin=begin, order=order, way=way):
                for c in range(NC):
                    for s in range(at + 1):
                        source = chip[c] == order(s)
                        if s == at and at < depth - 1:
                            @pl.when(source)
                            def _(c=c):
                                when = begin[at][at] + rank[c]
                                plan[when, 2 * way] = jnp.where(slot[c] % grid_cols == own_col, 1, 2)
                                plan[when, 2 * way + 1] = rank[c]
                        if s < at:
                            @pl.when(source)
                            def _(c=c, s=s):
                                got = begin[at - 1][s] + rank[c]
                                plan[c, 4] = jnp.int32(2 + way)
                                plan[c, 5] = got
                                if at < depth - 1:
                                    when = begin[at][s] + rank[c]
                                    plan[when, 2 * way] = jnp.int32(3)
                                    plan[when, 2 * way + 1] = got
    for c in range(NC):
        @pl.when(here[c])
        def _(c=c):
            plan[c, 4] = jnp.where(slot[c] % grid_cols == own_col, 0, 1)
            plan[c, 5] = rank[c]
    plan[0, 6] = last

    for item in moves[one + two :]:
        send_out(*item)
    for condition, middle, targets, index in moves:
        if index < one + two or index >= one + two + 2 * NC:
            pltpu.make_async_copy(middle, middle, out_sems.at[index]).wait()
        else:
            @pl.when(condition)
            def _(middle=middle, index=index):
                pltpu.make_async_copy(middle, middle, out_sems.at[index]).wait()


def start(front, block_slots, rows_first, rows_second):
    row_blocks, col_blocks = front.shape[0], front.shape[3]
    half = row_blocks // 2
    one = PB * (PB + 1) // 2
    two = NC * (NC + 1) // 2 - one
    f32 = lambda *shape: jax.ShapeDtypeStruct(shape, jnp.float32)
    outs = pl.pallas_call(
        start_kernel,
        out_shape=(
            jax.ShapeDtypeStruct((row_blocks, 8), jnp.int32),
            jax.ShapeDtypeStruct((LONG, 8), jnp.int32),
            f32(NC, BS, col_blocks, BS),
            f32(one // 2, BS, 1, BS),
            f32(one // 2, BS, 1, BS),
            f32(two // 2, BS, 1, BS),
            f32(two // 2, BS, 1, BS),
            f32(NC, half, BS, 1, BS),
            f32(2, half, BS, 1, BS),
            f32(NC - 2, half, BS, 1, BS),
        ),
        in_specs=[SMEM, SMEM, SMEM, HBM, HBM],
        out_specs=(SMEM, SMEM) + (HBM,) * 8,
        scratch_shapes=[
            pltpu.VMEM((BS, 1, BS), jnp.float32),
            pltpu.VMEM((BS, col_blocks, BS), jnp.float32),
            pltpu.VMEM((one + two, BS, 1, BS), jnp.float32),
            pltpu.VMEM((NC, 2, half, BS, 1, BS), jnp.float32),
            pltpu.VMEM((NC, BS, col_blocks, BS), jnp.float32),
            pltpu.SemaphoreType.DMA((one + two + 3 * NC,)),
            pltpu.SemaphoreType.DMA((one + two + 3 * NC,)),
        ],
        compiler_params=pltpu.CompilerParams(vmem_limit_bytes=ALMOST_ALL),
        name="start",
    )(
        block_slots,
        rows_first,
        rows_second,
        front.reshape(half, 2, BS, col_blocks, 1, BS),
        front.reshape(row_blocks, BS, col_blocks, BS),
    )
    flags, plan, rows = outs[:3]
    flat = [x.reshape(-1, BS) for x in outs[3:7]]
    chunks = [x.reshape(x.shape[0], half, BS, BS) for x in outs[7:]]
    return flags, plan, rows, flat, chunks


def choose_kernel(step, count, plan, mine, extra_a, extra_b, *rest):
    right = rest[:step]
    left = rest[step : 2 * step]
    outs = rest[2 * step + count : 2 * step + count + 2]
    token, middle, sems = rest[-3:]
    codes = []
    for way, got in ((0, right), (1, left)):
        code = plan[step, 2 * way]
        index = plan[step, 2 * way + 1]
        codes.append(code)
        parts = [(mine.at[index], code == 1)]
        parts.append((extra_a.at[jnp.minimum(index, 1)], jnp.logical_and(code == 2, index < 2)))
        parts.append((extra_b.at[jnp.maximum(index - 2, 0)], jnp.logical_and(code == 2, index >= 2)))
        for t in range(step):
            parts.append((got[t], jnp.logical_and(code == 3, index == t)))
        for source, condition in parts:
            @pl.when(condition)
            def _(source=source, way=way):
                pltpu.make_async_copy(source, middle.at[way], sems.at[way]).start()
    for way in range(2):
        @pl.when(codes[way] > 0)
        def _(way=way):
            pltpu.make_async_copy(middle.at[way], middle.at[way], sems.at[way]).wait()
            pltpu.make_async_copy(middle.at[way], outs[way], sems.at[2 + way]).start()
    token[0] = jnp.int32(0)
    for way in range(2):
        @pl.when(codes[way] > 0)
        def _(way=way):
            pltpu.make_async_copy(middle.at[way], outs[way], sems.at[2 + way]).wait()


TOKEN = jax.ShapeDtypeStruct((1,), jnp.int32)


def choose(step, plan, own, right, left, after):
    chunk = jax.ShapeDtypeStruct(own[0].shape[1:], jnp.float32)
    return pl.pallas_call(
        functools.partial(choose_kernel, step, len(after)),
        out_shape=(chunk, chunk, TOKEN),
        in_specs=[SMEM] + [HBM] * (3 + 2 * step) + [SMEM] * len(after),
        out_specs=(HBM, HBM, SMEM),
        scratch_shapes=[pltpu.VMEM((2,) + chunk.shape, jnp.float32), pltpu.SemaphoreType.DMA((4,))],
        compiler_params=pltpu.CompilerParams(vmem_limit_bytes=ALMOST_ALL),
        name="choose",
    )(plan, *own, *right, *left, *after)


def permute(value, flip):
    pairs = []
    for p in range(4):
        for q in range(8):
            to_p, to_q = flip(p, q)
            if 0 <= to_q < 8:
                pairs.append((p * 8 + q, to_p * 8 + to_q))
    return lax.ppermute(value, ("row", "col"), pairs)


def swap_core(value):
    return permute(value, lambda p, q: (p, q ^ 1))


def quarter_kernel(keep, got, *rest):
    outs, token, total = rest[-6:-2], rest[-2], rest[-1]
    total[...] = keep[...] + got[...]
    own = lax.axis_index("row")
    for d in range(4):
        outs[d][...] = total[own ^ d]
    token[0] = jnp.int32(0)


def quarters(keep, got, after):
    rows = keep.shape[0] // 4
    part = jax.ShapeDtypeStruct((rows, BS), jnp.float32)
    shape = (4, rows, BS)
    return pl.pallas_call(
        quarter_kernel,
        out_shape=(part,) * 4 + (TOKEN,),
        in_specs=[VMEM, VMEM] + [SMEM] * len(after),
        out_specs=(VMEM,) * 4 + (SMEM,),
        scratch_shapes=[pltpu.VMEM(shape, jnp.float32)],
        name="quarters",
    )(keep.reshape(shape), got.reshape(shape), *after)


def collect_kernel(own, one, two, three, out):
    at = lax.axis_index("row")
    for d, source in enumerate((own, one, two, three)):
        out[at ^ d] = source[...]


def collect(own, others):
    rows = own.shape[0]
    return pl.pallas_call(
        collect_kernel,
        out_shape=jax.ShapeDtypeStruct((4, rows, BS), jnp.float32),
        in_specs=[VMEM] * 4,
        out_specs=VMEM,
        name="collect",
    )(own, *others)


def join_kernel(own, other, out, token):
    core = lax.axis_index("col") % 2
    out[core] = own[...]
    out[1 - core] = other[...]
    token[0] = jnp.int32(0)


def join(own):
    other = swap_core(own)
    out, token = pl.pallas_call(
        join_kernel,
        out_shape=(jax.ShapeDtypeStruct((2,) + own.shape, jnp.float32), TOKEN),
        in_specs=[VMEM] * 2,
        out_specs=(VMEM, SMEM),
        name="join",
    )(own, other)
    return out.reshape(-1, BS, BS), token


def across_square(parts):
    return [permute(parts[d - 1], lambda p, q, d=d: (p ^ d, q)) for d in range(1, 4)]


def along_line(value):
    return [permute(value, lambda p, q, d=d: (p, q ^ (2 * d))) for d in range(1, 4)]


def sum_first(keep, send, after):
    own, *parts, token = quarters(keep, swap_core(send), after)
    got = across_square(parts)
    return own + got[0] + got[1] + got[2], token


def sum_second(value):
    got = along_line(value)
    return value + got[0] + got[1] + got[2]


def sum_third(value):
    return collect(value, across_square([value] * 3))


def piece_kernel(n, diag, *rest):
    lowers = rest[:n]
    inverses = rest[n : 2 * n]
    lower_out, inverse_out, token = rest[-3:]
    token[0] = jnp.int32(0)

    def row(i):
        return jnp.concatenate([lowers[j][(i - j) * BS : (i - j + 1) * BS, :] for j in range(n)], axis=1)

    column = []
    for i in range(n, PB):
        value = diag[lower_index(i, n)]
        if n:
            value = value - dot_nt(row(i), row(n))
        column.append(value)
    upper, inverse = factor_block(column[0])
    lower_out[0:BS, :] = upper.T
    if n + 1 < PB:
        lower_out[BS:, :] = dot_nt(jnp.concatenate(column[1:], axis=0), inverse)
    inverse_out[:, n * BS :] = inverse
    if n:
        before = jnp.concatenate(
            [
                jnp.concatenate([inverses[j][...], jnp.zeros((BS, (n - 1 - j) * BS), jnp.float32)], axis=1)
                if j + 1 < n
                else inverses[j][...]
                for j in range(n)
            ],
            axis=0,
        )
        inverse_out[:, : n * BS] = -dot_nn(inverse, dot_nn(row(n), before))


def piece(n, diag, lowers, inverses, after):
    return pl.pallas_call(
        functools.partial(piece_kernel, n),
        out_shape=(
            jax.ShapeDtypeStruct(((PB - n) * BS, BS), jnp.float32),
            jax.ShapeDtypeStruct((BS, (n + 1) * BS), jnp.float32),
            TOKEN,
        ),
        in_specs=[VMEM] * (1 + 2 * n) + [SMEM] * len(after),
        out_specs=(VMEM, VMEM, SMEM),
        compiler_params=pltpu.CompilerParams(vmem_limit_bytes=32 * 2**20),
        cost_estimate=pl.CostEstimate(flops=10**8, bytes_accessed=10**5, transcendentals=0),
        name="factor_piece",
    )(diag, *lowers, *inverses, *after)


def inverse_rows(inverses):
    rows = []
    for j in range(PB):
        if j + 1 < PB:
            rows.append(jnp.concatenate([inverses[j][...], jnp.zeros((BS, (PB - 1 - j) * BS), jnp.float32)], axis=1))
        else:
            rows.append(inverses[j][...])
    return jnp.concatenate(rows, axis=0)


def between_kernel(diag, *rest):
    inverses = rest[:PB]
    cross_out, rest_out = rest[-2:]
    inverse = inverse_rows(inverses)
    one = PB * (PB + 1) // 2
    left = [
        jnp.concatenate([diag[lower_index(i, j) - one] for j in range(PB)], axis=1) for i in range(PB, NC)
    ]
    cross = dot_nt(jnp.concatenate(left, axis=0), inverse)
    cross_out[...] = cross
    for i in range(PB):
        here = cross[i * BS : (i + 1) * BS, :]
        product = dot_nt(here, cross[: (i + 1) * BS, :])
        for j in range(i + 1):
            block = diag[lower_index(i + PB, j + PB) - one]
            rest_out[lower_index(i, j)] = block - product[:, j * BS : (j + 1) * BS]


def between(diag, inverses, after):
    return pl.pallas_call(
        between_kernel,
        out_shape=(
            jax.ShapeDtypeStruct((PB * BS, PB * BS), jnp.float32),
            jax.ShapeDtypeStruct((PB * (PB + 1) // 2, BS, BS), jnp.float32),
        ),
        in_specs=[VMEM] * (1 + PB) + [SMEM] * len(after),
        out_specs=(VMEM, VMEM),
        compiler_params=pltpu.CompilerParams(vmem_limit_bytes=32 * 2**20),
        cost_estimate=pl.CostEstimate(flops=10**8, bytes_accessed=10**5, transcendentals=0),
        name="between",
    )(diag, *inverses, *after)


def finish_kernel(*refs):
    first = inverse_rows(refs[:PB])
    second = inverse_rows(refs[PB : 2 * PB])
    cross = refs[2 * PB][...]
    lowers = refs[2 * PB + 1 : 4 * PB + 1]
    lower_out, high_out, low_out = refs[-3:]
    size = PB * BS
    lower_out[...] = jnp.zeros_like(lower_out)
    for j in range(PB):
        for half in range(2):
            rows = slice(half * size + j * BS, (half + 1) * size)
            lower_out[rows, j * BS : (j + 1) * BS] = lowers[half * PB + j][...]
    high_out[:size, size:] = jnp.zeros((size, size), jnp.bfloat16)
    low_out[:size, size:] = jnp.zeros((size, size), jnp.bfloat16)
    corner = -dot_nn(second, dot_nn(cross, first))
    for value, rows, cols in (
        (first, slice(0, size), slice(0, size)),
        (corner, slice(size, 2 * size), slice(0, size)),
        (second, slice(size, 2 * size), slice(size, 2 * size)),
    ):
        high, low = split(value)
        high_out[rows, cols] = high
        low_out[rows, cols] = low


def finish(first, second, cross, lowers):
    size = NC * BS
    return pl.pallas_call(
        finish_kernel,
        out_shape=(jax.ShapeDtypeStruct((size, size // 2), jnp.float32),)
        + (jax.ShapeDtypeStruct((size, size), jnp.bfloat16),) * 2,
        in_specs=[VMEM] * (4 * PB + 1),
        out_specs=(VMEM,) * 3,
        compiler_params=pltpu.CompilerParams(vmem_limit_bytes=32 * 2**20),
        cost_estimate=pl.CostEstimate(flops=10**8, bytes_accessed=10**5, transcendentals=0),
        name="finish",
    )(*first, *second, cross, *lowers)


def start_copies(condition, source, target, sem):
    @pl.when(condition)
    def _():
        pltpu.make_async_copy(source, target, sem).start()


def fetch_streams(steps, plan, refs, panel, sems):
    core = lax.axis_index("col") % 2
    mine, extra_a, extra_b, theirs_a, theirs_b, sibling = refs[:6]
    right, left, right_other, left_other = (refs[6 + i * steps : 6 + (i + 1) * steps] for i in range(4))
    for c in range(NC):
        code = plan[c, 4]
        index = plan[c, 5]
        near = index < 2
        low = jnp.minimum(index, 1)
        far = jnp.maximum(index - 2, 0)
        same = (panel.at[c, core], sems.at[c, 0])
        other = (panel.at[c, 1 - core], sems.at[c, 1])
        start_copies(code == 0, mine.at[index], *same)
        start_copies(jnp.logical_and(code == 1, near), extra_a.at[low], *same)
        start_copies(jnp.logical_and(code == 1, index >= 2), extra_b.at[far], *same)
        start_copies(jnp.logical_and(code == 0, near), theirs_a.at[low], *other)
        start_copies(jnp.logical_and(code == 0, index >= 2), theirs_b.at[far], *other)
        start_copies(code == 1, sibling.at[index], *other)
        for t in range(steps):
            start_copies(jnp.logical_and(code == 2, index == t), right[t], *same)
            start_copies(jnp.logical_and(code == 3, index == t), left[t], *same)
            start_copies(jnp.logical_and(code == 2, index == t), right_other[t], *other)
            start_copies(jnp.logical_and(code == 3, index == t), left_other[t], *other)


def fetch_rows(plan, refs, panel, sems):
    for c in range(NC):
        for k in range(2):
            pltpu.make_async_copy(refs[0].at[c, :, k], panel.at[c, k], sems.at[c, k]).start()


def three(dot, a_high, a_low, b_high, b_low):
    kwargs = dict(preferred_element_type=jnp.float32)
    return dot(a_high, b_high, **kwargs) + (dot(a_high, b_low, **kwargs) + dot(a_low, b_high, **kwargs))


def nt(a, b, **kwargs):
    return lax.dot_general(a, b, (((1,), (1,)), ((), ())), **kwargs)


def nn(a, b, **kwargs):
    return lax.dot_general(a, b, (((1,), (0,)), ((), ())), **kwargs)


def masked(tiles, axis, first, second):
    low_part = jnp.concatenate(tiles[:PB], axis=axis)
    high_part = jnp.concatenate(tiles[PB:], axis=axis)
    zero = jnp.zeros_like(low_part)
    return jnp.concatenate([jnp.where(first, low_part, zero), jnp.where(second, high_part, zero)], axis=axis)


def update_kernel(fetch, flags, plan, front_ref, cols_ref, lower_ref, high_ref, low_ref, *rest):
    refs = rest[:-10]
    out_ref, panel, raw_high, raw_low, col_high, col_low, solved, sol_high, sol_low, sems = rest[-10:]
    size = NC * BS
    half = PB * BS
    width = 2 * BS
    step = pl.program_id(0)
    col_blocks = cols_ref.shape[2]

    @pl.when(step == 0)
    def _():
        fetch(plan, refs, panel, sems)
        for b in range(col_blocks):
            at = slice(b * BS, (b + 1) * BS)
            raw = masked([cols_ref[c, :, b, :] for c in range(NC)], 0, flags[b, 3] != 0, flags[b, 4] != 0)
            high, low = split(raw)
            raw_high[:, at] = high
            raw_low[:, at] = low
        for m in range(0, size, width):
            deep = m + width
            value = three(nn, high_ref[m:deep, :deep], low_ref[m:deep, :deep], raw_high[:deep, :], raw_low[:deep, :])
            if m >= half:
                value = jnp.concatenate(
                    [
                        jnp.where(flags[b, 4] != 0, value[:, b * BS : (b + 1) * BS], 0.0)
                        for b in range(col_blocks)
                    ],
                    axis=1,
                )
            high, low = split(value)
            col_high[m:deep, :] = high
            col_low[m:deep, :] = low
        for c in range(NC):
            for k in range(2):
                pltpu.make_async_copy(panel.at[c, k], panel.at[c, k], sems.at[c, k]).wait()

    for k in range(2):
        a = step * 2 + k
        raw = masked([panel[c, k, step] for c in range(NC)], 1, flags[a, 0] != 0, flags[a, 1] != 0)
        high, low = split(raw)
        sol_high[k * BS : (k + 1) * BS, :] = high
        sol_low[k * BS : (k + 1) * BS, :] = low
    for m in range(0, size, width):
        deep = m + width
        value = three(nt, sol_high[:, :deep], sol_low[:, :deep], high_ref[m:deep, :deep], low_ref[m:deep, :deep])
        if m >= half:
            value = jnp.concatenate(
                [
                    jnp.where(flags[step * 2 + k, 1] != 0, value[k * BS : (k + 1) * BS, :], 0.0)
                    for k in range(2)
                ],
                axis=0,
            )
        solved[:, m:deep] = value
    high, low = split(solved[...])
    sol_high[...] = high
    sol_low[...] = low
    for b in range(0, col_blocks, 2):
        at = slice(b * BS, (b + 2) * BS)
        value = three(nn, sol_high[...], sol_low[...], col_high[:, at], col_low[:, at])
        for s in range(2):
            out_ref[:, b + s, :] = front_ref[:, b + s, :] - value[:, s * BS : (s + 1) * BS]
    for b in range(col_blocks):
        j = flags[b, 5]

        @pl.when(j >= 0)
        def _(b=b, j=j):
            at = pl.ds(pl.multiple_of(j * BS, BS), BS)
            for k in range(2):
                a = step * 2 + k
                rows = slice(k * BS, (k + 1) * BS)
                listed = jnp.where(j < PB, flags[a, 0], flags[a, 1])
                own = flags[a, 2]

                @pl.when(listed != 0)
                def _():
                    out_ref[rows, b, :] = solved[rows, at]

                @pl.when(jnp.logical_and(own >= 0, own // PB == j // PB))
                def _():
                    source = pl.ds(pl.multiple_of(own * BS, BS), BS)
                    inside = pl.ds(pl.multiple_of(j % PB * BS, BS), BS)
                    out_ref[rows, b, :] = lower_ref[source, inside]


def update_front(fetch, flags, plan, front, cols, lower, high, low, sources):
    row_blocks, _, col_blocks = front.shape[:3]
    size = NC * BS
    flops = 3 * 2 * row_blocks * BS * size * (col_blocks * BS + size)
    block = pl.BlockSpec((2 * BS, col_blocks, BS), lambda i: (i, 0, 0))
    return pl.pallas_call(
        functools.partial(update_kernel, fetch),
        out_shape=jax.ShapeDtypeStruct((row_blocks * BS, col_blocks, BS), jnp.float32),
        grid=(row_blocks // 2,),
        in_specs=[SMEM, SMEM, block] + [VMEM] * 4 + [HBM] * len(sources),
        out_specs=block,
        scratch_shapes=[
            pltpu.VMEM((NC, 2, row_blocks // 2, BS, BS), jnp.float32),
            pltpu.VMEM((size, col_blocks * BS), jnp.bfloat16),
            pltpu.VMEM((size, col_blocks * BS), jnp.bfloat16),
            pltpu.VMEM((size, col_blocks * BS), jnp.bfloat16),
            pltpu.VMEM((size, col_blocks * BS), jnp.bfloat16),
            pltpu.VMEM((2 * BS, size), jnp.float32),
            pltpu.VMEM((2 * BS, size), jnp.bfloat16),
            pltpu.VMEM((2 * BS, size), jnp.bfloat16),
            pltpu.SemaphoreType.DMA((NC, 2)),
        ],
        compiler_params=pltpu.CompilerParams(vmem_limit_bytes=ALMOST_ALL),
        cost_estimate=pl.CostEstimate(flops=flops, bytes_accessed=4 * 10**7, transcendentals=0),
        name="update_front",
    )(flags, plan, front.reshape(row_blocks * BS, col_blocks, BS), cols, lower, high, low, *sources)


def block_flags(slots, listed_one, listed_two, diag_slots):
    one = jnp.any(slots[:, None] == listed_one[None, :], axis=1).astype(jnp.int32)
    two = jnp.any(slots[:, None] == listed_two[None, :], axis=1).astype(jnp.int32)
    order = jnp.arange(1, NC + 1, dtype=jnp.int32)
    where = jnp.sum(jnp.where(slots[:, None] == diag_slots[None, :], order[None, :], 0), axis=1) - 1
    return jnp.stack([one, two, where], axis=1)


def gather_summed(front, block_slots, rows_first, rows_second):
    grid_rows, grid_cols = lax.axis_size("row"), lax.axis_size("col")
    own_row, own_col = lax.axis_index("row"), lax.axis_index("col")
    row_blocks, col_blocks = front.shape[0], front.shape[3]
    diag_slots = block_slots[:NC]
    listed_one = block_slots[rows_first]
    listed_two = block_slots[rows_second]
    row_slots = jnp.arange(row_blocks, dtype=jnp.int32) * grid_rows + own_row
    col_slots = jnp.arange(row_blocks, dtype=jnp.int32) * grid_cols + own_col
    flags = jnp.concatenate(
        [block_flags(slots, listed_one, listed_two, diag_slots) for slots in (row_slots, col_slots)], axis=1
    )
    flags = jnp.pad(flags, ((0, 0), (0, 2)))
    local = front.reshape(row_blocks, BS, col_blocks, BS)
    pieces = []
    rows = []
    for c in range(NC):
        piece = lax.dynamic_index_in_dim(local, diag_slots[c] // grid_cols, 2, keepdims=False)
        pieces.append(jnp.where(diag_slots[c] % grid_cols == own_col, piece, jnp.zeros_like(piece)))
        piece = lax.dynamic_index_in_dim(local, diag_slots[c] // grid_rows, 0, keepdims=False)
        rows.append(jnp.where(diag_slots[c] % grid_rows == own_row, piece, jnp.zeros_like(piece)))
    pieces = jnp.stack(pieces, axis=0)
    blocks = []
    for i in range(NC):
        part = lax.dynamic_index_in_dim(pieces, diag_slots[i] // grid_rows, 1, keepdims=False)[: i + 1]
        blocks.append(jnp.where(diag_slots[i] % grid_rows == own_row, part, jnp.zeros_like(part)))
    diag = lax.psum(jnp.concatenate(blocks, axis=0), ("row", "col"))
    panel = lax.psum(pieces, "col").reshape(NC, row_blocks // 2, 2, BS, BS)
    return flags, jnp.stack(rows, axis=0), diag, panel


def factor_panel(diag, hooks):
    lowers, inverses = [], []
    after = []
    for n in range(PB):
        lower, inverse, token = piece(n, diag, lowers, inverses, hooks(n, after))
        lowers.append(lower)
        inverses.append(inverse)
        after = [token]
    return lowers, inverses, after


def on_device(front, block_slots, rows_first, rows_second):
    if (lax.axis_size("row"), lax.axis_size("col")) != (4, 8):
        flags, rows, diag, panel = gather_summed(front, block_slots, rows_first, rows_second)
        cols = lax.psum(rows, "row")
        one = PB * (PB + 1) // 2
        nothing = lambda n, done: []
        lowers, inverses, _ = factor_panel(diag[:one], nothing)
        cross, corner = between(diag[one:], inverses, [])
        more_lowers, more_inverses, _ = factor_panel(corner, nothing)
        factors = finish(inverses, more_inverses, cross, lowers + more_lowers)
        out = update_front(fetch_rows, flags, flags, local_blocks(front), cols, *factors, [panel])
        return out.reshape(front.shape)

    flags, plan, rows, flat, chunks = start(front, block_slots, rows_first, rows_second)
    cols = lax.psum(rows, "row")
    mine, theirs_a, theirs_b = chunks
    extra_a = swap_core(theirs_a)
    extra_b = swap_core(theirs_b)
    right, left, right_other, left_other, sent = [], [], [], [], []

    def stream(after):
        step = len(right)
        own = (mine, extra_a, extra_b if step >= 2 else extra_a)
        to_right, to_left, token = choose(step, plan, own, right, left, after)
        right.append(permute(to_right, lambda p, q: (p, q + 2)))
        left.append(permute(to_left, lambda p, q: (p, q - 2)))
        right_other.append(swap_core(right[-1]))
        left_other.append(swap_core(left[-1]))
        sent.append(token)

    def hooks(n, after):
        if after:
            stream(after)
        return [sent[-1]]

    stream([])
    part, token = sum_first(flat[0], flat[1], [])
    stream([token])
    diag, token = join(sum_third(sum_second(part)))
    sibling = swap_core(mine)
    stream([token])
    lowers, inverses, after = factor_panel(diag, hooks)
    second, _ = sum_first(flat[2], flat[3], [sent[2]])
    second, _ = join(sum_third(sum_second(second)))
    stream(after)
    cross, corner = between(second, inverses, [sent[-1]])
    more_lowers, more_inverses, after = factor_panel(
        corner, lambda n, after: hooks(n, after) if n == 1 else [sent[-1]]
    )
    factors = finish(inverses, more_inverses, cross, lowers + more_lowers)

    def complete():
        steps = len(right)
        sources = [mine, extra_a, extra_b, theirs_a, theirs_b, sibling]
        sources += right + left + right_other + left_other
        fetch = functools.partial(fetch_streams, steps)
        return update_front(fetch, flags, plan, local_blocks(front), cols, *factors, sources)

    def longer():
        lists = (right, left, right_other, left_other, sent)
        kept = len(right)
        while len(right) < LONG:
            stream([])
        out = complete()
        for values in lists:
            del values[kept:]
        return out

    assert len(right) == SHORT
    out = lax.cond(plan[0, 6] > SHORT, longer, complete)
    return out.reshape(front.shape)


def local_blocks(front):
    return front.reshape(front.shape[0], BS, front.shape[3], BS)


def solution(mesh):
    placed = (P(None, "row", None, None, "col", None), P(), P(), P())
    return jax.shard_map(
        on_device,
        mesh=mesh,
        in_specs=placed,
        out_specs=P(None, "row", None, None, "col", None),
        check_vma=False,
    )
```

```python
import functools

import jax
import jax.numpy as jnp
from jax import lax
from jax.experimental import pallas as pl
from jax.experimental.pallas import tpu as pltpu
from jax.sharding import PartitionSpec as P

BS = 128
PB = 4
NC = 2 * PB
STEP = 4
ALMOST_ALL = 63 * 2**20
HIGHEST = lax.Precision.HIGHEST
HBM = pl.BlockSpec(memory_space=pltpu.HBM)
VMEM = pl.BlockSpec(memory_space=pltpu.VMEM)
SMEM = pl.BlockSpec(memory_space=pltpu.SMEM)


def lane_copy(tile, lane):
    return jnp.broadcast_to(tile[:, lane : lane + 1], tile.shape)


def row_copy(tile, row):
    return jnp.broadcast_to(tile[row : row + 1, :], tile.shape)


def factor_block(block):
    tiles = BS // 8
    sub = lax.broadcasted_iota(jnp.int32, (8, BS), 0)
    lanes = lax.broadcasted_iota(jnp.int32, (8, BS), 1)
    left = [block[8 * i : 8 * i + 8, :] for i in range(tiles)]
    right = [jnp.where(lanes == sub + 8 * i, 1.0, 0.0).astype(jnp.float32) for i in range(tiles)]
    upper = []
    inverse = []
    for j in range(0, BS, STEP):
        g, o = divmod(j, 8)
        if o == 0:
            upper_tile = jnp.zeros((8, BS), jnp.float32)
            inverse_tile = jnp.zeros((8, BS), jnp.float32)
        rows = [row_copy(left[g], o + s) for s in range(STEP)]
        extra = [row_copy(right[g], o + s) for s in range(STEP)]
        first = g if o + STEP < 8 else g + 1
        cols = {i: [lane_copy(left[i], j + s) for s in range(STEP)] for i in range(first, tiles)}
        pivot = [[lane_copy(rows[s], j + t) if t >= s else None for t in range(STEP)] for s in range(STEP)]
        ratio = [[None] * STEP for _ in range(STEP)]
        recip = []
        for s in range(STEP):
            inv = 1.0 / pivot[s][s]
            recip.append(inv)
            for t in range(s + 1, STEP):
                ratio[s][t] = pivot[s][t] * inv
            for t in range(s + 1, STEP):
                for u in range(t, STEP):
                    pivot[t][u] = pivot[t][u] - ratio[s][t] * pivot[s][u]
                rows[t] = rows[t] - ratio[s][t] * rows[s]
                extra[t] = extra[t] - ratio[s][t] * extra[s]
        for s in range(STEP):
            scale = lax.rsqrt(pivot[s][s])
            scale = scale * (1.5 - 0.5 * pivot[s][s] * scale * scale)
            here = sub == o + s
            upper_tile = jnp.where(here, rows[s] * scale, upper_tile)
            inverse_tile = jnp.where(here, extra[s] * scale, inverse_tile)
        if o + STEP == 8:
            upper.append(jnp.where(lanes >= sub + 8 * g, upper_tile, 0.0))
            inverse.append(jnp.where(lanes <= sub + 8 * g, inverse_tile, 0.0))
        for s in reversed(range(STEP)):
            rows[s] = rows[s] * recip[s]
            extra[s] = extra[s] * recip[s]
            for t in range(s + 1, STEP):
                rows[s] = rows[s] - ratio[s][t] * rows[t]
                extra[s] = extra[s] - ratio[s][t] * extra[t]
        for i in range(first, tiles):
            less = cols[i][0] * rows[0]
            less_extra = cols[i][0] * extra[0]
            for s in range(1, STEP):
                less = less + cols[i][s] * rows[s]
                less_extra = less_extra + cols[i][s] * extra[s]
            if i == g:
                below = sub >= o + STEP
                left[i] = jnp.where(below, left[i] - less, left[i])
                right[i] = jnp.where(below, right[i] - less_extra, right[i])
            else:
                left[i] = left[i] - less
                right[i] = right[i] - less_extra
    return jnp.concatenate(upper, axis=0), jnp.concatenate(inverse, axis=0)


def lower_index(i, j):
    return i * (i + 1) // 2 + j


def dot_nt(a, b):
    return lax.dot_general(a, b, (((1,), (1,)), ((), ())), precision=HIGHEST, preferred_element_type=jnp.float32)


def dot_nn(a, b):
    return lax.dot_general(a, b, (((1,), (0,)), ((), ())), precision=HIGHEST, preferred_element_type=jnp.float32)


def split(x):
    high = x.astype(jnp.bfloat16)
    return high, (x - high.astype(jnp.float32)).astype(jnp.bfloat16)


def place(count, core, block):
    half = count // 2
    return (block // half) == core, block % half


def start_kernel(slots, first, second, front_ref, flags, token, panel, keep, send, zero, blocks, columns, sems, out_sems):
    row_blocks, _, col_blocks = front_ref.shape[:3]
    grid_rows, grid_cols = 4, 8
    own_row = lax.axis_index("row")
    own_col = lax.axis_index("col")
    core = own_col % 2
    slot = [slots[i] for i in range(NC)]
    count = NC * (NC + 1) // 2
    half = count // 2
    moves = []
    fills = []

    def move(condition, source, middle, targets):
        index = len(moves)

        @pl.when(condition)
        def _():
            pltpu.make_async_copy(source, middle, sems.at[index]).start()

        moves.append((condition, middle, targets, index))

    always = core >= 0
    group = zero.shape[0]
    for c in range(NC):
        owned = slot[c] % grid_cols == own_col
        for a in range(0, row_blocks, group):
            fills.append((jnp.logical_not(owned), zero, panel.at[c, a : a + group], len(moves)))
        move(owned, front_ref.at[:, :, slot[c] // grid_cols], columns.at[c], ((panel.at[c], always),))
    for i in range(NC):
        for j in range(i + 1):
            block = lower_index(i, j)
            a = slot[i] // grid_rows
            b = slot[j] // grid_cols
            owned = jnp.logical_and(slot[i] % grid_rows == own_row, slot[j] % grid_cols == own_col)
            stay = core == block // half
            targets = ((keep.at[block % half], stay), (send.at[block % half], jnp.logical_not(stay)))
            for target, chosen in targets:
                fills.append((jnp.logical_and(chosen, jnp.logical_not(owned)), zero.at[0], target, len(moves)))
            move(owned, front_ref.at[a, :, b], blocks.at[block], targets)

    zero[...] = jnp.zeros_like(zero)
    for condition, source, target, index in fills:
        @pl.when(condition)
        def _(source=source, target=target, index=index):
            pltpu.make_async_copy(source, target, out_sems.at[index]).start()

    for a in range(row_blocks):
        for f in range(8):
            flags[a, f] = jnp.int32(-1 if f in (2, 5) else 0)
    for c in range(NC):
        @pl.when(slot[c] % grid_rows == own_row)
        def _(c=c):
            flags[slot[c] // grid_rows, 2] = jnp.int32(c)

        @pl.when(slot[c] % grid_cols == own_col)
        def _(c=c):
            flags[slot[c] // grid_cols, 5] = jnp.int32(c)

    for listed, f in ((first, 0), (second, 1)):
        @pl.loop(0, listed.shape[0])
        def _(i, listed=listed, f=f):
            s = slots[listed[i]]

            @pl.when(s % grid_rows == own_row)
            def _():
                flags[s // grid_rows, f] = jnp.int32(1)

            @pl.when(s % grid_cols == own_col)
            def _():
                flags[s // grid_cols, 3 + f] = jnp.int32(1)

    token[0] = jnp.int32(0)
    for condition, middle, targets, index in moves:
        @pl.when(condition)
        def _(middle=middle, targets=targets, index=index):
            pltpu.make_async_copy(middle, middle, sems.at[index]).wait()
            for target, chosen in targets:
                @pl.when(chosen)
                def _(target=target):
                    pltpu.make_async_copy(middle, target, out_sems.at[index]).start()
    for condition, middle, targets, index in moves:
        pltpu.make_async_copy(middle, middle, out_sems.at[index]).wait()


TOKEN = jax.ShapeDtypeStruct((1,), jnp.int32)


def start(front, block_slots, rows_first, rows_second):
    row_blocks, col_blocks = front.shape[0], front.shape[3]
    count = NC * (NC + 1) // 2
    f32 = lambda *shape: jax.ShapeDtypeStruct(shape, jnp.float32)
    flags, token, panel, keep, send = pl.pallas_call(
        start_kernel,
        out_shape=(
            jax.ShapeDtypeStruct((row_blocks, 8), jnp.int32),
            TOKEN,
            f32(NC, row_blocks, BS, 1, BS),
            f32(count // 2, BS, 1, BS),
            f32(count // 2, BS, 1, BS),
        ),
        in_specs=[SMEM, SMEM, SMEM, HBM],
        out_specs=(SMEM, SMEM) + (HBM,) * 3,
        scratch_shapes=[
            pltpu.VMEM((row_blocks // 4, BS, 1, BS), jnp.float32),
            pltpu.VMEM((count, BS, 1, BS), jnp.float32),
            pltpu.VMEM((NC, row_blocks, BS, 1, BS), jnp.float32),
            pltpu.SemaphoreType.DMA((count + NC,)),
            pltpu.SemaphoreType.DMA((count + NC,)),
        ],
        compiler_params=pltpu.CompilerParams(vmem_limit_bytes=ALMOST_ALL),
        name="start",
    )(block_slots, rows_first, rows_second, front.reshape(row_blocks, BS, col_blocks, 1, BS))
    return flags, token, panel.reshape(NC, row_blocks, BS, BS), keep.reshape(-1, BS), send.reshape(-1, BS)


def lines_kernel(slots, after, wide_ref, one, two, token, zero, lines, sems, out_sems):
    own_row = lax.axis_index("row")
    owned = [slots[c] % 4 == own_row for c in range(NC)]
    targets = [(one if c < PB else two).at[c % PB] for c in range(NC)]
    for c in range(NC):
        @pl.when(owned[c])
        def _(c=c):
            pltpu.make_async_copy(wide_ref.at[slots[c] // 4], lines.at[c], sems.at[c]).start()
    zero[...] = jnp.zeros_like(zero)
    for c in range(NC):
        @pl.when(jnp.logical_not(owned[c]))
        def _(c=c):
            pltpu.make_async_copy(zero, targets[c], out_sems.at[c]).start()
    for c in range(NC):
        @pl.when(owned[c])
        def _(c=c):
            pltpu.make_async_copy(lines.at[c], lines.at[c], sems.at[c]).wait()
            pltpu.make_async_copy(lines.at[c], targets[c], out_sems.at[c]).start()
    token[0] = jnp.int32(0)
    for c in range(NC):
        pltpu.make_async_copy(zero, targets[c], out_sems.at[c]).wait()


def lines(front, block_slots, after):
    row_blocks, col_blocks = front.shape[0], front.shape[3]
    part = jax.ShapeDtypeStruct((PB, BS, col_blocks, BS), jnp.float32)
    return pl.pallas_call(
        lines_kernel,
        out_shape=(part, part, TOKEN),
        in_specs=[SMEM, SMEM, HBM],
        out_specs=(HBM, HBM, SMEM),
        scratch_shapes=[
            pltpu.VMEM((BS, col_blocks, BS), jnp.float32),
            pltpu.VMEM((NC, BS, col_blocks, BS), jnp.float32),
            pltpu.SemaphoreType.DMA((NC,)),
            pltpu.SemaphoreType.DMA((NC,)),
        ],
        name="lines",
    )(block_slots, after, local_blocks(front))


def add_kernel(after, a, b, c, d, first, second, token):
    first[...] = a[...] + b[...]
    second[...] = c[...] + d[...]

    @pl.when(pl.program_id(0) == 0)
    def _():
        token[0] = jnp.int32(0)


def add_pairs(a, b, c, d, after):
    block = pl.BlockSpec((1,) + a.shape[1:], lambda i: (i,) + (0,) * (a.ndim - 1))
    return pl.pallas_call(
        add_kernel,
        out_shape=(jax.ShapeDtypeStruct(a.shape, a.dtype),) * 2 + (TOKEN,),
        grid=(a.shape[0],),
        in_specs=[SMEM] + [block] * 4,
        out_specs=(block, block, SMEM),
        name="add_pairs",
    )(after, a, b, c, d)


def permute(value, flip):
    pairs = []
    for p in range(4):
        for q in range(8):
            to_p, to_q = flip(p, q)
            if 0 <= to_q < 8:
                pairs.append((p * 8 + q, to_p * 8 + to_q))
    return lax.ppermute(value, ("row", "col"), pairs)


def swap_core(value):
    return permute(value, lambda p, q: (p, q ^ 1))


def place(axis):
    return lax.axis_index("row") if axis == "row" else lax.axis_index("col") // 2


def spread_kernel(axis, count, *refs):
    total = refs[-1]
    outs = refs[count:-1]
    value = refs[0][...]
    for ref in refs[1:count]:
        value = value + ref[...]
    total[...] = value
    own = place(axis)
    for d in range(4):
        outs[d][...] = total[own ^ d]


def spread(axis, terms):
    rows = terms[0].shape[0] // 4
    shape = (4, rows, BS)
    return pl.pallas_call(
        functools.partial(spread_kernel, axis, len(terms)),
        out_shape=(jax.ShapeDtypeStruct((rows, BS), jnp.float32),) * 4,
        in_specs=[VMEM] * len(terms),
        out_specs=(VMEM,) * 4,
        scratch_shapes=[pltpu.VMEM(shape, jnp.float32)],
        name="spread",
    )(*[term.reshape(shape) for term in terms])


def collect_kernel(axis, own, one, two, three, out):
    at = place(axis)
    for d, source in enumerate((own, one, two, three)):
        out[at ^ d] = source[...]


def collect(axis, own, others):
    rows = own.shape[0]
    out = pl.pallas_call(
        functools.partial(collect_kernel, axis),
        out_shape=jax.ShapeDtypeStruct((4, rows, BS), jnp.float32),
        in_specs=[VMEM] * 4,
        out_specs=VMEM,
        name="collect",
    )(own, *others)
    return out.reshape(4 * rows, BS)


def join_kernel(own, other, first, second, token):
    core = lax.axis_index("col") % 2
    one = first.shape[0]
    half = own.shape[0]
    for which, low, high in ((0, own, other), (1, other, own)):
        @pl.when(core == which)
        def _(low=low, high=high):
            first[...] = low[:one]
            second[: half - one] = low[one:]
            second[half - one :] = high[...]
    token[0] = jnp.int32(0)


def join(own):
    other = swap_core(own)
    one = PB * (PB + 1) // 2
    count = NC * (NC + 1) // 2
    block = lambda n: jax.ShapeDtypeStruct((n, BS, BS), jnp.float32)
    return pl.pallas_call(
        join_kernel,
        out_shape=(block(one), block(count - one), TOKEN),
        in_specs=[VMEM] * 2,
        out_specs=(VMEM, VMEM, SMEM),
        name="join",
    )(own.reshape(-1, BS, BS), other.reshape(-1, BS, BS))


def across(axis, parts):
    if axis == "row":
        return [permute(parts[d - 1], lambda p, q, d=d: (p ^ d, q)) for d in range(1, 4)]
    return [permute(parts[d - 1], lambda p, q, d=d: (p, q ^ (2 * d))) for d in range(1, 4)]


def sum_square(keep, send):
    own, *parts = spread("row", [keep, swap_core(send)])
    own, *parts = spread("col", [own] + across("row", parts))
    got = across("col", parts)
    value = own + got[0] + got[1] + got[2]
    for axis in ("col", "row"):
        value = collect(axis, value, across(axis, [value] * 3))
    return join(value)


def piece_kernel(n, diag, *rest):
    lowers = rest[:n]
    inverses = rest[n : 2 * n]
    lower_out, inverse_out, token = rest[-3:]
    token[0] = jnp.int32(0)

    def row(i):
        return jnp.concatenate([lowers[j][(i - j) * BS : (i - j + 1) * BS, :] for j in range(n)], axis=1)

    column = []
    for i in range(n, PB):
        value = diag[lower_index(i, n)]
        if n:
            value = value - dot_nt(row(i), row(n))
        column.append(value)
    upper, inverse = factor_block(column[0])
    lower_out[0:BS, :] = upper.T
    if n + 1 < PB:
        lower_out[BS:, :] = dot_nt(jnp.concatenate(column[1:], axis=0), inverse)
    inverse_out[:, n * BS :] = inverse
    if n:
        before = jnp.concatenate(
            [
                jnp.concatenate([inverses[j][...], jnp.zeros((BS, (n - 1 - j) * BS), jnp.float32)], axis=1)
                if j + 1 < n
                else inverses[j][...]
                for j in range(n)
            ],
            axis=0,
        )
        inverse_out[:, : n * BS] = -dot_nn(inverse, dot_nn(row(n), before))


def piece(n, diag, lowers, inverses, after):
    return pl.pallas_call(
        functools.partial(piece_kernel, n),
        out_shape=(
            jax.ShapeDtypeStruct(((PB - n) * BS, BS), jnp.float32),
            jax.ShapeDtypeStruct((BS, (n + 1) * BS), jnp.float32),
            TOKEN,
        ),
        in_specs=[VMEM] * (1 + 2 * n) + [SMEM] * len(after),
        out_specs=(VMEM, VMEM, SMEM),
        compiler_params=pltpu.CompilerParams(vmem_limit_bytes=32 * 2**20),
        cost_estimate=pl.CostEstimate(flops=10**8, bytes_accessed=10**5, transcendentals=0),
        name="factor_piece",
    )(diag, *lowers, *inverses, *after)


def inverse_rows(inverses):
    rows = []
    for j in range(PB):
        if j + 1 < PB:
            rows.append(jnp.concatenate([inverses[j][...], jnp.zeros((BS, (PB - 1 - j) * BS), jnp.float32)], axis=1))
        else:
            rows.append(inverses[j][...])
    return jnp.concatenate(rows, axis=0)


def between_kernel(diag, *rest):
    inverses = rest[:PB]
    cross_out, rest_out = rest[-2:]
    inverse = inverse_rows(inverses)
    one = PB * (PB + 1) // 2
    left = [
        jnp.concatenate([diag[lower_index(i, j) - one] for j in range(PB)], axis=1) for i in range(PB, NC)
    ]
    cross = dot_nt(jnp.concatenate(left, axis=0), inverse)
    cross_out[...] = cross
    for i in range(PB):
        here = cross[i * BS : (i + 1) * BS, :]
        product = dot_nt(here, cross[: (i + 1) * BS, :])
        for j in range(i + 1):
            block = diag[lower_index(i + PB, j + PB) - one]
            rest_out[lower_index(i, j)] = block - product[:, j * BS : (j + 1) * BS]


def between(diag, inverses, after):
    return pl.pallas_call(
        between_kernel,
        out_shape=(
            jax.ShapeDtypeStruct((PB * BS, PB * BS), jnp.float32),
            jax.ShapeDtypeStruct((PB * (PB + 1) // 2, BS, BS), jnp.float32),
        ),
        in_specs=[VMEM] * (1 + PB) + [SMEM] * len(after),
        out_specs=(VMEM, VMEM),
        compiler_params=pltpu.CompilerParams(vmem_limit_bytes=32 * 2**20),
        cost_estimate=pl.CostEstimate(flops=10**8, bytes_accessed=10**5, transcendentals=0),
        name="between",
    )(diag, *inverses, *after)


def finish_kernel(*refs):
    first = inverse_rows(refs[:PB])
    second = inverse_rows(refs[PB : 2 * PB])
    cross = refs[2 * PB][...]
    lowers = refs[2 * PB + 1 : 4 * PB + 1]
    lower_out, high_out, low_out = refs[-3:]
    size = PB * BS
    lower_out[...] = jnp.zeros_like(lower_out)
    for j in range(PB):
        for half in range(2):
            rows = slice(half * size + j * BS, (half + 1) * size)
            lower_out[rows, j * BS : (j + 1) * BS] = lowers[half * PB + j][...]
    high_out[:size, size:] = jnp.zeros((size, size), jnp.bfloat16)
    low_out[:size, size:] = jnp.zeros((size, size), jnp.bfloat16)
    corner = -dot_nn(second, dot_nn(cross, first))
    for value, rows, cols in (
        (first, slice(0, size), slice(0, size)),
        (corner, slice(size, 2 * size), slice(0, size)),
        (second, slice(size, 2 * size), slice(size, 2 * size)),
    ):
        high, low = split(value)
        high_out[rows, cols] = high
        low_out[rows, cols] = low


def finish(first, second, cross, lowers):
    size = NC * BS
    return pl.pallas_call(
        finish_kernel,
        out_shape=(jax.ShapeDtypeStruct((size, size // 2), jnp.float32),)
        + (jax.ShapeDtypeStruct((size, size), jnp.bfloat16),) * 2,
        in_specs=[VMEM] * (4 * PB + 1),
        out_specs=(VMEM,) * 3,
        compiler_params=pltpu.CompilerParams(vmem_limit_bytes=32 * 2**20),
        cost_estimate=pl.CostEstimate(flops=10**8, bytes_accessed=10**5, transcendentals=0),
        name="finish",
    )(*first, *second, cross, *lowers)


def three(dot, a_high, a_low, b_high, b_low):
    kwargs = dict(preferred_element_type=jnp.float32)
    return dot(a_high, b_high, **kwargs) + (dot(a_high, b_low, **kwargs) + dot(a_low, b_high, **kwargs))


def nt(a, b, **kwargs):
    return lax.dot_general(a, b, (((1,), (1,)), ((), ())), **kwargs)


def nn(a, b, **kwargs):
    return lax.dot_general(a, b, (((1,), (0,)), ((), ())), **kwargs)


def masked(tiles, axis, first, second):
    low_part = jnp.concatenate(tiles[:PB], axis=axis)
    high_part = jnp.concatenate(tiles[PB:], axis=axis)
    zero = jnp.zeros_like(low_part)
    return jnp.concatenate([jnp.where(first, low_part, zero), jnp.where(second, high_part, zero)], axis=axis)


def columns_kernel(flags, one, one_more, two, two_more, high_ref, low_ref, col_high, col_low, raw_high, raw_low):
    size = NC * BS
    half = PB * BS
    width = 2 * BS
    col_blocks = one.shape[2]
    for b in range(col_blocks):
        at = slice(b * BS, (b + 1) * BS)
        tiles = [one[c, :, b, :] + one_more[c, :, b, :] for c in range(PB)]
        tiles += [two[c, :, b, :] + two_more[c, :, b, :] for c in range(PB)]
        raw = masked(tiles, 0, flags[b, 3] != 0, flags[b, 4] != 0)
        high, low = split(raw)
        raw_high[:, at] = high
        raw_low[:, at] = low
    for m in range(0, size, width):
        deep = m + width
        value = three(nn, high_ref[m:deep, :deep], low_ref[m:deep, :deep], raw_high[:deep, :], raw_low[:deep, :])
        if m >= half:
            value = jnp.concatenate(
                [jnp.where(flags[b, 4] != 0, value[:, b * BS : (b + 1) * BS], 0.0) for b in range(col_blocks)],
                axis=1,
            )
        high, low = split(value)
        col_high[m:deep, :] = high
        col_low[m:deep, :] = low


def solve_columns(flags, one, one_more, two, two_more, high, low):
    size = NC * BS
    shape = (size, one.shape[2] * BS)
    return pl.pallas_call(
        columns_kernel,
        out_shape=(jax.ShapeDtypeStruct(shape, jnp.bfloat16),) * 2,
        in_specs=[SMEM] + [VMEM] * 6,
        out_specs=(VMEM, VMEM),
        scratch_shapes=[pltpu.VMEM(shape, jnp.bfloat16), pltpu.VMEM(shape, jnp.bfloat16)],
        compiler_params=pltpu.CompilerParams(vmem_limit_bytes=48 * 2**20),
        cost_estimate=pl.CostEstimate(flops=10**9, bytes_accessed=10**6, transcendentals=0),
        name="solve_columns",
    )(flags, one, one_more, two, two_more, high, low)


def update_kernel(flags, front_ref, rows_ref, lower_ref, high_ref, low_ref, col_high, col_low, out_ref,
                  solved, sol_high, sol_low):
    size = NC * BS
    half = PB * BS
    width = 2 * BS
    step = pl.program_id(0)
    col_blocks = front_ref.shape[1]
    for k in range(2):
        a = step * 2 + k
        raw = masked([rows_ref[c, k] for c in range(NC)], 1, flags[a, 0] != 0, flags[a, 1] != 0)
        high, low = split(raw)
        sol_high[k * BS : (k + 1) * BS, :] = high
        sol_low[k * BS : (k + 1) * BS, :] = low
    for m in range(0, size, width):
        deep = m + width
        value = three(nt, sol_high[:, :deep], sol_low[:, :deep], high_ref[m:deep, :deep], low_ref[m:deep, :deep])
        if m >= half:
            value = jnp.concatenate(
                [
                    jnp.where(flags[step * 2 + k, 1] != 0, value[k * BS : (k + 1) * BS, :], 0.0)
                    for k in range(2)
                ],
                axis=0,
            )
        solved[:, m:deep] = value
    high, low = split(solved[...])
    sol_high[...] = high
    sol_low[...] = low
    for b in range(0, col_blocks, 2):
        at = slice(b * BS, (b + 2) * BS)
        value = three(nn, sol_high[...], sol_low[...], col_high[:, at], col_low[:, at])
        for s in range(2):
            out_ref[:, b + s, :] = front_ref[:, b + s, :] - value[:, s * BS : (s + 1) * BS]
    for b in range(col_blocks):
        j = flags[b, 5]

        @pl.when(j >= 0)
        def _(b=b, j=j):
            at = pl.ds(pl.multiple_of(j * BS, BS), BS)
            for k in range(2):
                a = step * 2 + k
                rows = slice(k * BS, (k + 1) * BS)
                listed = jnp.where(j < PB, flags[a, 0], flags[a, 1])
                own = flags[a, 2]

                @pl.when(listed != 0)
                def _():
                    out_ref[rows, b, :] = solved[rows, at]

                @pl.when(jnp.logical_and(own >= 0, own // PB == j // PB))
                def _():
                    source = pl.ds(pl.multiple_of(own * BS, BS), BS)
                    inside = pl.ds(pl.multiple_of(j % PB * BS, BS), BS)
                    out_ref[rows, b, :] = lower_ref[source, inside]


def update_front(flags, front, rows, lower, high, low, col_high, col_low):
    row_blocks, _, col_blocks = front.shape[:3]
    size = NC * BS
    block = pl.BlockSpec((2 * BS, col_blocks, BS), lambda i: (i, 0, 0))
    return pl.pallas_call(
        update_kernel,
        out_shape=jax.ShapeDtypeStruct((row_blocks * BS, col_blocks, BS), jnp.float32),
        grid=(row_blocks // 2,),
        in_specs=[SMEM, block, pl.BlockSpec((NC, 2, BS, BS), lambda i: (0, i, 0, 0))] + [VMEM] * 5,
        out_specs=block,
        scratch_shapes=[
            pltpu.VMEM((2 * BS, size), jnp.float32),
            pltpu.VMEM((2 * BS, size), jnp.bfloat16),
            pltpu.VMEM((2 * BS, size), jnp.bfloat16),
        ],
        compiler_params=pltpu.CompilerParams(vmem_limit_bytes=40 * 2**20),
        cost_estimate=pl.CostEstimate(flops=10**9, bytes_accessed=10**6, transcendentals=0),
        name="update_front",
    )(flags, front.reshape(row_blocks * BS, col_blocks, BS), rows, lower, high, low, col_high, col_low)


def block_flags(slots, listed_one, listed_two, diag_slots):
    one = jnp.any(slots[:, None] == listed_one[None, :], axis=1).astype(jnp.int32)
    two = jnp.any(slots[:, None] == listed_two[None, :], axis=1).astype(jnp.int32)
    order = jnp.arange(1, NC + 1, dtype=jnp.int32)
    where = jnp.sum(jnp.where(slots[:, None] == diag_slots[None, :], order[None, :], 0), axis=1) - 1
    return jnp.stack([one, two, where], axis=1)


def gather_summed(front, block_slots, rows_first, rows_second):
    grid_rows, grid_cols = lax.axis_size("row"), lax.axis_size("col")
    own_row, own_col = lax.axis_index("row"), lax.axis_index("col")
    row_blocks, col_blocks = front.shape[0], front.shape[3]
    diag_slots = block_slots[:NC]
    listed_one = block_slots[rows_first]
    listed_two = block_slots[rows_second]
    row_slots = jnp.arange(row_blocks, dtype=jnp.int32) * grid_rows + own_row
    col_slots = jnp.arange(row_blocks, dtype=jnp.int32) * grid_cols + own_col
    flags = jnp.concatenate(
        [block_flags(slots, listed_one, listed_two, diag_slots) for slots in (row_slots, col_slots)], axis=1
    )
    flags = jnp.pad(flags, ((0, 0), (0, 2)))
    local = front.reshape(row_blocks, BS, col_blocks, BS)
    pieces = []
    rows = []
    for c in range(NC):
        piece = lax.dynamic_index_in_dim(local, diag_slots[c] // grid_cols, 2, keepdims=False)
        pieces.append(jnp.where(diag_slots[c] % grid_cols == own_col, piece, jnp.zeros_like(piece)))
        piece = lax.dynamic_index_in_dim(local, diag_slots[c] // grid_rows, 0, keepdims=False)
        rows.append(jnp.where(diag_slots[c] % grid_rows == own_row, piece, jnp.zeros_like(piece)))
    pieces = jnp.stack(pieces, axis=0)
    blocks = []
    for i in range(NC):
        part = lax.dynamic_index_in_dim(pieces, diag_slots[i] // grid_rows, 1, keepdims=False)[: i + 1]
        blocks.append(jnp.where(diag_slots[i] % grid_rows == own_row, part, jnp.zeros_like(part)))
    diag = lax.psum(jnp.concatenate(blocks, axis=0), ("row", "col"))
    return flags, lax.psum(jnp.stack(rows, axis=0), "row"), diag, lax.psum(pieces, "col")


def factor_panel(diag, after, hooks):
    lowers, inverses = [], []
    for n in range(PB):
        lower, inverse, token = piece(n, diag, lowers, inverses, hooks(n, after))
        lowers.append(lower)
        inverses.append(inverse)
        after = [token]
    return lowers, inverses, after


def on_device(front, block_slots, rows_first, rows_second):
    simple = (lax.axis_size("row"), lax.axis_size("col")) != (4, 8)
    nothing = lambda n, after: after
    if simple:
        flags, cols, diag, panel = gather_summed(front, block_slots, rows_first, rows_second)
        one = PB * (PB + 1) // 2
        diag, second = diag[:one], diag[one:]
        token = jnp.zeros((1,), jnp.int32)
    else:
        flags, _, panel, keep, send = start(front, block_slots, rows_first, rows_second)
        panel = lax.psum(panel, "col")
        diag, second, token = sum_square(keep, send)
        lines_one, lines_two, token = lines(front, block_slots, token)
        got_one = permute(lines_one, lambda p, q: (p ^ 1, q))
        got_two = permute(lines_two, lambda p, q: (p ^ 2, q))
    lowers, inverses, after = factor_panel(diag, [token], nothing)
    cross, corner = between(second, inverses, after)

    def half_way(n, after):
        if n != 1 or simple:
            return after
        sums.extend(add_pairs(lines_one, got_one, lines_two, got_two, after[0]))
        sums.append(permute(sums[0], lambda p, q: (p ^ 2, q)))
        sums.append(permute(sums[1], lambda p, q: (p ^ 1, q)))
        return [sums[2]]

    sums = []
    more_lowers, more_inverses, _ = factor_panel(corner, [], half_way)
    lower, high, low = finish(inverses, more_inverses, cross, lowers + more_lowers)
    if simple:
        parts = [cols[:PB], jnp.zeros_like(cols[:PB]), cols[PB:], jnp.zeros_like(cols[PB:])]
    else:
        parts = [sums[0], sums[3], sums[1], sums[4]]
    col_high, col_low = solve_columns(flags, *parts, high, low)
    out = update_front(flags, local_blocks(front), panel, lower, high, low, col_high, col_low)
    return out.reshape(front.shape)


def local_blocks(front):
    return front.reshape(front.shape[0], BS, front.shape[3], BS)


def solution(mesh):
    placed = (P(None, "row", None, None, "col", None), P(), P(), P())
    return jax.shard_map(
        on_device,
        mesh=mesh,
        in_specs=placed,
        out_specs=P(None, "row", None, None, "col", None),
        check_vma=False,
    )
```

```python
import functools

import jax
import jax.numpy as jnp
from jax import lax
from jax.experimental import pallas as pl
from jax.experimental.pallas import tpu as pltpu
from jax.sharding import PartitionSpec as P

BS = 128
PB = 4
NC = 2 * PB
STEP = 8
ALMOST_ALL = 63 * 2**20
HIGHEST = lax.Precision.HIGHEST
HBM = pl.BlockSpec(memory_space=pltpu.HBM)
VMEM = pl.BlockSpec(memory_space=pltpu.VMEM)
SMEM = pl.BlockSpec(memory_space=pltpu.SMEM)


def lane_copy(tile, lane):
    return jnp.broadcast_to(tile[:, lane : lane + 1], tile.shape)


def row_copy(tile, row):
    return jnp.broadcast_to(tile[row : row + 1, :], tile.shape)


def factor_block(block):
    tiles = BS // 8
    sub = lax.broadcasted_iota(jnp.int32, (8, BS), 0)
    lanes = lax.broadcasted_iota(jnp.int32, (8, BS), 1)
    left = [block[8 * i : 8 * i + 8, :] for i in range(tiles)]
    right = [jnp.where(lanes == sub + 8 * i, 1.0, 0.0).astype(jnp.float32) for i in range(tiles)]
    upper = []
    inverse = []
    for j in range(0, BS, STEP):
        g, o = divmod(j, 8)
        if o == 0:
            upper_tile = jnp.zeros((8, BS), jnp.float32)
            inverse_tile = jnp.zeros((8, BS), jnp.float32)
        rows = [row_copy(left[g], o + s) for s in range(STEP)]
        extra = [row_copy(right[g], o + s) for s in range(STEP)]
        first = g if o + STEP < 8 else g + 1
        cols = {i: [lane_copy(left[i], j + s) for s in range(STEP)] for i in range(first, tiles)}
        pivot = [[lane_copy(rows[s], j + t) if t >= s else None for t in range(STEP)] for s in range(STEP)]
        ratio = [[None] * STEP for _ in range(STEP)]
        recip = []
        for s in range(STEP):
            inv = 1.0 / pivot[s][s]
            recip.append(inv)
            for t in range(s + 1, STEP):
                ratio[s][t] = pivot[s][t] * inv
            for t in range(s + 1, STEP):
                for u in range(t, STEP):
                    pivot[t][u] = pivot[t][u] - ratio[s][t] * pivot[s][u]
                rows[t] = rows[t] - ratio[s][t] * rows[s]
                extra[t] = extra[t] - ratio[s][t] * extra[s]
        for s in range(STEP):
            scale = lax.rsqrt(pivot[s][s])
            scale = scale * (1.5 - 0.5 * pivot[s][s] * scale * scale)
            here = sub == o + s
            upper_tile = jnp.where(here, rows[s] * scale, upper_tile)
            inverse_tile = jnp.where(here, extra[s] * scale, inverse_tile)
        if o + STEP == 8:
            upper.append(jnp.where(lanes >= sub + 8 * g, upper_tile, 0.0))
            inverse.append(jnp.where(lanes <= sub + 8 * g, inverse_tile, 0.0))
        for s in reversed(range(STEP)):
            rows[s] = rows[s] * recip[s]
            extra[s] = extra[s] * recip[s]
            for t in range(s + 1, STEP):
                rows[s] = rows[s] - ratio[s][t] * rows[t]
                extra[s] = extra[s] - ratio[s][t] * extra[t]
        for i in range(first, tiles):
            less = cols[i][0] * rows[0]
            less_extra = cols[i][0] * extra[0]
            for s in range(1, STEP):
                less = less + cols[i][s] * rows[s]
                less_extra = less_extra + cols[i][s] * extra[s]
            if i == g:
                below = sub >= o + STEP
                left[i] = jnp.where(below, left[i] - less, left[i])
                right[i] = jnp.where(below, right[i] - less_extra, right[i])
            else:
                left[i] = left[i] - less
                right[i] = right[i] - less_extra
    return jnp.concatenate(upper, axis=0), jnp.concatenate(inverse, axis=0)


def lower_index(i, j):
    return i * (i + 1) // 2 + j


def dot_nt(a, b):
    return lax.dot_general(a, b, (((1,), (1,)), ((), ())), precision=HIGHEST, preferred_element_type=jnp.float32)


def dot_nn(a, b):
    return lax.dot_general(a, b, (((1,), (0,)), ((), ())), precision=HIGHEST, preferred_element_type=jnp.float32)


def split(x):
    high = x.astype(jnp.bfloat16)
    return high, (x - high.astype(jnp.float32)).astype(jnp.bfloat16)


def place(count, core, block):
    half = count // 2
    return (block // half) == core, block % half


def start_kernel(slots, first, second, front_ref, flags, token, panel, keep, send, zero, blocks, columns, sems, out_sems):
    row_blocks, _, col_blocks = front_ref.shape[:3]
    grid_rows, grid_cols = 4, 8
    own_row = lax.axis_index("row")
    own_col = lax.axis_index("col")
    core = own_col % 2
    slot = [slots[i] for i in range(NC)]
    count = NC * (NC + 1) // 2
    half = count // 2
    moves = []
    fills = []

    def move(condition, source, middle, targets):
        index = len(moves)

        @pl.when(condition)
        def _():
            pltpu.make_async_copy(source, middle, sems.at[index]).start()

        moves.append((condition, middle, targets, index))

    always = core >= 0
    group = zero.shape[0]
    for c in range(NC):
        owned = slot[c] % grid_cols == own_col
        for a in range(0, row_blocks, group):
            fills.append((jnp.logical_not(owned), zero, panel.at[c, a : a + group], len(moves)))
        move(owned, front_ref.at[:, :, slot[c] // grid_cols], columns.at[c], ((panel.at[c], always),))
    for i in range(NC):
        for j in range(i + 1):
            block = lower_index(i, j)
            a = slot[i] // grid_rows
            b = slot[j] // grid_cols
            owned = jnp.logical_and(slot[i] % grid_rows == own_row, slot[j] % grid_cols == own_col)
            stay = core == block // half
            targets = ((keep.at[block % half], stay), (send.at[block % half], jnp.logical_not(stay)))
            for target, chosen in targets:
                fills.append((jnp.logical_and(chosen, jnp.logical_not(owned)), zero.at[0], target, len(moves)))
            move(owned, front_ref.at[a, :, b], blocks.at[block], targets)

    zero[...] = jnp.zeros_like(zero)
    for condition, source, target, index in fills:
        @pl.when(condition)
        def _(source=source, target=target, index=index):
            pltpu.make_async_copy(source, target, out_sems.at[index]).start()

    for a in range(row_blocks):
        for f in range(8):
            flags[a, f] = jnp.int32(-1 if f in (2, 5) else 0)
    for c in range(NC):
        @pl.when(slot[c] % grid_rows == own_row)
        def _(c=c):
            flags[slot[c] // grid_rows, 2] = jnp.int32(c)

        @pl.when(slot[c] % grid_cols == own_col)
        def _(c=c):
            flags[slot[c] // grid_cols, 5] = jnp.int32(c)

    for listed, f in ((first, 0), (second, 1)):
        @pl.loop(0, listed.shape[0])
        def _(i, listed=listed, f=f):
            s = slots[listed[i]]

            @pl.when(s % grid_rows == own_row)
            def _():
                flags[s // grid_rows, f] = jnp.int32(1)

            @pl.when(s % grid_cols == own_col)
            def _():
                flags[s // grid_cols, 3 + f] = jnp.int32(1)

    token[0] = jnp.int32(0)
    for condition, middle, targets, index in moves:
        @pl.when(condition)
        def _(middle=middle, targets=targets, index=index):
            pltpu.make_async_copy(middle, middle, sems.at[index]).wait()
            for target, chosen in targets:
                @pl.when(chosen)
                def _(target=target):
                    pltpu.make_async_copy(middle, target, out_sems.at[index]).start()
    for condition, middle, targets, index in moves:
        pltpu.make_async_copy(middle, middle, out_sems.at[index]).wait()


TOKEN = jax.ShapeDtypeStruct((1,), jnp.int32)


def start(front, block_slots, rows_first, rows_second):
    row_blocks, col_blocks = front.shape[0], front.shape[3]
    count = NC * (NC + 1) // 2
    f32 = lambda *shape: jax.ShapeDtypeStruct(shape, jnp.float32)
    flags, token, panel, keep, send = pl.pallas_call(
        start_kernel,
        out_shape=(
            jax.ShapeDtypeStruct((row_blocks, 8), jnp.int32),
            TOKEN,
            f32(NC, row_blocks, BS, 1, BS),
            f32(count // 2, BS, 1, BS),
            f32(count // 2, BS, 1, BS),
        ),
        in_specs=[SMEM, SMEM, SMEM, HBM],
        out_specs=(SMEM, SMEM) + (HBM,) * 3,
        scratch_shapes=[
            pltpu.VMEM((row_blocks // 4, BS, 1, BS), jnp.float32),
            pltpu.VMEM((count, BS, 1, BS), jnp.float32),
            pltpu.VMEM((NC, row_blocks, BS, 1, BS), jnp.float32),
            pltpu.SemaphoreType.DMA((count + NC,)),
            pltpu.SemaphoreType.DMA((count + NC,)),
        ],
        compiler_params=pltpu.CompilerParams(vmem_limit_bytes=ALMOST_ALL),
        name="start",
    )(block_slots, rows_first, rows_second, front.reshape(row_blocks, BS, col_blocks, 1, BS))
    return flags, token, panel.reshape(NC, row_blocks, BS, BS), keep.reshape(-1, BS), send.reshape(-1, BS)


def lines_kernel(slots, after, wide_ref, one, two, token, zero, lines, sems, out_sems):
    own_row = lax.axis_index("row")
    owned = [slots[c] % 4 == own_row for c in range(NC)]
    targets = [(one if c < PB else two).at[c % PB] for c in range(NC)]
    for c in range(NC):
        @pl.when(owned[c])
        def _(c=c):
            pltpu.make_async_copy(wide_ref.at[slots[c] // 4], lines.at[c], sems.at[c]).start()
    zero[...] = jnp.zeros_like(zero)
    for c in range(NC):
        @pl.when(jnp.logical_not(owned[c]))
        def _(c=c):
            pltpu.make_async_copy(zero, targets[c], out_sems.at[c]).start()
    for c in range(NC):
        @pl.when(owned[c])
        def _(c=c):
            pltpu.make_async_copy(lines.at[c], lines.at[c], sems.at[c]).wait()
            pltpu.make_async_copy(lines.at[c], targets[c], out_sems.at[c]).start()
    token[0] = jnp.int32(0)
    for c in range(NC):
        pltpu.make_async_copy(zero, targets[c], out_sems.at[c]).wait()


def lines(front, block_slots, after):
    row_blocks, col_blocks = front.shape[0], front.shape[3]
    part = jax.ShapeDtypeStruct((PB, BS, col_blocks, BS), jnp.float32)
    return pl.pallas_call(
        lines_kernel,
        out_shape=(part, part, TOKEN),
        in_specs=[SMEM, SMEM, HBM],
        out_specs=(HBM, HBM, SMEM),
        scratch_shapes=[
            pltpu.VMEM((BS, col_blocks, BS), jnp.float32),
            pltpu.VMEM((NC, BS, col_blocks, BS), jnp.float32),
            pltpu.SemaphoreType.DMA((NC,)),
            pltpu.SemaphoreType.DMA((NC,)),
        ],
        name="lines",
    )(block_slots, after, local_blocks(front))


def add_kernel(after, a, b, c, d, first, second, token):
    first[...] = a[...] + b[...]
    second[...] = c[...] + d[...]

    @pl.when(pl.program_id(0) == 0)
    def _():
        token[0] = jnp.int32(0)


def add_pairs(a, b, c, d, after):
    block = pl.BlockSpec((1,) + a.shape[1:], lambda i: (i,) + (0,) * (a.ndim - 1))
    return pl.pallas_call(
        add_kernel,
        out_shape=(jax.ShapeDtypeStruct(a.shape, a.dtype),) * 2 + (TOKEN,),
        grid=(a.shape[0],),
        in_specs=[SMEM] + [block] * 4,
        out_specs=(block, block, SMEM),
        name="add_pairs",
    )(after, a, b, c, d)


def permute(value, flip):
    pairs = []
    for p in range(4):
        for q in range(8):
            to_p, to_q = flip(p, q)
            if 0 <= to_q < 8:
                pairs.append((p * 8 + q, to_p * 8 + to_q))
    return lax.ppermute(value, ("row", "col"), pairs)


def swap_core(value):
    return permute(value, lambda p, q: (p, q ^ 1))


def place(axis):
    return lax.axis_index("row") if axis == "row" else lax.axis_index("col") // 2


def spread_kernel(axis, count, *refs):
    total = refs[-1]
    outs = refs[count:-1]
    value = refs[0][...]
    for ref in refs[1:count]:
        value = value + ref[...]
    total[...] = value
    own = place(axis)
    for d in range(4):
        outs[d][...] = total[own ^ d]


def spread(axis, terms):
    rows = terms[0].shape[0] // 4
    shape = (4, rows, BS)
    return pl.pallas_call(
        functools.partial(spread_kernel, axis, len(terms)),
        out_shape=(jax.ShapeDtypeStruct((rows, BS), jnp.float32),) * 4,
        in_specs=[VMEM] * len(terms),
        out_specs=(VMEM,) * 4,
        scratch_shapes=[pltpu.VMEM(shape, jnp.float32)],
        name="spread",
    )(*[term.reshape(shape) for term in terms])


def collect_kernel(axis, own, one, two, three, out):
    at = place(axis)
    for d, source in enumerate((own, one, two, three)):
        out[at ^ d] = source[...]


def collect(axis, own, others):
    rows = own.shape[0]
    out = pl.pallas_call(
        functools.partial(collect_kernel, axis),
        out_shape=jax.ShapeDtypeStruct((4, rows, BS), jnp.float32),
        in_specs=[VMEM] * 4,
        out_specs=VMEM,
        name="collect",
    )(own, *others)
    return out.reshape(4 * rows, BS)


def join_kernel(own, other, first, second, token):
    core = lax.axis_index("col") % 2
    one = first.shape[0]
    half = own.shape[0]
    for which, low, high in ((0, own, other), (1, other, own)):
        @pl.when(core == which)
        def _(low=low, high=high):
            first[...] = low[:one]
            second[: half - one] = low[one:]
            second[half - one :] = high[...]
    token[0] = jnp.int32(0)


def join(own):
    other = swap_core(own)
    one = PB * (PB + 1) // 2
    count = NC * (NC + 1) // 2
    block = lambda n: jax.ShapeDtypeStruct((n, BS, BS), jnp.float32)
    return pl.pallas_call(
        join_kernel,
        out_shape=(block(one), block(count - one), TOKEN),
        in_specs=[VMEM] * 2,
        out_specs=(VMEM, VMEM, SMEM),
        name="join",
    )(own.reshape(-1, BS, BS), other.reshape(-1, BS, BS))


def across(axis, parts):
    if axis == "row":
        return [permute(parts[d - 1], lambda p, q, d=d: (p ^ d, q)) for d in range(1, 4)]
    return [permute(parts[d - 1], lambda p, q, d=d: (p, q ^ (2 * d))) for d in range(1, 4)]


def sum_square(keep, send):
    own, *parts = spread("row", [keep, swap_core(send)])
    own, *parts = spread("col", [own] + across("row", parts))
    got = across("col", parts)
    value = own + got[0] + got[1] + got[2]
    for axis in ("col", "row"):
        value = collect(axis, value, across(axis, [value] * 3))
    return join(value)


def piece_kernel(n, diag, *rest):
    lowers = rest[:n]
    inverses = rest[n : 2 * n]
    lower_out, inverse_out, token = rest[-3:]
    token[0] = jnp.int32(0)

    def row(i):
        return jnp.concatenate([lowers[j][(i - j) * BS : (i - j + 1) * BS, :] for j in range(n)], axis=1)

    column = []
    for i in range(n, PB):
        value = diag[lower_index(i, n)]
        if n:
            value = value - dot_nt(row(i), row(n))
        column.append(value)
    upper, inverse = factor_block(column[0])
    lower_out[0:BS, :] = upper.T
    if n + 1 < PB:
        lower_out[BS:, :] = dot_nt(jnp.concatenate(column[1:], axis=0), inverse)
    inverse_out[:, n * BS :] = inverse
    if n:
        before = jnp.concatenate(
            [
                jnp.concatenate([inverses[j][...], jnp.zeros((BS, (n - 1 - j) * BS), jnp.float32)], axis=1)
                if j + 1 < n
                else inverses[j][...]
                for j in range(n)
            ],
            axis=0,
        )
        inverse_out[:, : n * BS] = -dot_nn(inverse, dot_nn(row(n), before))


def piece(n, diag, lowers, inverses, after):
    return pl.pallas_call(
        functools.partial(piece_kernel, n),
        out_shape=(
            jax.ShapeDtypeStruct(((PB - n) * BS, BS), jnp.float32),
            jax.ShapeDtypeStruct((BS, (n + 1) * BS), jnp.float32),
            TOKEN,
        ),
        in_specs=[VMEM] * (1 + 2 * n) + [SMEM] * len(after),
        out_specs=(VMEM, VMEM, SMEM),
        compiler_params=pltpu.CompilerParams(vmem_limit_bytes=32 * 2**20),
        cost_estimate=pl.CostEstimate(flops=10**8, bytes_accessed=10**5, transcendentals=0),
        name="factor_piece",
    )(diag, *lowers, *inverses, *after)


def inverse_rows(inverses):
    rows = []
    for j in range(PB):
        if j + 1 < PB:
            rows.append(jnp.concatenate([inverses[j][...], jnp.zeros((BS, (PB - 1 - j) * BS), jnp.float32)], axis=1))
        else:
            rows.append(inverses[j][...])
    return jnp.concatenate(rows, axis=0)


def between_kernel(diag, *rest):
    inverses = rest[:PB]
    cross_out, rest_out = rest[-2:]
    inverse = inverse_rows(inverses)
    one = PB * (PB + 1) // 2
    left = [
        jnp.concatenate([diag[lower_index(i, j) - one] for j in range(PB)], axis=1) for i in range(PB, NC)
    ]
    cross = dot_nt(jnp.concatenate(left, axis=0), inverse)
    cross_out[...] = cross
    for i in range(PB):
        here = cross[i * BS : (i + 1) * BS, :]
        product = dot_nt(here, cross[: (i + 1) * BS, :])
        for j in range(i + 1):
            block = diag[lower_index(i + PB, j + PB) - one]
            rest_out[lower_index(i, j)] = block - product[:, j * BS : (j + 1) * BS]


def between(diag, inverses, after):
    return pl.pallas_call(
        between_kernel,
        out_shape=(
            jax.ShapeDtypeStruct((PB * BS, PB * BS), jnp.float32),
            jax.ShapeDtypeStruct((PB * (PB + 1) // 2, BS, BS), jnp.float32),
        ),
        in_specs=[VMEM] * (1 + PB) + [SMEM] * len(after),
        out_specs=(VMEM, VMEM),
        compiler_params=pltpu.CompilerParams(vmem_limit_bytes=32 * 2**20),
        cost_estimate=pl.CostEstimate(flops=10**8, bytes_accessed=10**5, transcendentals=0),
        name="between",
    )(diag, *inverses, *after)


def finish_kernel(*refs):
    first = inverse_rows(refs[:PB])
    second = inverse_rows(refs[PB : 2 * PB])
    cross = refs[2 * PB][...]
    lowers = refs[2 * PB + 1 : 4 * PB + 1]
    lower_out, high_out, low_out, turned_high, turned_low = refs[-5:]
    size = PB * BS
    turned_high[size:, :size] = jnp.zeros((size, size), jnp.bfloat16)
    turned_low[size:, :size] = jnp.zeros((size, size), jnp.bfloat16)
    lower_out[...] = jnp.zeros_like(lower_out)
    for j in range(PB):
        for half in range(2):
            rows = slice(half * size + j * BS, (half + 1) * size)
            lower_out[rows, j * BS : (j + 1) * BS] = lowers[half * PB + j][...]
    high_out[:size, size:] = jnp.zeros((size, size), jnp.bfloat16)
    low_out[:size, size:] = jnp.zeros((size, size), jnp.bfloat16)
    corner = -dot_nn(second, dot_nn(cross, first))
    for value, rows, cols in (
        (first, slice(0, size), slice(0, size)),
        (corner, slice(size, 2 * size), slice(0, size)),
        (second, slice(size, 2 * size), slice(size, 2 * size)),
    ):
        high, low = split(value)
        high_out[rows, cols] = high
        low_out[rows, cols] = low
        high, low = split(value.T)
        turned_high[cols, rows] = high
        turned_low[cols, rows] = low


def finish(first, second, cross, lowers):
    size = NC * BS
    return pl.pallas_call(
        finish_kernel,
        out_shape=(jax.ShapeDtypeStruct((size, size // 2), jnp.float32),)
        + (jax.ShapeDtypeStruct((size, size), jnp.bfloat16),) * 4,
        in_specs=[VMEM] * (4 * PB + 1),
        out_specs=(VMEM,) * 5,
        compiler_params=pltpu.CompilerParams(vmem_limit_bytes=32 * 2**20),
        cost_estimate=pl.CostEstimate(flops=10**8, bytes_accessed=10**5, transcendentals=0),
        name="finish",
    )(*first, *second, cross, *lowers)


def three(dot, a_high, a_low, b_high, b_low):
    kwargs = dict(preferred_element_type=jnp.float32)
    return dot(a_high, b_high, **kwargs) + (dot(a_high, b_low, **kwargs) + dot(a_low, b_high, **kwargs))


def nt(a, b, **kwargs):
    return lax.dot_general(a, b, (((1,), (1,)), ((), ())), **kwargs)


def nn(a, b, **kwargs):
    return lax.dot_general(a, b, (((1,), (0,)), ((), ())), **kwargs)


def masked(tiles, axis, first, second):
    low_part = jnp.concatenate(tiles[:PB], axis=axis)
    high_part = jnp.concatenate(tiles[PB:], axis=axis)
    zero = jnp.zeros_like(low_part)
    return jnp.concatenate([jnp.where(first, low_part, zero), jnp.where(second, high_part, zero)], axis=axis)


def columns_kernel(flags, one, one_more, two, two_more, high_ref, low_ref, col_high, col_low, total):
    size = NC * BS
    half = PB * BS
    width = 2 * BS
    step = pl.program_id(0)
    col_blocks = one.shape[2]
    first_half = step < PB // 2
    for chosen, part, more, column in (
        (first_half, one, one_more, 3),
        (jnp.logical_not(first_half), two, two_more, 4),
    ):
        @pl.when(chosen)
        def _(part=part, more=more, column=column):
            for b in range(col_blocks):
                at = slice(b * BS, (b + 1) * BS)
                raw = jnp.concatenate([part[c, :, b, :] + more[c, :, b, :] for c in range(2)], axis=0)
                high, low = split(jnp.where(flags[b, column] != 0, raw, jnp.zeros_like(raw)))
                col_high[:width, at] = high
                col_low[:width, at] = low

    high, low = col_high[:width, :], col_low[:width, :]
    for m in range(0, size, width):
        rows = slice(m, m + width)

        @pl.when(step == 0)
        def _(rows=rows):
            total[rows, :] = three(nn, high_ref[rows, :], low_ref[rows, :], high, low)

        if m > 0:
            @pl.when(jnp.logical_and(step > 0, step * width <= m))
            def _(rows=rows):
                total[rows, :] = total[rows, :] + three(nn, high_ref[rows, :], low_ref[rows, :], high, low)

    @pl.when(step == pl.num_programs(0) - 1)
    def _():
        for b in range(col_blocks):
            at = slice(b * BS, (b + 1) * BS)
            for rows, f in ((slice(0, half), 3), (slice(half, size), 4)):
                value = total[rows, at]
                high, low = split(jnp.where(flags[b, f] != 0, value, jnp.zeros_like(value)))
                col_high[rows, at] = high
                col_low[rows, at] = low


def solve_columns(flags, one, one_more, two, two_more, high, low):
    size = NC * BS
    width = 2 * BS
    shape = (size, one.shape[2] * BS)
    first = pl.BlockSpec((2,) + one.shape[1:], lambda i: (jnp.minimum(i, PB // 2 - 1), 0, 0, 0))
    second = pl.BlockSpec((2,) + one.shape[1:], lambda i: (jnp.maximum(i - PB // 2, 0), 0, 0, 0))
    strip = pl.BlockSpec((size, width), lambda i: (0, i))
    whole = pl.BlockSpec(shape, lambda i: (0, 0))
    return pl.pallas_call(
        columns_kernel,
        out_shape=(jax.ShapeDtypeStruct(shape, jnp.bfloat16),) * 2,
        grid=(NC // 2,),
        in_specs=[SMEM, first, first, second, second, strip, strip],
        out_specs=(whole, whole),
        scratch_shapes=[pltpu.VMEM(shape, jnp.float32)],
        compiler_params=pltpu.CompilerParams(vmem_limit_bytes=48 * 2**20),
        name="solve_columns",
    )(flags, one, one_more, two, two_more, high, low)


def update_kernel(flags, front_ref, rows_ref, lower_ref, high_ref, low_ref, col_high, col_low, out_ref,
                  solved, sol_high, sol_low):
    size = NC * BS
    half = PB * BS
    width = 2 * BS
    step = pl.program_id(0)
    col_blocks = front_ref.shape[1]
    tall = rows_ref.shape[1]
    for k in range(tall):
        a = step * tall + k
        raw = masked([rows_ref[c, k] for c in range(NC)], 1, flags[a, 0] != 0, flags[a, 1] != 0)
        high, low = split(raw)
        sol_high[k * BS : (k + 1) * BS, :] = high
        sol_low[k * BS : (k + 1) * BS, :] = low
    for m in range(0, size, width):
        deep = m + width
        value = three(nn, sol_high[:, :deep], sol_low[:, :deep], high_ref[:deep, m:deep], low_ref[:deep, m:deep])
        if m >= half:
            value = jnp.concatenate(
                [
                    jnp.where(flags[step * tall + k, 1] != 0, value[k * BS : (k + 1) * BS, :], 0.0)
                    for k in range(tall)
                ],
                axis=0,
            )
        solved[:, m:deep] = value
    high, low = split(solved[...])
    sol_high[...] = high
    sol_low[...] = low
    for b in range(0, col_blocks, 2):
        at = slice(b * BS, (b + 2) * BS)
        value = three(nn, sol_high[...], sol_low[...], col_high[:, at], col_low[:, at])
        for s in range(2):
            out_ref[:, b + s, :] = front_ref[:, b + s, :] - value[:, s * BS : (s + 1) * BS]
    for b in range(col_blocks):
        j = flags[b, 5]

        @pl.when(j >= 0)
        def _(b=b, j=j):
            at = pl.ds(pl.multiple_of(j * BS, BS), BS)
            for k in range(tall):
                a = step * tall + k
                rows = slice(k * BS, (k + 1) * BS)
                listed = jnp.where(j < PB, flags[a, 0], flags[a, 1])
                own = flags[a, 2]

                @pl.when(listed != 0)
                def _():
                    out_ref[rows, b, :] = solved[rows, at]

                @pl.when(jnp.logical_and(own >= 0, own // PB == j // PB))
                def _():
                    source = pl.ds(pl.multiple_of(own * BS, BS), BS)
                    inside = pl.ds(pl.multiple_of(j % PB * BS, BS), BS)
                    out_ref[rows, b, :] = lower_ref[source, inside]


def update_front(flags, front, rows, lower, high, low, col_high, col_low):
    row_blocks, _, col_blocks = front.shape[:3]
    size = NC * BS
    tall = 4
    block = pl.BlockSpec((tall * BS, col_blocks, BS), lambda i: (i, 0, 0))
    return pl.pallas_call(
        update_kernel,
        out_shape=jax.ShapeDtypeStruct((row_blocks * BS, col_blocks, BS), jnp.float32),
        grid=(row_blocks // tall,),
        in_specs=[SMEM, block, pl.BlockSpec((NC, tall, BS, BS), lambda i: (0, i, 0, 0))] + [VMEM] * 5,
        out_specs=block,
        scratch_shapes=[
            pltpu.VMEM((tall * BS, size), jnp.float32),
            pltpu.VMEM((tall * BS, size), jnp.bfloat16),
            pltpu.VMEM((tall * BS, size), jnp.bfloat16),
        ],
        compiler_params=pltpu.CompilerParams(vmem_limit_bytes=40 * 2**20),
        cost_estimate=pl.CostEstimate(flops=10**9, bytes_accessed=10**6, transcendentals=0),
        name="update_front",
    )(flags, front.reshape(row_blocks * BS, col_blocks, BS), rows, lower, high, low, col_high, col_low)


def block_flags(slots, listed_one, listed_two, diag_slots):
    one = jnp.any(slots[:, None] == listed_one[None, :], axis=1).astype(jnp.int32)
    two = jnp.any(slots[:, None] == listed_two[None, :], axis=1).astype(jnp.int32)
    order = jnp.arange(1, NC + 1, dtype=jnp.int32)
    where = jnp.sum(jnp.where(slots[:, None] == diag_slots[None, :], order[None, :], 0), axis=1) - 1
    return jnp.stack([one, two, where], axis=1)


def gather_summed(front, block_slots, rows_first, rows_second):
    grid_rows, grid_cols = lax.axis_size("row"), lax.axis_size("col")
    own_row, own_col = lax.axis_index("row"), lax.axis_index("col")
    row_blocks, col_blocks = front.shape[0], front.shape[3]
    diag_slots = block_slots[:NC]
    listed_one = block_slots[rows_first]
    listed_two = block_slots[rows_second]
    row_slots = jnp.arange(row_blocks, dtype=jnp.int32) * grid_rows + own_row
    col_slots = jnp.arange(row_blocks, dtype=jnp.int32) * grid_cols + own_col
    flags = jnp.concatenate(
        [block_flags(slots, listed_one, listed_two, diag_slots) for slots in (row_slots, col_slots)], axis=1
    )
    flags = jnp.pad(flags, ((0, 0), (0, 2)))
    local = front.reshape(row_blocks, BS, col_blocks, BS)
    pieces = []
    rows = []
    for c in range(NC):
        piece = lax.dynamic_index_in_dim(local, diag_slots[c] // grid_cols, 2, keepdims=False)
        pieces.append(jnp.where(diag_slots[c] % grid_cols == own_col, piece, jnp.zeros_like(piece)))
        piece = lax.dynamic_index_in_dim(local, diag_slots[c] // grid_rows, 0, keepdims=False)
        rows.append(jnp.where(diag_slots[c] % grid_rows == own_row, piece, jnp.zeros_like(piece)))
    pieces = jnp.stack(pieces, axis=0)
    blocks = []
    for i in range(NC):
        part = lax.dynamic_index_in_dim(pieces, diag_slots[i] // grid_rows, 1, keepdims=False)[: i + 1]
        blocks.append(jnp.where(diag_slots[i] % grid_rows == own_row, part, jnp.zeros_like(part)))
    diag = lax.psum(jnp.concatenate(blocks, axis=0), ("row", "col"))
    return flags, lax.psum(jnp.stack(rows, axis=0), "row"), diag, lax.psum(pieces, "col")


def factor_panel(diag, after, hooks):
    lowers, inverses = [], []
    for n in range(PB):
        lower, inverse, token = piece(n, diag, lowers, inverses, hooks(n, after))
        lowers.append(lower)
        inverses.append(inverse)
        after = [token]
    return lowers, inverses, after


def factor(front, flags, block_slots, keep, send):
    diag, second, token = sum_square(keep, send)
    lines_one, lines_two, token = lines(front, block_slots, token)
    got_one = permute(lines_one, lambda p, q: (p ^ 1, q))
    got_two = permute(lines_two, lambda p, q: (p ^ 2, q))
    sums = []

    def half_way(n, after):
        if n != 1:
            return after
        *total, token = add_pairs(lines_one, got_one, lines_two, got_two, after[0])
        sums.extend(total)
        return [token]

    factors = factor_both(diag, second, [token], half_way)
    return factors, sums


def factor_both(diag, second, after, half_way):
    lowers, inverses, after = factor_panel(diag, after, lambda n, after: after)
    cross, corner = between(second, inverses, after)
    more_lowers, more_inverses, _ = factor_panel(corner, [], half_way)
    return finish(inverses, more_inverses, cross, lowers + more_lowers)


def on_device(front, block_slots, rows_first, rows_second):
    if (lax.axis_size("row"), lax.axis_size("col")) != (4, 8):
        flags, cols, diag, panel = gather_summed(front, block_slots, rows_first, rows_second)
        one = PB * (PB + 1) // 2
        lower, high, low, *turned = factor_both(
            diag[:one], diag[one:], [jnp.zeros((1,), jnp.int32)], lambda n, after: after
        )
        none = jnp.zeros_like(cols[:PB])
        columns = solve_columns(flags, cols[:PB], none, cols[PB:], none, high, low)
    else:
        flags, token, panel, keep, send = start(front, block_slots, rows_first, rows_second)
        panel = lax.psum(panel, "col")

        def work():
            (lower, high, low, *turned), (one, two) = factor(front, flags, block_slots, keep, send)
            more_one = permute(one, lambda p, q: (p ^ 2, q))
            more_two = permute(two, lambda p, q: (p ^ 1, q))
            columns = solve_columns(flags, one, more_one, two, more_two, high, low)
            return lower, *turned, *columns

        shapes = jax.eval_shape(work)
        lower, *turned, col_high, col_low = lax.cond(
            token[0] == 0, work, lambda: tuple(jnp.zeros(x.shape, x.dtype) for x in shapes)
        )
        columns = col_high, col_low
    out = update_front(flags, local_blocks(front), panel, lower, *turned, *columns)
    return out.reshape(front.shape)


def local_blocks(front):
    return front.reshape(front.shape[0], BS, front.shape[3], BS)


def solution(mesh):
    placed = (P(None, "row", None, None, "col", None), P(), P(), P())
    return jax.shard_map(
        on_device,
        mesh=mesh,
        in_specs=placed,
        out_specs=P(None, "row", None, None, "col", None),
        check_vma=False,
    )
```

```python
import functools

import jax
import jax.numpy as jnp
from jax import lax
from jax.experimental import pallas as pl
from jax.experimental.pallas import tpu as pltpu
from jax.sharding import PartitionSpec as P

BS = 128
PB = 4
NC = 2 * PB
STEP = 8
ALMOST_ALL = 63 * 2**20
HIGHEST = lax.Precision.HIGHEST
HBM = pl.BlockSpec(memory_space=pltpu.HBM)
VMEM = pl.BlockSpec(memory_space=pltpu.VMEM)
SMEM = pl.BlockSpec(memory_space=pltpu.SMEM)


def lane_copy(tile, lane):
    return jnp.broadcast_to(tile[:, lane : lane + 1], tile.shape)


def row_copy(tile, row):
    return jnp.broadcast_to(tile[row : row + 1, :], tile.shape)


def reciprocal(value):
    guess = pl.reciprocal(value, approx=True)
    guess = guess * (2.0 - value * guess)
    return guess * (2.0 - value * guess)


def factor_block(block):
    tiles = BS // 8
    sub = lax.broadcasted_iota(jnp.int32, (8, BS), 0)
    lanes = lax.broadcasted_iota(jnp.int32, (8, BS), 1)
    left = [block[8 * i : 8 * i + 8, :] for i in range(tiles)]
    right = [jnp.where(lanes == sub + 8 * i, 1.0, 0.0).astype(jnp.float32) for i in range(tiles)]
    upper = []
    inverse = []
    for j in range(0, BS, STEP):
        g, o = divmod(j, 8)
        if o == 0:
            upper_tile = jnp.zeros((8, BS), jnp.float32)
            inverse_tile = jnp.zeros((8, BS), jnp.float32)
        rows = [row_copy(left[g], o + s) for s in range(STEP)]
        extra = [row_copy(right[g], o + s) for s in range(STEP)]
        first = g if o + STEP < 8 else g + 1
        cols = {i: [lane_copy(left[i], j + s) for s in range(STEP)] for i in range(first, tiles)}
        pivot = [[lane_copy(rows[s], j + t) if t >= s else None for t in range(STEP)] for s in range(STEP)]
        ratio = [[None] * STEP for _ in range(STEP)]
        recip = []
        for s in range(STEP):
            inv = reciprocal(pivot[s][s])
            recip.append(inv)
            for t in range(s + 1, STEP):
                ratio[s][t] = pivot[s][t] * inv
            for t in range(s + 1, STEP):
                for u in range(t, STEP):
                    pivot[t][u] = pivot[t][u] - ratio[s][t] * pivot[s][u]
                rows[t] = rows[t] - ratio[s][t] * rows[s]
                extra[t] = extra[t] - ratio[s][t] * extra[s]
        for s in range(STEP):
            scale = lax.rsqrt(pivot[s][s])
            scale = scale * (1.5 - 0.5 * pivot[s][s] * scale * scale)
            here = sub == o + s
            upper_tile = jnp.where(here, rows[s] * scale, upper_tile)
            inverse_tile = jnp.where(here, extra[s] * scale, inverse_tile)
        if o + STEP == 8:
            upper.append(jnp.where(lanes >= sub + 8 * g, upper_tile, 0.0))
            inverse.append(jnp.where(lanes <= sub + 8 * g, inverse_tile, 0.0))
        for s in reversed(range(STEP)):
            rows[s] = rows[s] * recip[s]
            extra[s] = extra[s] * recip[s]
            for t in range(s + 1, STEP):
                rows[s] = rows[s] - ratio[s][t] * rows[t]
                extra[s] = extra[s] - ratio[s][t] * extra[t]
        for i in range(first, tiles):
            less = cols[i][0] * rows[0]
            less_extra = cols[i][0] * extra[0]
            for s in range(1, STEP):
                less = less + cols[i][s] * rows[s]
                less_extra = less_extra + cols[i][s] * extra[s]
            if i == g:
                below = sub >= o + STEP
                left[i] = jnp.where(below, left[i] - less, left[i])
                right[i] = jnp.where(below, right[i] - less_extra, right[i])
            else:
                left[i] = left[i] - less
                right[i] = right[i] - less_extra
    return jnp.concatenate(upper, axis=0), jnp.concatenate(inverse, axis=0)


def lower_index(i, j):
    return i * (i + 1) // 2 + j


def dot_nt(a, b):
    return lax.dot_general(a, b, (((1,), (1,)), ((), ())), precision=HIGHEST, preferred_element_type=jnp.float32)


def dot_nn(a, b):
    return lax.dot_general(a, b, (((1,), (0,)), ((), ())), precision=HIGHEST, preferred_element_type=jnp.float32)


def split(x):
    high = x.astype(jnp.bfloat16)
    return high, (x - high.astype(jnp.float32)).astype(jnp.bfloat16)


def place(count, core, block):
    half = count // 2
    return (block // half) == core, block % half


def start_kernel(slots, first, second, front_ref, flags, sides, mine, theirs, keep_one, send_one, keep_two, send_two,
                 zero, blocks, columns, sems, out_sems):
    halves, _, _, col_blocks = front_ref.shape[:4]
    row_blocks = 2 * halves
    grid_rows, grid_cols = 4, 8
    own_row = lax.axis_index("row")
    own_col = lax.axis_index("col")
    core = own_col % 2
    slot = [slots[i] for i in range(NC)]
    one = PB * (PB + 1) // 2
    moves = []
    fills = []

    def move(condition, source, middle, targets):
        index = len(moves)

        @pl.when(condition)
        def _():
            pltpu.make_async_copy(source, middle, sems.at[index]).start()

        moves.append((condition, middle, targets, index))

    always = core >= 0
    group = zero.shape[0]
    for target, parity in ((theirs, 1 - core), (mine, core)):
        for c in range(NC):
            owned = slot[c] % grid_cols == own_col
            for a in range(0, halves, group):
                fills.append((jnp.logical_not(owned), zero, target.at[c, a : a + group], len(moves)))
            middle = columns.at[c, parity]
            move(owned, front_ref.at[:, parity, :, slot[c] // grid_cols], middle, ((target.at[c], always),))
    for i in range(NC):
        for j in range(i + 1):
            block = lower_index(i, j)
            if i < PB:
                half, at, keep, send = one // 2, block, keep_one, send_one
            else:
                half, at, keep, send = keep_two.shape[0], block - one, keep_two, send_two
            a = slot[i] // grid_rows
            b = slot[j] // grid_cols
            owned = jnp.logical_and(slot[i] % grid_rows == own_row, slot[j] % grid_cols == own_col)
            stay = core == at // half
            targets = ((keep.at[at % half], stay), (send.at[at % half], jnp.logical_not(stay)))
            for target, chosen in targets:
                fills.append((jnp.logical_and(chosen, jnp.logical_not(owned)), zero.at[0], target, len(moves)))
            move(owned, front_ref.at[a // 2, a % 2, :, b], blocks.at[block], targets)

    zero[...] = jnp.zeros_like(zero)
    for condition, source, target, index in fills:
        @pl.when(condition)
        def _(source=source, target=target, index=index):
            pltpu.make_async_copy(source, target, out_sems.at[index]).start()

    for a in range(row_blocks):
        for f in range(8):
            flags[a, f] = jnp.int32(-1 if f in (2, 5) else 0)
    for c in range(NC):
        @pl.when(slot[c] % grid_rows == own_row)
        def _(c=c):
            flags[slot[c] // grid_rows, 2] = jnp.int32(c)

        @pl.when(slot[c] % grid_cols == own_col)
        def _(c=c):
            flags[slot[c] // grid_cols, 5] = jnp.int32(c)

    for listed, f in ((first, 0), (second, 1)):
        @pl.loop(0, listed.shape[0])
        def _(i, listed=listed, f=f):
            s = slots[listed[i]]

            @pl.when(s % grid_rows == own_row)
            def _():
                flags[s // grid_rows, f] = jnp.int32(1)

            @pl.when(s % grid_cols == own_col)
            def _():
                flags[s // grid_cols, 3 + f] = jnp.int32(1)

    sides[0] = core
    sides[1] = 1 - core
    for condition, middle, targets, index in moves:
        @pl.when(condition)
        def _(middle=middle, targets=targets, index=index):
            pltpu.make_async_copy(middle, middle, sems.at[index]).wait()
            for target, chosen in targets:
                @pl.when(chosen)
                def _(target=target):
                    pltpu.make_async_copy(middle, target, out_sems.at[index]).start()
    for condition, middle, targets, index in moves:
        pltpu.make_async_copy(middle, middle, out_sems.at[index]).wait()


TOKEN = jax.ShapeDtypeStruct((1,), jnp.int32)


def start(front, block_slots, rows_first, rows_second):
    row_blocks, col_blocks = front.shape[0], front.shape[3]
    half = row_blocks // 2
    one = PB * (PB + 1) // 2
    count = NC * (NC + 1) // 2
    two = count - one
    f32 = lambda *shape: jax.ShapeDtypeStruct(shape, jnp.float32)
    flags, sides, mine, theirs, *parts = pl.pallas_call(
        start_kernel,
        out_shape=(
            jax.ShapeDtypeStruct((row_blocks, 8), jnp.int32),
            jax.ShapeDtypeStruct((2,), jnp.int32),
            f32(NC, half, BS, 1, BS),
            f32(NC, half, BS, 1, BS),
            f32(one // 2, BS, 1, BS),
            f32(one // 2, BS, 1, BS),
            f32(two // 2, BS, 1, BS),
            f32(two // 2, BS, 1, BS),
        ),
        in_specs=[SMEM, SMEM, SMEM, HBM],
        out_specs=(SMEM, SMEM) + (HBM,) * 6,
        scratch_shapes=[
            pltpu.VMEM((half // 2, BS, 1, BS), jnp.float32),
            pltpu.VMEM((count, BS, 1, BS), jnp.float32),
            pltpu.VMEM((NC, 2, half, BS, 1, BS), jnp.float32),
            pltpu.SemaphoreType.DMA((count + 2 * NC,)),
            pltpu.SemaphoreType.DMA((count + 2 * NC,)),
        ],
        compiler_params=pltpu.CompilerParams(vmem_limit_bytes=ALMOST_ALL),
        name="start",
    )(block_slots, rows_first, rows_second, front.reshape(half, 2, BS, col_blocks, 1, BS))
    shape = (NC, half, BS, BS)
    return flags, sides, mine.reshape(shape), theirs.reshape(shape), [x.reshape(-1, BS) for x in parts]


def lines_kernel(slots, after, wide_ref, one, two, token, zero, lines, sems, out_sems):
    own_row = lax.axis_index("row")
    owned = [slots[c] % 4 == own_row for c in range(NC)]
    targets = [(one if c < PB else two).at[c % PB] for c in range(NC)]
    for c in range(NC):
        @pl.when(owned[c])
        def _(c=c):
            pltpu.make_async_copy(wide_ref.at[slots[c] // 4], lines.at[c], sems.at[c]).start()
    zero[...] = jnp.zeros_like(zero)
    for c in range(NC):
        @pl.when(jnp.logical_not(owned[c]))
        def _(c=c):
            pltpu.make_async_copy(zero, targets[c], out_sems.at[c]).start()
    for c in range(NC):
        @pl.when(owned[c])
        def _(c=c):
            pltpu.make_async_copy(lines.at[c], lines.at[c], sems.at[c]).wait()
            pltpu.make_async_copy(lines.at[c], targets[c], out_sems.at[c]).start()
    token[0] = jnp.int32(0)
    for c in range(NC):
        pltpu.make_async_copy(zero, targets[c], out_sems.at[c]).wait()


def lines(front, block_slots, after):
    row_blocks, col_blocks = front.shape[0], front.shape[3]
    part = jax.ShapeDtypeStruct((PB, BS, col_blocks, BS), jnp.float32)
    return pl.pallas_call(
        lines_kernel,
        out_shape=(part, part, TOKEN),
        in_specs=[SMEM, SMEM, HBM],
        out_specs=(HBM, HBM, SMEM),
        scratch_shapes=[
            pltpu.VMEM((BS, col_blocks, BS), jnp.float32),
            pltpu.VMEM((NC, BS, col_blocks, BS), jnp.float32),
            pltpu.SemaphoreType.DMA((NC,)),
            pltpu.SemaphoreType.DMA((NC,)),
        ],
        name="lines",
    )(block_slots, after, local_blocks(front))


def merge_kernel(after, a, b, out):
    out[...] = a[...] + b[...]


def merge(a, b, after):
    block = pl.BlockSpec((1,) + a.shape[1:], lambda i: (i,) + (0,) * (a.ndim - 1))
    return pl.pallas_call(
        merge_kernel,
        out_shape=jax.ShapeDtypeStruct(a.shape, a.dtype),
        grid=(a.shape[0],),
        in_specs=[SMEM, block, block],
        out_specs=block,
        name="merge",
    )(after, a, b)


def add_kernel(after, a, b, c, d, first, second, token):
    first[...] = a[...] + b[...]
    second[...] = c[...] + d[...]

    @pl.when(pl.program_id(0) == 0)
    def _():
        token[0] = jnp.int32(0)


def add_pairs(a, b, c, d, after):
    block = pl.BlockSpec((1,) + a.shape[1:], lambda i: (i,) + (0,) * (a.ndim - 1))
    return pl.pallas_call(
        add_kernel,
        out_shape=(jax.ShapeDtypeStruct(a.shape, a.dtype),) * 2 + (TOKEN,),
        grid=(a.shape[0],),
        in_specs=[SMEM] + [block] * 4,
        out_specs=(block, block, SMEM),
        name="add_pairs",
    )(after, a, b, c, d)


def permute(value, flip):
    pairs = []
    for p in range(4):
        for q in range(8):
            to_p, to_q = flip(p, q)
            if 0 <= to_q < 8:
                pairs.append((p * 8 + q, to_p * 8 + to_q))
    return lax.ppermute(value, ("row", "col"), pairs)


def swap_core(value):
    return permute(value, lambda p, q: (p, q ^ 1))


def place(axis):
    return lax.axis_index("row") if axis == "row" else lax.axis_index("col") // 2


def spread_kernel(axis, count, *refs):
    token, total = refs[-2:]
    outs = refs[-6:-2]
    value = refs[0][...]
    for ref in refs[1:count]:
        value = value + ref[...]
    total[...] = value
    own = place(axis)
    for d in range(4):
        outs[d][...] = total[own ^ d]
    token[0] = jnp.int32(0)


def spread(axis, terms, after):
    rows = terms[0].shape[0] // 4
    shape = (4, rows, BS)
    *parts, token = pl.pallas_call(
        functools.partial(spread_kernel, axis, len(terms)),
        out_shape=(jax.ShapeDtypeStruct((rows, BS), jnp.float32),) * 4 + (TOKEN,),
        in_specs=[VMEM] * len(terms) + [SMEM] * len(after),
        out_specs=(VMEM,) * 4 + (SMEM,),
        scratch_shapes=[pltpu.VMEM(shape, jnp.float32)],
        name="spread",
    )(*[term.reshape(shape) for term in terms], *after)
    return parts, token


def total_kernel(*refs):
    out, token = refs[-2:]
    out[...] = refs[0][...] + refs[1][...] + refs[2][...] + refs[3][...]
    token[0] = jnp.int32(0)


def total(terms, after):
    return pl.pallas_call(
        total_kernel,
        out_shape=(jax.ShapeDtypeStruct(terms[0].shape, jnp.float32), TOKEN),
        in_specs=[VMEM] * 4 + [SMEM] * len(after),
        out_specs=(VMEM, SMEM),
        name="total",
    )(*terms, *after)


def collect_kernel(axis, own, one, two, three, *rest):
    out, token = rest[-2:]
    at = place(axis)
    for d, source in enumerate((own, one, two, three)):
        out[at ^ d] = source[...]
    token[0] = jnp.int32(0)


def collect(axis, own, others, after):
    rows = own.shape[0]
    out, token = pl.pallas_call(
        functools.partial(collect_kernel, axis),
        out_shape=(jax.ShapeDtypeStruct((4, rows, BS), jnp.float32), TOKEN),
        in_specs=[VMEM] * 4 + [SMEM] * len(after),
        out_specs=(VMEM, SMEM),
        name="collect",
    )(own, *others, *after)
    return out.reshape(4 * rows, BS), token


def join_kernel(own, other, out, token):
    core = lax.axis_index("col") % 2
    out[core] = own[...]
    out[1 - core] = other[...]
    token[0] = jnp.int32(0)


def join(own, other):
    out, token = pl.pallas_call(
        join_kernel,
        out_shape=(jax.ShapeDtypeStruct((2,) + own.shape, jnp.float32), TOKEN),
        in_specs=[VMEM] * 2,
        out_specs=(VMEM, SMEM),
        name="join",
    )(own, other)
    return out.reshape(-1, BS, BS), token


def across(axis, parts):
    if axis == "row":
        return [permute(parts[d - 1], lambda p, q, d=d: (p ^ d, q)) for d in range(1, 4)]
    return [permute(parts[d - 1], lambda p, q, d=d: (p, q ^ (2 * d))) for d in range(1, 4)]


def piece_kernel(n, diag, *rest):
    lowers = rest[:n]
    inverses = rest[n : 2 * n]
    lower_out, inverse_out, token = rest[-3:]
    token[0] = jnp.int32(0)

    def row(i):
        return jnp.concatenate([lowers[j][(i - j) * BS : (i - j + 1) * BS, :] for j in range(n)], axis=1)

    column = []
    for i in range(n, PB):
        value = diag[lower_index(i, n)]
        if n:
            value = value - dot_nt(row(i), row(n))
        column.append(value)
    upper, inverse = factor_block(column[0])
    lower_out[0:BS, :] = upper.T
    if n + 1 < PB:
        lower_out[BS:, :] = dot_nt(jnp.concatenate(column[1:], axis=0), inverse)
    inverse_out[:, n * BS :] = inverse
    if n:
        before = jnp.concatenate(
            [
                jnp.concatenate([inverses[j][...], jnp.zeros((BS, (n - 1 - j) * BS), jnp.float32)], axis=1)
                if j + 1 < n
                else inverses[j][...]
                for j in range(n)
            ],
            axis=0,
        )
        inverse_out[:, : n * BS] = -dot_nn(inverse, dot_nn(row(n), before))


def piece(n, diag, lowers, inverses, after):
    return pl.pallas_call(
        functools.partial(piece_kernel, n),
        out_shape=(
            jax.ShapeDtypeStruct(((PB - n) * BS, BS), jnp.float32),
            jax.ShapeDtypeStruct((BS, (n + 1) * BS), jnp.float32),
            TOKEN,
        ),
        in_specs=[VMEM] * (1 + 2 * n) + [SMEM] * len(after),
        out_specs=(VMEM, VMEM, SMEM),
        compiler_params=pltpu.CompilerParams(vmem_limit_bytes=32 * 2**20),
        cost_estimate=pl.CostEstimate(flops=10**8, bytes_accessed=10**5, transcendentals=0),
        name="factor_piece",
    )(diag, *lowers, *inverses, *after)


def inverse_rows(inverses):
    rows = []
    for j in range(PB):
        if j + 1 < PB:
            rows.append(jnp.concatenate([inverses[j][...], jnp.zeros((BS, (PB - 1 - j) * BS), jnp.float32)], axis=1))
        else:
            rows.append(inverses[j][...])
    return jnp.concatenate(rows, axis=0)


def between_kernel(diag, *rest):
    inverses = rest[:PB]
    cross_out, rest_out = rest[-2:]
    inverse = inverse_rows(inverses)
    one = PB * (PB + 1) // 2
    left = [
        jnp.concatenate([diag[lower_index(i, j) - one] for j in range(PB)], axis=1) for i in range(PB, NC)
    ]
    cross = dot_nt(jnp.concatenate(left, axis=0), inverse)
    cross_out[...] = cross
    for i in range(PB):
        here = cross[i * BS : (i + 1) * BS, :]
        product = dot_nt(here, cross[: (i + 1) * BS, :])
        for j in range(i + 1):
            block = diag[lower_index(i + PB, j + PB) - one]
            rest_out[lower_index(i, j)] = block - product[:, j * BS : (j + 1) * BS]


def between(diag, inverses, after):
    return pl.pallas_call(
        between_kernel,
        out_shape=(
            jax.ShapeDtypeStruct((PB * BS, PB * BS), jnp.float32),
            jax.ShapeDtypeStruct((PB * (PB + 1) // 2, BS, BS), jnp.float32),
        ),
        in_specs=[VMEM] * (1 + PB) + [SMEM] * len(after),
        out_specs=(VMEM, VMEM),
        compiler_params=pltpu.CompilerParams(vmem_limit_bytes=32 * 2**20),
        cost_estimate=pl.CostEstimate(flops=10**8, bytes_accessed=10**5, transcendentals=0),
        name="between",
    )(diag, *inverses, *after)


def finish_kernel(*refs):
    first = inverse_rows(refs[:PB])
    second = inverse_rows(refs[PB : 2 * PB])
    cross = refs[2 * PB][...]
    lowers = refs[2 * PB + 1 : 4 * PB + 1]
    lower_out, high_out, low_out = refs[-3:]
    size = PB * BS
    lower_out[...] = jnp.zeros_like(lower_out)
    for j in range(PB):
        for half in range(2):
            rows = slice(half * size + j * BS, (half + 1) * size)
            lower_out[rows, j * BS : (j + 1) * BS] = lowers[half * PB + j][...]
    high_out[:size, size:] = jnp.zeros((size, size), jnp.bfloat16)
    low_out[:size, size:] = jnp.zeros((size, size), jnp.bfloat16)
    corner = -dot_nn(second, dot_nn(cross, first))
    for value, rows, cols in (
        (first, slice(0, size), slice(0, size)),
        (corner, slice(size, 2 * size), slice(0, size)),
        (second, slice(size, 2 * size), slice(size, 2 * size)),
    ):
        high, low = split(value)
        high_out[rows, cols] = high
        low_out[rows, cols] = low


def finish(first, second, cross, lowers):
    size = NC * BS
    return pl.pallas_call(
        finish_kernel,
        out_shape=(jax.ShapeDtypeStruct((size, size // 2), jnp.float32),)
        + (jax.ShapeDtypeStruct((size, size), jnp.bfloat16),) * 2,
        in_specs=[VMEM] * (4 * PB + 1),
        out_specs=(VMEM,) * 3,
        compiler_params=pltpu.CompilerParams(vmem_limit_bytes=32 * 2**20),
        cost_estimate=pl.CostEstimate(flops=10**8, bytes_accessed=10**5, transcendentals=0),
        name="finish",
    )(*first, *second, cross, *lowers)


def three(dot, a_high, a_low, b_high, b_low):
    kwargs = dict(preferred_element_type=jnp.float32)
    return dot(a_high, b_high, **kwargs) + (dot(a_high, b_low, **kwargs) + dot(a_low, b_high, **kwargs))


def nt(a, b, **kwargs):
    return lax.dot_general(a, b, (((1,), (1,)), ((), ())), **kwargs)


def nn(a, b, **kwargs):
    return lax.dot_general(a, b, (((1,), (0,)), ((), ())), **kwargs)


def masked(tiles, axis, first, second):
    low_part = jnp.concatenate(tiles[:PB], axis=axis)
    high_part = jnp.concatenate(tiles[PB:], axis=axis)
    zero = jnp.zeros_like(low_part)
    return jnp.concatenate([jnp.where(first, low_part, zero), jnp.where(second, high_part, zero)], axis=axis)


def columns_kernel(flags, one, one_more, two, two_more, high_ref, low_ref, col_high, col_low, total):
    size = NC * BS
    half = PB * BS
    width = 2 * BS
    step = pl.program_id(0)
    col_blocks = one.shape[2]
    first_half = step < PB // 2
    for chosen, part, more, column in (
        (first_half, one, one_more, 3),
        (jnp.logical_not(first_half), two, two_more, 4),
    ):
        @pl.when(chosen)
        def _(part=part, more=more, column=column):
            for b in range(col_blocks):
                at = slice(b * BS, (b + 1) * BS)
                raw = jnp.concatenate([part[c, :, b, :] + more[c, :, b, :] for c in range(2)], axis=0)
                high, low = split(jnp.where(flags[b, column] != 0, raw, jnp.zeros_like(raw)))
                col_high[:width, at] = high
                col_low[:width, at] = low

    high, low = col_high[:width, :], col_low[:width, :]
    for m in range(0, size, width):
        rows = slice(m, m + width)

        @pl.when(step == 0)
        def _(rows=rows):
            total[rows, :] = three(nn, high_ref[rows, :], low_ref[rows, :], high, low)

        if m > 0:
            @pl.when(jnp.logical_and(step > 0, step * width <= m))
            def _(rows=rows):
                total[rows, :] = total[rows, :] + three(nn, high_ref[rows, :], low_ref[rows, :], high, low)

    @pl.when(step == pl.num_programs(0) - 1)
    def _():
        for b in range(col_blocks):
            at = slice(b * BS, (b + 1) * BS)
            for rows, f in ((slice(0, half), 3), (slice(half, size), 4)):
                value = total[rows, at]
                high, low = split(jnp.where(flags[b, f] != 0, value, jnp.zeros_like(value)))
                col_high[rows, at] = high
                col_low[rows, at] = low


def solve_columns(flags, one, one_more, two, two_more, high, low):
    size = NC * BS
    width = 2 * BS
    shape = (size, one.shape[2] * BS)
    first = pl.BlockSpec((2,) + one.shape[1:], lambda i: (jnp.minimum(i, PB // 2 - 1), 0, 0, 0))
    second = pl.BlockSpec((2,) + one.shape[1:], lambda i: (jnp.maximum(i - PB // 2, 0), 0, 0, 0))
    strip = pl.BlockSpec((size, width), lambda i: (0, i))
    whole = pl.BlockSpec(shape, lambda i: (0, 0))
    return pl.pallas_call(
        columns_kernel,
        out_shape=(jax.ShapeDtypeStruct(shape, jnp.bfloat16),) * 2,
        grid=(NC // 2,),
        in_specs=[SMEM, first, first, second, second, strip, strip],
        out_specs=(whole, whole),
        scratch_shapes=[pltpu.VMEM(shape, jnp.float32)],
        compiler_params=pltpu.CompilerParams(vmem_limit_bytes=48 * 2**20),
        name="solve_columns",
    )(flags, one, one_more, two, two_more, high, low)


def update_kernel(side, flags, front_ref, rows_ref, lower_ref, high_ref, low_ref, col_high, col_low, *rest):
    out_ref, solved, sol_high, sol_low = rest[-4:]
    size = NC * BS
    half = PB * BS
    width = 2 * BS
    parity = side[0]
    step = pl.program_id(0)
    col_blocks = front_ref.shape[3]
    tall = rows_ref.shape[1]
    index = [(step * tall + k) * 2 + parity for k in range(tall)]
    for k, a in enumerate(index):
        raw = masked([rows_ref[c, k] for c in range(NC)], 1, flags[a, 0] != 0, flags[a, 1] != 0)
        high, low = split(raw)
        sol_high[k * BS : (k + 1) * BS, :] = high
        sol_low[k * BS : (k + 1) * BS, :] = low
    for m in range(0, size, width):
        deep = m + width
        value = three(nt, sol_high[:, :deep], sol_low[:, :deep], high_ref[m:deep, :deep], low_ref[m:deep, :deep])
        if m >= half:
            value = jnp.concatenate(
                [jnp.where(flags[a, 1] != 0, value[k * BS : (k + 1) * BS, :], 0.0) for k, a in enumerate(index)],
                axis=0,
            )
        solved[:, m:deep] = value
    high, low = split(solved[...])
    sol_high[...] = high
    sol_low[...] = low
    for b in range(0, col_blocks, 2):
        at = slice(b * BS, (b + 2) * BS)
        value = three(nn, sol_high[...], sol_low[...], col_high[:, at], col_low[:, at])
        for s in range(2):
            for k in range(tall):
                less = value[k * BS : (k + 1) * BS, s * BS : (s + 1) * BS]
                out_ref[k, 0, :, b + s, :] = front_ref[k, 0, :, b + s, :] - less
    for b in range(col_blocks):
        j = flags[b, 5]

        @pl.when(j >= 0)
        def _(b=b, j=j):
            at = pl.ds(pl.multiple_of(j * BS, BS), BS)
            for k, a in enumerate(index):
                rows = slice(k * BS, (k + 1) * BS)
                listed = jnp.where(j < PB, flags[a, 0], flags[a, 1])
                own = flags[a, 2]

                @pl.when(listed != 0)
                def _(k=k, rows=rows):
                    out_ref[k, 0, :, b, :] = solved[rows, at]

                @pl.when(jnp.logical_and(own >= 0, own // PB == j // PB))
                def _(k=k, own=own):
                    source = pl.ds(pl.multiple_of(own * BS, BS), BS)
                    inside = pl.ds(pl.multiple_of(j % PB * BS, BS), BS)
                    out_ref[k, 0, :, b, :] = lower_ref[source, inside]


def update_front(side, flags, front, rows, lower, high, low, col_high, col_low, before):
    halves, _, _, col_blocks, _ = front.shape
    size = NC * BS
    tall = 2
    block = pl.BlockSpec((tall, 1, BS, col_blocks, BS), lambda i, side: (i, side[0], 0, 0, 0))
    return pl.pallas_call(
        update_kernel,
        out_shape=jax.ShapeDtypeStruct(front.shape, jnp.float32),
        grid_spec=pltpu.PrefetchScalarGridSpec(
            num_scalar_prefetch=1,
            grid=(halves // tall,),
            in_specs=[SMEM, block, pl.BlockSpec((NC, tall, BS, BS), lambda i, side: (0, i, 0, 0))]
            + [VMEM] * 5
            + [HBM] * len(before),
            out_specs=block,
            scratch_shapes=[
                pltpu.VMEM((tall * BS, size), jnp.float32),
                pltpu.VMEM((tall * BS, size), jnp.bfloat16),
                pltpu.VMEM((tall * BS, size), jnp.bfloat16),
            ],
        ),
        input_output_aliases={9: 0} if before else {},
        compiler_params=pltpu.CompilerParams(vmem_limit_bytes=40 * 2**20),
        cost_estimate=pl.CostEstimate(flops=10**10, bytes_accessed=10**6, transcendentals=0),
        name="update_front",
    )(side, flags, front, rows, lower, high, low, col_high, col_low, *before)


def block_flags(slots, listed_one, listed_two, diag_slots):
    one = jnp.any(slots[:, None] == listed_one[None, :], axis=1).astype(jnp.int32)
    two = jnp.any(slots[:, None] == listed_two[None, :], axis=1).astype(jnp.int32)
    order = jnp.arange(1, NC + 1, dtype=jnp.int32)
    where = jnp.sum(jnp.where(slots[:, None] == diag_slots[None, :], order[None, :], 0), axis=1) - 1
    return jnp.stack([one, two, where], axis=1)


def gather_summed(front, block_slots, rows_first, rows_second):
    grid_rows, grid_cols = lax.axis_size("row"), lax.axis_size("col")
    own_row, own_col = lax.axis_index("row"), lax.axis_index("col")
    row_blocks, col_blocks = front.shape[0], front.shape[3]
    diag_slots = block_slots[:NC]
    listed_one = block_slots[rows_first]
    listed_two = block_slots[rows_second]
    row_slots = jnp.arange(row_blocks, dtype=jnp.int32) * grid_rows + own_row
    col_slots = jnp.arange(row_blocks, dtype=jnp.int32) * grid_cols + own_col
    flags = jnp.concatenate(
        [block_flags(slots, listed_one, listed_two, diag_slots) for slots in (row_slots, col_slots)], axis=1
    )
    flags = jnp.pad(flags, ((0, 0), (0, 2)))
    local = front.reshape(row_blocks, BS, col_blocks, BS)
    pieces = []
    rows = []
    for c in range(NC):
        piece = lax.dynamic_index_in_dim(local, diag_slots[c] // grid_cols, 2, keepdims=False)
        pieces.append(jnp.where(diag_slots[c] % grid_cols == own_col, piece, jnp.zeros_like(piece)))
        piece = lax.dynamic_index_in_dim(local, diag_slots[c] // grid_rows, 0, keepdims=False)
        rows.append(jnp.where(diag_slots[c] % grid_rows == own_row, piece, jnp.zeros_like(piece)))
    pieces = jnp.stack(pieces, axis=0)
    blocks = []
    for i in range(NC):
        part = lax.dynamic_index_in_dim(pieces, diag_slots[i] // grid_rows, 1, keepdims=False)[: i + 1]
        blocks.append(jnp.where(diag_slots[i] % grid_rows == own_row, part, jnp.zeros_like(part)))
    diag = lax.psum(jnp.concatenate(blocks, axis=0), ("row", "col"))
    return flags, lax.psum(jnp.stack(rows, axis=0), "row"), diag, lax.psum(pieces, "col")


def factor_panel(diag, after, hooks):
    lowers, inverses = [], []
    for n in range(PB):
        lower, inverse, token = piece(n, diag, lowers, inverses, hooks(n, after))
        lowers.append(lower)
        inverses.append(inverse)
        after = [token]
    return lowers, inverses, after


def factor_both(diag, after, hooks):
    lowers, inverses, after = factor_panel(diag, after, hooks[0])
    second, after = hooks[1](after)
    cross, corner = between(second, inverses, after)
    more_lowers, more_inverses, _ = factor_panel(corner, [], lambda n, after: after)
    return finish(inverses, more_inverses, cross, lowers + more_lowers)


def work(front, flags, block_slots, terms, keep, got):
    (own, *parts), _ = spread("col", terms, [])
    (own_two, *parts_two), _ = spread("row", [keep, got], [])
    state = {"two": [own_two] + across("row", parts_two)}
    value = [own] + across("col", parts)
    value, _ = total(value, [])
    value, token = collect("col", value, across("col", [value] * 3), [])
    one, two, token = lines(front, block_slots, token)
    got_one = permute(one, lambda p, q: (p ^ 1, q))
    got_two = permute(two, lambda p, q: (p ^ 2, q))
    value, _ = collect("row", value, across("row", [value] * 3), [])
    diag, ready = join(value, swap_core(value))

    def beside(n, after):
        terms = state["two"]
        if n == 0:
            (own, *parts), token = spread("col", terms, [ready, token_lines])
            state["two"] = [own] + across("col", parts)
        elif n == 1:
            value, token = total(terms, after)
            state["two"] = [value] + across("col", [value] * 3)
        elif n == 2:
            value, token = collect("col", terms[0], terms[1:], after)
            state["two"] = [value] + across("row", [value] * 3)
        else:
            value, token = collect("row", terms[0], terms[1:], after)
            state["two"] = [value, swap_core(value)]
        return [token]

    token_lines = token

    def second(after):
        *sums, token = add_pairs(one, got_one, two, got_two, after[0])
        state["sums"] = sums
        state["more"] = [permute(sums[0], lambda p, q: (p ^ 2, q)), permute(sums[1], lambda p, q: (p ^ 1, q))]
        blocks, _ = join(*state["two"])
        return blocks, [token]

    lower, high, low = factor_both(diag, [], (beside, second))
    (one, two), (more_one, more_two) = state["sums"], state["more"]
    return lower, high, low, *solve_columns(flags, one, more_one, two, more_two, high, low)


def on_device(front, block_slots, rows_first, rows_second):
    half = front.shape[0] // 2
    if (lax.axis_size("row"), lax.axis_size("col")) != (4, 8):
        flags, cols, diag, panel = gather_summed(front, block_slots, rows_first, rows_second)
        one = PB * (PB + 1) // 2
        hooks = (lambda n, after: after), (lambda after: (diag[one:], after))
        factors = factor_both(diag[:one], [], hooks)
        none = jnp.zeros_like(cols[:PB])
        columns = solve_columns(flags, cols[:PB], none, cols[PB:], none, *factors[1:])
        rows = [panel[:, 0::2], panel[:, 1::2]]
        sides = jnp.arange(2, dtype=jnp.int32)
    else:
        flags, sides, mine, theirs, parts = start(front, block_slots, rows_first, rows_second)
        keep_one, send_one, keep_two, send_two = parts
        got = swap_core(send_one)
        sibling = swap_core(theirs)
        (own, *others), token = spread("row", [keep_one, got], [])
        summed = merge(mine, sibling, token)
        lined = lax.psum(summed, "col", axis_index_groups=[[0, 2, 4, 6], [1, 3, 5, 7]])
        terms = [own] + across("row", others)
        got = swap_core(send_two)
        run = functools.partial(work, front, flags, block_slots, terms, keep_two, got)
        shapes = jax.eval_shape(run)
        *factors, col_high, col_low = lax.cond(
            sides[0] + sides[1] == 1, run, lambda: tuple(jnp.zeros(x.shape, x.dtype) for x in shapes)
        )
        columns = col_high, col_low
        rows = [lined, swap_core(lined)]
    local = front.reshape(half, 2, BS, front.shape[3], BS)
    out = update_front(sides[:1], flags, local, rows[0], *factors, *columns, [])
    out = update_front(sides[1:], flags, local, rows[1], *factors, *columns, [out])
    return out.reshape(front.shape)


def local_blocks(front):
    return front.reshape(front.shape[0], BS, front.shape[3], BS)


def solution(mesh):
    placed = (P(None, "row", None, None, "col", None), P(), P(), P())
    return jax.shard_map(
        on_device,
        mesh=mesh,
        in_specs=placed,
        out_specs=P(None, "row", None, None, "col", None),
        check_vma=False,
    )
```

```python
import functools

import jax
import jax.numpy as jnp
from jax import lax
from jax.experimental import pallas as pl
from jax.experimental.pallas import tpu as pltpu
from jax.sharding import PartitionSpec as P

BS = 128
PB = 4
NC = 2 * PB
STEP = 8
ALMOST_ALL = 63 * 2**20
HIGHEST = lax.Precision.HIGHEST
HBM = pl.BlockSpec(memory_space=pltpu.HBM)
VMEM = pl.BlockSpec(memory_space=pltpu.VMEM)
SMEM = pl.BlockSpec(memory_space=pltpu.SMEM)


def lane_copy(tile, lane):
    return jnp.broadcast_to(tile[:, lane : lane + 1], tile.shape)


def row_copy(tile, row):
    return jnp.broadcast_to(tile[row : row + 1, :], tile.shape)


def factor_block(block):
    tiles = BS // 8
    sub = lax.broadcasted_iota(jnp.int32, (8, BS), 0)
    lanes = lax.broadcasted_iota(jnp.int32, (8, BS), 1)
    left = [block[8 * i : 8 * i + 8, :] for i in range(tiles)]
    right = [jnp.where(lanes == sub + 8 * i, 1.0, 0.0).astype(jnp.float32) for i in range(tiles)]
    upper = []
    inverse = []
    for j in range(0, BS, STEP):
        g, o = divmod(j, 8)
        if o == 0:
            upper_tile = jnp.zeros((8, BS), jnp.float32)
            inverse_tile = jnp.zeros((8, BS), jnp.float32)
        rows = [row_copy(left[g], o + s) for s in range(STEP)]
        extra = [row_copy(right[g], o + s) for s in range(STEP)]
        first = g if o + STEP < 8 else g + 1
        cols = {i: [lane_copy(left[i], j + s) for s in range(STEP)] for i in range(first, tiles)}
        pivot = [[lane_copy(rows[s], j + t) if t >= s else None for t in range(STEP)] for s in range(STEP)]
        ratio = [[None] * STEP for _ in range(STEP)]
        recip = []
        for s in range(STEP):
            inv = 1.0 / pivot[s][s]
            recip.append(inv)
            for t in range(s + 1, STEP):
                ratio[s][t] = pivot[s][t] * inv
            for t in range(s + 1, STEP):
                for u in range(t, STEP):
                    pivot[t][u] = pivot[t][u] - ratio[s][t] * pivot[s][u]
                rows[t] = rows[t] - ratio[s][t] * rows[s]
                extra[t] = extra[t] - ratio[s][t] * extra[s]
        for s in range(STEP):
            scale = lax.rsqrt(pivot[s][s])
            scale = scale * (1.5 - 0.5 * pivot[s][s] * scale * scale)
            here = sub == o + s
            upper_tile = jnp.where(here, rows[s] * scale, upper_tile)
            inverse_tile = jnp.where(here, extra[s] * scale, inverse_tile)
        if o + STEP == 8:
            upper.append(jnp.where(lanes >= sub + 8 * g, upper_tile, 0.0))
            inverse.append(jnp.where(lanes <= sub + 8 * g, inverse_tile, 0.0))
        for s in reversed(range(STEP)):
            rows[s] = rows[s] * recip[s]
            extra[s] = extra[s] * recip[s]
            for t in range(s + 1, STEP):
                rows[s] = rows[s] - ratio[s][t] * rows[t]
                extra[s] = extra[s] - ratio[s][t] * extra[t]
        for i in range(first, tiles):
            less = cols[i][0] * rows[0]
            less_extra = cols[i][0] * extra[0]
            for s in range(1, STEP):
                less = less + cols[i][s] * rows[s]
                less_extra = less_extra + cols[i][s] * extra[s]
            if i == g:
                below = sub >= o + STEP
                left[i] = jnp.where(below, left[i] - less, left[i])
                right[i] = jnp.where(below, right[i] - less_extra, right[i])
            else:
                left[i] = left[i] - less
                right[i] = right[i] - less_extra
    return jnp.concatenate(upper, axis=0), jnp.concatenate(inverse, axis=0)


def lower_index(i, j):
    return i * (i + 1) // 2 + j


def dot_nt(a, b):
    return lax.dot_general(a, b, (((1,), (1,)), ((), ())), precision=HIGHEST, preferred_element_type=jnp.float32)


def dot_nn(a, b):
    return lax.dot_general(a, b, (((1,), (0,)), ((), ())), precision=HIGHEST, preferred_element_type=jnp.float32)


def split(x):
    high = x.astype(jnp.bfloat16)
    return high, (x - high.astype(jnp.float32)).astype(jnp.bfloat16)


def place(count, core, block):
    half = count // 2
    return (block // half) == core, block % half


def start_kernel(slots, first, second, front_ref, flags, token, panel, keep_one, send_one, keep_two, send_two,
                 zero, blocks, columns, sems, out_sems):
    row_blocks, _, col_blocks = front_ref.shape[:3]
    grid_rows, grid_cols = 4, 8
    own_row = lax.axis_index("row")
    own_col = lax.axis_index("col")
    core = own_col % 2
    slot = [slots[i] for i in range(NC)]
    one = PB * (PB + 1) // 2
    moves = []
    fills = []

    def move(condition, source, middle, targets):
        index = len(moves)

        @pl.when(condition)
        def _():
            pltpu.make_async_copy(source, middle, sems.at[index]).start()

        moves.append((condition, middle, targets, index))

    always = core >= 0
    group = zero.shape[0]
    for c in range(NC):
        owned = slot[c] % grid_cols == own_col
        for a in range(0, row_blocks, group):
            fills.append((jnp.logical_not(owned), zero, panel.at[c, a : a + group], len(moves)))
        move(owned, front_ref.at[:, :, slot[c] // grid_cols], columns.at[c], ((panel.at[c], always),))
    for i in range(NC):
        for j in range(i + 1):
            block = lower_index(i, j)
            if i < PB:
                half, at, keep, send = one // 2, block, keep_one, send_one
            else:
                half, at, keep, send = keep_two.shape[0], block - one, keep_two, send_two
            a = slot[i] // grid_rows
            b = slot[j] // grid_cols
            owned = jnp.logical_and(slot[i] % grid_rows == own_row, slot[j] % grid_cols == own_col)
            stay = core == at // half
            targets = ((keep.at[at % half], stay), (send.at[at % half], jnp.logical_not(stay)))
            for target, chosen in targets:
                fills.append((jnp.logical_and(chosen, jnp.logical_not(owned)), zero.at[0], target, len(moves)))
            move(owned, front_ref.at[a, :, b], blocks.at[block], targets)

    zero[...] = jnp.zeros_like(zero)
    for condition, source, target, index in fills:
        @pl.when(condition)
        def _(source=source, target=target, index=index):
            pltpu.make_async_copy(source, target, out_sems.at[index]).start()

    for a in range(row_blocks):
        for f in range(8):
            flags[a, f] = jnp.int32(-1 if f in (2, 5) else 0)
    for c in range(NC):
        @pl.when(slot[c] % grid_rows == own_row)
        def _(c=c):
            flags[slot[c] // grid_rows, 2] = jnp.int32(c)

        @pl.when(slot[c] % grid_cols == own_col)
        def _(c=c):
            flags[slot[c] // grid_cols, 5] = jnp.int32(c)

    for listed, f in ((first, 0), (second, 1)):
        @pl.loop(0, listed.shape[0])
        def _(i, listed=listed, f=f):
            s = slots[listed[i]]

            @pl.when(s % grid_rows == own_row)
            def _():
                flags[s // grid_rows, f] = jnp.int32(1)

            @pl.when(s % grid_cols == own_col)
            def _():
                flags[s // grid_cols, 3 + f] = jnp.int32(1)

    token[0] = jnp.int32(0)
    for condition, middle, targets, index in moves:
        @pl.when(condition)
        def _(middle=middle, targets=targets, index=index):
            pltpu.make_async_copy(middle, middle, sems.at[index]).wait()
            for target, chosen in targets:
                @pl.when(chosen)
                def _(target=target):
                    pltpu.make_async_copy(middle, target, out_sems.at[index]).start()
    for condition, middle, targets, index in moves:
        pltpu.make_async_copy(middle, middle, out_sems.at[index]).wait()


TOKEN = jax.ShapeDtypeStruct((1,), jnp.int32)


def start(front, block_slots, rows_first, rows_second):
    row_blocks, col_blocks = front.shape[0], front.shape[3]
    one = PB * (PB + 1) // 2
    count = NC * (NC + 1) // 2
    two = count - one
    f32 = lambda *shape: jax.ShapeDtypeStruct(shape, jnp.float32)
    flags, token, panel, *parts = pl.pallas_call(
        start_kernel,
        out_shape=(
            jax.ShapeDtypeStruct((row_blocks, 8), jnp.int32),
            TOKEN,
            f32(NC, row_blocks, BS, 1, BS),
            f32(one // 2, BS, 1, BS),
            f32(one // 2, BS, 1, BS),
            f32(two // 2, BS, 1, BS),
            f32(two // 2, BS, 1, BS),
        ),
        in_specs=[SMEM, SMEM, SMEM, HBM],
        out_specs=(SMEM, SMEM) + (HBM,) * 5,
        scratch_shapes=[
            pltpu.VMEM((row_blocks // 4, BS, 1, BS), jnp.float32),
            pltpu.VMEM((count, BS, 1, BS), jnp.float32),
            pltpu.VMEM((NC, row_blocks, BS, 1, BS), jnp.float32),
            pltpu.SemaphoreType.DMA((count + NC,)),
            pltpu.SemaphoreType.DMA((count + NC,)),
        ],
        compiler_params=pltpu.CompilerParams(vmem_limit_bytes=ALMOST_ALL),
        name="start",
    )(block_slots, rows_first, rows_second, front.reshape(row_blocks, BS, col_blocks, 1, BS))
    return flags, token, panel.reshape(NC, row_blocks, BS, BS), [x.reshape(-1, BS) for x in parts]


def lines_kernel(slots, after, wide_ref, one, two, token, zero, lines, sems, out_sems):
    own_row = lax.axis_index("row")
    col_blocks = wide_ref.shape[2]
    owned = [slots[c] % 4 == own_row for c in range(NC)]
    targets = [(one if c < PB else two).at[c % PB] for c in range(NC)]
    for c in range(NC):
        @pl.when(owned[c])
        def _(c=c):
            for b in range(col_blocks):
                pltpu.make_async_copy(wide_ref.at[slots[c] // 4, :, b], lines.at[c, b], sems.at[c]).start()
    zero[...] = jnp.zeros_like(zero)
    group = zero.shape[0]
    for c in range(NC):
        @pl.when(jnp.logical_not(owned[c]))
        def _(c=c):
            for b in range(0, col_blocks, group):
                pltpu.make_async_copy(zero, targets[c].at[b : b + group], out_sems.at[c]).start()
    for c in range(NC):
        @pl.when(owned[c])
        def _(c=c):
            pltpu.make_async_copy(lines.at[c], lines.at[c], sems.at[c]).wait()
            pltpu.make_async_copy(lines.at[c], targets[c], out_sems.at[c]).start()
    token[0] = jnp.int32(0)
    for c in range(NC):
        pltpu.make_async_copy(lines.at[c], targets[c], out_sems.at[c]).wait()


def lines(front, block_slots, after):
    row_blocks, col_blocks = front.shape[0], front.shape[3]
    part = jax.ShapeDtypeStruct((PB, col_blocks, BS, 1, BS), jnp.float32)
    one, two, token = pl.pallas_call(
        lines_kernel,
        out_shape=(part, part, TOKEN),
        in_specs=[SMEM, SMEM, HBM],
        out_specs=(HBM, HBM, SMEM),
        scratch_shapes=[
            pltpu.VMEM((2, BS, 1, BS), jnp.float32),
            pltpu.VMEM((NC, col_blocks, BS, 1, BS), jnp.float32),
            pltpu.SemaphoreType.DMA((NC,)),
            pltpu.SemaphoreType.DMA((NC,)),
        ],
        compiler_params=pltpu.CompilerParams(vmem_limit_bytes=ALMOST_ALL),
        name="lines",
    )(block_slots, after, front.reshape(row_blocks, BS, col_blocks, 1, BS))
    shape = (PB, col_blocks, BS, BS)
    return one.reshape(shape), two.reshape(shape), token


def add_kernel(after, a, b, c, d, first, second, token):
    first[...] = a[...] + b[...]
    second[...] = c[...] + d[...]

    @pl.when(pl.program_id(0) == 0)
    def _():
        token[0] = jnp.int32(0)


def add_pairs(a, b, c, d, after):
    block = pl.BlockSpec((1,) + a.shape[1:], lambda i: (i,) + (0,) * (a.ndim - 1))
    return pl.pallas_call(
        add_kernel,
        out_shape=(jax.ShapeDtypeStruct(a.shape, a.dtype),) * 2 + (TOKEN,),
        grid=(a.shape[0],),
        in_specs=[SMEM] + [block] * 4,
        out_specs=(block, block, SMEM),
        name="add_pairs",
    )(after, a, b, c, d)


def permute(value, flip):
    pairs = []
    for p in range(4):
        for q in range(8):
            to_p, to_q = flip(p, q)
            if 0 <= to_q < 8:
                pairs.append((p * 8 + q, to_p * 8 + to_q))
    return lax.ppermute(value, ("row", "col"), pairs)


def swap_core(value):
    return permute(value, lambda p, q: (p, q ^ 1))


def place(axis):
    return lax.axis_index("row") if axis == "row" else lax.axis_index("col") // 2


def spread_kernel(axis, count, *refs):
    token, total = refs[-2:]
    outs = refs[-6:-2]
    value = refs[0][...]
    for ref in refs[1:count]:
        value = value + ref[...]
    total[...] = value
    own = place(axis)
    for d in range(4):
        outs[d][...] = total[own ^ d]
    token[0] = jnp.int32(0)


def spread(axis, terms, after):
    rows = terms[0].shape[0] // 4
    shape = (4, rows, BS)
    *parts, token = pl.pallas_call(
        functools.partial(spread_kernel, axis, len(terms)),
        out_shape=(jax.ShapeDtypeStruct((rows, BS), jnp.float32),) * 4 + (TOKEN,),
        in_specs=[VMEM] * len(terms) + [SMEM] * len(after),
        out_specs=(VMEM,) * 4 + (SMEM,),
        scratch_shapes=[pltpu.VMEM(shape, jnp.float32)],
        name="spread",
    )(*[term.reshape(shape) for term in terms], *after)
    return parts, token


def total_kernel(*refs):
    out, token = refs[-2:]
    out[...] = refs[0][...] + refs[1][...] + refs[2][...] + refs[3][...]
    token[0] = jnp.int32(0)


def total(terms, after):
    return pl.pallas_call(
        total_kernel,
        out_shape=(jax.ShapeDtypeStruct(terms[0].shape, jnp.float32), TOKEN),
        in_specs=[VMEM] * 4 + [SMEM] * len(after),
        out_specs=(VMEM, SMEM),
        name="total",
    )(*terms, *after)


def collect_kernel(axis, own, one, two, three, *rest):
    out, token = rest[-2:]
    at = place(axis)
    for d, source in enumerate((own, one, two, three)):
        out[at ^ d] = source[...]
    token[0] = jnp.int32(0)


def collect(axis, own, others, after):
    rows = own.shape[0]
    out, token = pl.pallas_call(
        functools.partial(collect_kernel, axis),
        out_shape=(jax.ShapeDtypeStruct((4, rows, BS), jnp.float32), TOKEN),
        in_specs=[VMEM] * 4 + [SMEM] * len(after),
        out_specs=(VMEM, SMEM),
        name="collect",
    )(own, *others, *after)
    return out.reshape(4 * rows, BS), token


def join_kernel(own, other, out, token):
    core = lax.axis_index("col") % 2
    out[core] = own[...]
    out[1 - core] = other[...]
    token[0] = jnp.int32(0)


def join(own, other):
    out, token = pl.pallas_call(
        join_kernel,
        out_shape=(jax.ShapeDtypeStruct((2,) + own.shape, jnp.float32), TOKEN),
        in_specs=[VMEM] * 2,
        out_specs=(VMEM, SMEM),
        name="join",
    )(own, other)
    return out.reshape(-1, BS, BS), token


def across(axis, parts):
    if axis == "row":
        return [permute(parts[d - 1], lambda p, q, d=d: (p ^ d, q)) for d in range(1, 4)]
    return [permute(parts[d - 1], lambda p, q, d=d: (p, q ^ (2 * d))) for d in range(1, 4)]


def piece_kernel(n, diag, *rest):
    lowers = rest[:n]
    inverses = rest[n : 2 * n]
    lower_out, inverse_out, token = rest[-3:]
    token[0] = jnp.int32(0)

    def row(i):
        return jnp.concatenate([lowers[j][(i - j) * BS : (i - j + 1) * BS, :] for j in range(n)], axis=1)

    column = []
    for i in range(n, PB):
        value = diag[lower_index(i, n)]
        if n:
            value = value - dot_nt(row(i), row(n))
        column.append(value)
    upper, inverse = factor_block(column[0])
    lower_out[0:BS, :] = upper.T
    if n + 1 < PB:
        lower_out[BS:, :] = dot_nt(jnp.concatenate(column[1:], axis=0), inverse)
    inverse_out[:, n * BS :] = inverse
    if n:
        before = jnp.concatenate(
            [
                jnp.concatenate([inverses[j][...], jnp.zeros((BS, (n - 1 - j) * BS), jnp.float32)], axis=1)
                if j + 1 < n
                else inverses[j][...]
                for j in range(n)
            ],
            axis=0,
        )
        inverse_out[:, : n * BS] = -dot_nn(inverse, dot_nn(row(n), before))


def piece(n, diag, lowers, inverses, after):
    return pl.pallas_call(
        functools.partial(piece_kernel, n),
        out_shape=(
            jax.ShapeDtypeStruct(((PB - n) * BS, BS), jnp.float32),
            jax.ShapeDtypeStruct((BS, (n + 1) * BS), jnp.float32),
            TOKEN,
        ),
        in_specs=[VMEM] * (1 + 2 * n) + [SMEM] * len(after),
        out_specs=(VMEM, VMEM, SMEM),
        compiler_params=pltpu.CompilerParams(vmem_limit_bytes=32 * 2**20),
        cost_estimate=pl.CostEstimate(flops=10**8, bytes_accessed=10**5, transcendentals=0),
        name="factor_piece",
    )(diag, *lowers, *inverses, *after)


def inverse_rows(inverses):
    rows = []
    for j in range(PB):
        if j + 1 < PB:
            rows.append(jnp.concatenate([inverses[j][...], jnp.zeros((BS, (PB - 1 - j) * BS), jnp.float32)], axis=1))
        else:
            rows.append(inverses[j][...])
    return jnp.concatenate(rows, axis=0)


def between_kernel(diag, *rest):
    inverses = rest[:PB]
    cross_out, rest_out = rest[-2:]
    inverse = inverse_rows(inverses)
    one = PB * (PB + 1) // 2
    left = [
        jnp.concatenate([diag[lower_index(i, j) - one] for j in range(PB)], axis=1) for i in range(PB, NC)
    ]
    cross = dot_nt(jnp.concatenate(left, axis=0), inverse)
    cross_out[...] = cross
    for i in range(PB):
        here = cross[i * BS : (i + 1) * BS, :]
        product = dot_nt(here, cross[: (i + 1) * BS, :])
        for j in range(i + 1):
            block = diag[lower_index(i + PB, j + PB) - one]
            rest_out[lower_index(i, j)] = block - product[:, j * BS : (j + 1) * BS]


def between(diag, inverses, after):
    return pl.pallas_call(
        between_kernel,
        out_shape=(
            jax.ShapeDtypeStruct((PB * BS, PB * BS), jnp.float32),
            jax.ShapeDtypeStruct((PB * (PB + 1) // 2, BS, BS), jnp.float32),
        ),
        in_specs=[VMEM] * (1 + PB) + [SMEM] * len(after),
        out_specs=(VMEM, VMEM),
        compiler_params=pltpu.CompilerParams(vmem_limit_bytes=32 * 2**20),
        cost_estimate=pl.CostEstimate(flops=10**8, bytes_accessed=10**5, transcendentals=0),
        name="between",
    )(diag, *inverses, *after)


def finish_kernel(*refs):
    first = inverse_rows(refs[:PB])
    second = inverse_rows(refs[PB : 2 * PB])
    cross = refs[2 * PB][...]
    lowers = refs[2 * PB + 1 : 4 * PB + 1]
    lower_out, high_out, low_out = refs[-3:]
    size = PB * BS
    lower_out[...] = jnp.zeros_like(lower_out)
    for j in range(PB):
        for half in range(2):
            rows = slice(half * size + j * BS, (half + 1) * size)
            lower_out[rows, j * BS : (j + 1) * BS] = lowers[half * PB + j][...]
    high_out[:size, size:] = jnp.zeros((size, size), jnp.bfloat16)
    low_out[:size, size:] = jnp.zeros((size, size), jnp.bfloat16)
    inner = three(nn, *split(cross), *split(first))
    corner = -three(nn, *split(second), *split(inner))
    for value, rows, cols in (
        (first, slice(0, size), slice(0, size)),
        (corner, slice(size, 2 * size), slice(0, size)),
        (second, slice(size, 2 * size), slice(size, 2 * size)),
    ):
        high, low = split(value)
        high_out[rows, cols] = high
        low_out[rows, cols] = low


def finish(first, second, cross, lowers):
    size = NC * BS
    return pl.pallas_call(
        finish_kernel,
        out_shape=(jax.ShapeDtypeStruct((size, size // 2), jnp.float32),)
        + (jax.ShapeDtypeStruct((size, size), jnp.bfloat16),) * 2,
        in_specs=[VMEM] * (4 * PB + 1),
        out_specs=(VMEM,) * 3,
        compiler_params=pltpu.CompilerParams(vmem_limit_bytes=32 * 2**20),
        cost_estimate=pl.CostEstimate(flops=10**8, bytes_accessed=10**5, transcendentals=0),
        name="finish",
    )(*first, *second, cross, *lowers)


def three(dot, a_high, a_low, b_high, b_low):
    kwargs = dict(preferred_element_type=jnp.float32)
    return dot(a_high, b_high, **kwargs) + (dot(a_high, b_low, **kwargs) + dot(a_low, b_high, **kwargs))


def nt(a, b, **kwargs):
    return lax.dot_general(a, b, (((1,), (1,)), ((), ())), **kwargs)


def nn(a, b, **kwargs):
    return lax.dot_general(a, b, (((1,), (0,)), ((), ())), **kwargs)


def masked(tiles, axis, first, second):
    low_part = jnp.concatenate(tiles[:PB], axis=axis)
    high_part = jnp.concatenate(tiles[PB:], axis=axis)
    zero = jnp.zeros_like(low_part)
    return jnp.concatenate([jnp.where(first, low_part, zero), jnp.where(second, high_part, zero)], axis=axis)


def columns_kernel(flags, one, one_more, two, two_more, high_ref, low_ref, col_high, col_low, total):
    size = NC * BS
    half = PB * BS
    width = 2 * BS
    step = pl.program_id(0)
    col_blocks = one.shape[1]
    first_half = step < PB // 2
    for chosen, part, more, column in (
        (first_half, one, one_more, 3),
        (jnp.logical_not(first_half), two, two_more, 4),
    ):
        @pl.when(chosen)
        def _(part=part, more=more, column=column):
            for b in range(col_blocks):
                at = slice(b * BS, (b + 1) * BS)
                raw = jnp.concatenate([part[c, b] + more[c, b] for c in range(2)], axis=0)
                high, low = split(jnp.where(flags[b, column] != 0, raw, jnp.zeros_like(raw)))
                col_high[:width, at] = high
                col_low[:width, at] = low

    high, low = col_high[:width, :], col_low[:width, :]
    for m in range(0, size, width):
        rows = slice(m, m + width)

        @pl.when(step == 0)
        def _(rows=rows):
            total[rows, :] = three(nn, high_ref[rows, :], low_ref[rows, :], high, low)

        if m > 0:
            @pl.when(jnp.logical_and(step > 0, step * width <= m))
            def _(rows=rows):
                total[rows, :] = total[rows, :] + three(nn, high_ref[rows, :], low_ref[rows, :], high, low)

    @pl.when(step == pl.num_programs(0) - 1)
    def _():
        for b in range(col_blocks):
            at = slice(b * BS, (b + 1) * BS)
            for rows, f in ((slice(0, half), 3), (slice(half, size), 4)):
                value = total[rows, at]
                high, low = split(jnp.where(flags[b, f] != 0, value, jnp.zeros_like(value)))
                col_high[rows, at] = high
                col_low[rows, at] = low


def solve_columns(flags, one, one_more, two, two_more, high, low):
    size = NC * BS
    width = 2 * BS
    shape = (size, one.shape[1] * BS)
    first = pl.BlockSpec((2,) + one.shape[1:], lambda i: (jnp.minimum(i, PB // 2 - 1), 0, 0, 0))
    second = pl.BlockSpec((2,) + one.shape[1:], lambda i: (jnp.maximum(i - PB // 2, 0), 0, 0, 0))
    strip = pl.BlockSpec((size, width), lambda i: (0, i))
    whole = pl.BlockSpec(shape, lambda i: (0, 0))
    return pl.pallas_call(
        columns_kernel,
        out_shape=(jax.ShapeDtypeStruct(shape, jnp.bfloat16),) * 2,
        grid=(NC // 2,),
        in_specs=[SMEM, first, first, second, second, strip, strip],
        out_specs=(whole, whole),
        scratch_shapes=[pltpu.VMEM(shape, jnp.float32)],
        compiler_params=pltpu.CompilerParams(vmem_limit_bytes=48 * 2**20),
        name="solve_columns",
    )(flags, one, one_more, two, two_more, high, low)


def update_kernel(flags, front_ref, rows_ref, lower_ref, high_ref, low_ref, col_high, col_low, out_ref,
                  solved, sol_high, sol_low):
    size = NC * BS
    half = PB * BS
    width = 2 * BS
    step = pl.program_id(0)
    col_blocks = front_ref.shape[1]
    tall = rows_ref.shape[1]
    index = [step * tall + k for k in range(tall)]
    for k, a in enumerate(index):
        raw = masked([rows_ref[c, k] for c in range(NC)], 1, flags[a, 0] != 0, flags[a, 1] != 0)
        high, low = split(raw)
        sol_high[k * BS : (k + 1) * BS, :] = high
        sol_low[k * BS : (k + 1) * BS, :] = low
    for m in range(0, size, width):
        deep = m + width
        value = three(nt, sol_high[:, :deep], sol_low[:, :deep], high_ref[m:deep, :deep], low_ref[m:deep, :deep])
        if m >= half:
            value = jnp.concatenate(
                [jnp.where(flags[a, 1] != 0, value[k * BS : (k + 1) * BS, :], 0.0) for k, a in enumerate(index)],
                axis=0,
            )
        solved[:, m:deep] = value
    high, low = split(solved[...])
    sol_high[...] = high
    sol_low[...] = low
    for k in range(tall):
        rows = slice(k * BS, (k + 1) * BS)
        value = three(nn, sol_high[rows, :], sol_low[rows, :], col_high[...], col_low[...])
        out_ref[rows] = front_ref[rows] - value.reshape(BS, col_blocks, BS)
    for b in range(col_blocks):
        j = flags[b, 5]

        @pl.when(j >= 0)
        def _(b=b, j=j):
            at = pl.ds(pl.multiple_of(j * BS, BS), BS)
            for k, a in enumerate(index):
                rows = slice(k * BS, (k + 1) * BS)
                listed = jnp.where(j < PB, flags[a, 0], flags[a, 1])
                own = flags[a, 2]

                @pl.when(listed != 0)
                def _(rows=rows):
                    out_ref[rows, b, :] = solved[rows, at]

                @pl.when(jnp.logical_and(own >= 0, own // PB == j // PB))
                def _(rows=rows, own=own):
                    source = pl.ds(pl.multiple_of(own * BS, BS), BS)
                    inside = pl.ds(pl.multiple_of(j % PB * BS, BS), BS)
                    out_ref[rows, b, :] = lower_ref[source, inside]


def update_front(flags, front, rows, lower, high, low, col_high, col_low):
    row_blocks, _, col_blocks = front.shape[:3]
    size = NC * BS
    tall = 2
    block = pl.BlockSpec((tall * BS, col_blocks, BS), lambda i: (i, 0, 0))
    return pl.pallas_call(
        update_kernel,
        out_shape=jax.ShapeDtypeStruct((row_blocks * BS, col_blocks, BS), jnp.float32),
        grid=(row_blocks // tall,),
        in_specs=[SMEM, block, pl.BlockSpec((NC, tall, BS, BS), lambda i: (0, i, 0, 0))] + [VMEM] * 5,
        out_specs=block,
        scratch_shapes=[
            pltpu.VMEM((tall * BS, size), jnp.float32),
            pltpu.VMEM((tall * BS, size), jnp.bfloat16),
            pltpu.VMEM((tall * BS, size), jnp.bfloat16),
        ],
        compiler_params=pltpu.CompilerParams(vmem_limit_bytes=ALMOST_ALL),
        cost_estimate=pl.CostEstimate(flops=10**9, bytes_accessed=10**6, transcendentals=0),
        name="update_front",
    )(flags, front.reshape(row_blocks * BS, col_blocks, BS), rows, lower, high, low, col_high, col_low)


def block_flags(slots, listed_one, listed_two, diag_slots):
    one = jnp.any(slots[:, None] == listed_one[None, :], axis=1).astype(jnp.int32)
    two = jnp.any(slots[:, None] == listed_two[None, :], axis=1).astype(jnp.int32)
    order = jnp.arange(1, NC + 1, dtype=jnp.int32)
    where = jnp.sum(jnp.where(slots[:, None] == diag_slots[None, :], order[None, :], 0), axis=1) - 1
    return jnp.stack([one, two, where], axis=1)


def gather_summed(front, block_slots, rows_first, rows_second):
    grid_rows, grid_cols = lax.axis_size("row"), lax.axis_size("col")
    own_row, own_col = lax.axis_index("row"), lax.axis_index("col")
    row_blocks, col_blocks = front.shape[0], front.shape[3]
    diag_slots = block_slots[:NC]
    listed_one = block_slots[rows_first]
    listed_two = block_slots[rows_second]
    row_slots = jnp.arange(row_blocks, dtype=jnp.int32) * grid_rows + own_row
    col_slots = jnp.arange(row_blocks, dtype=jnp.int32) * grid_cols + own_col
    flags = jnp.concatenate(
        [block_flags(slots, listed_one, listed_two, diag_slots) for slots in (row_slots, col_slots)], axis=1
    )
    flags = jnp.pad(flags, ((0, 0), (0, 2)))
    local = front.reshape(row_blocks, BS, col_blocks, BS)
    pieces = []
    rows = []
    for c in range(NC):
        piece = lax.dynamic_index_in_dim(local, diag_slots[c] // grid_cols, 2, keepdims=False)
        pieces.append(jnp.where(diag_slots[c] % grid_cols == own_col, piece, jnp.zeros_like(piece)))
        piece = lax.dynamic_index_in_dim(local, diag_slots[c] // grid_rows, 0, keepdims=False)
        rows.append(jnp.where(diag_slots[c] % grid_rows == own_row, piece, jnp.zeros_like(piece)))
    pieces = jnp.stack(pieces, axis=0)
    blocks = []
    for i in range(NC):
        part = lax.dynamic_index_in_dim(pieces, diag_slots[i] // grid_rows, 1, keepdims=False)[: i + 1]
        blocks.append(jnp.where(diag_slots[i] % grid_rows == own_row, part, jnp.zeros_like(part)))
    diag = lax.psum(jnp.concatenate(blocks, axis=0), ("row", "col"))
    return flags, lax.psum(jnp.stack(rows, axis=0), "row"), diag, lax.psum(pieces, "col")


def factor_panel(diag, after, hooks):
    lowers, inverses = [], []
    for n in range(PB):
        lower, inverse, token = piece(n, diag, lowers, inverses, hooks(n, after))
        lowers.append(lower)
        inverses.append(inverse)
        after = [token]
    return lowers, inverses, after


def factor_both(diag, after, hooks):
    lowers, inverses, after = factor_panel(diag, after, hooks[0])
    second, after = hooks[1](after)
    cross, corner = between(second, inverses, after)
    more_lowers, more_inverses, _ = factor_panel(corner, [], lambda n, after: after)
    return finish(inverses, more_inverses, cross, lowers + more_lowers)


def work(front, flags, block_slots, terms, keep, got):
    (own, *parts), _ = spread("col", terms, [])
    (own_two, *parts_two), _ = spread("row", [keep, got], [])
    state = {"two": [own_two] + across("row", parts_two)}
    value = [own] + across("col", parts)
    value, _ = total(value, [])
    value, _ = collect("col", value, across("col", [value] * 3), [])
    value, token = collect("row", value, across("row", [value] * 3), [])
    other = swap_core(value)
    one, two, token = lines(front, block_slots, token)
    got_one = permute(one, lambda p, q: (p ^ 1, q))
    got_two = permute(two, lambda p, q: (p ^ 2, q))
    diag, ready = join(value, other)

    def beside(n, after):
        terms = state["two"]
        if n == 0:
            (own, *parts), token = spread("col", terms, [ready, token_lines])
            state["two"] = [own] + across("col", parts)
        elif n == 1:
            value, token = total(terms, after)
            state["two"] = [value] + across("col", [value] * 3)
        elif n == 2:
            value, token = collect("col", terms[0], terms[1:], after)
            state["two"] = [value] + across("row", [value] * 3)
        else:
            value, token = collect("row", terms[0], terms[1:], after)
            state["two"] = [value, swap_core(value)]
        return [token]

    token_lines = token

    def second(after):
        *sums, token = add_pairs(one, got_one, two, got_two, after[0])
        state["sums"] = sums
        state["more"] = [permute(sums[0], lambda p, q: (p ^ 2, q)), permute(sums[1], lambda p, q: (p ^ 1, q))]
        blocks, _ = join(*state["two"])
        return blocks, [token]

    lower, high, low = factor_both(diag, [], (beside, second))
    (one, two), (more_one, more_two) = state["sums"], state["more"]
    return lower, high, low, *solve_columns(flags, one, more_one, two, more_two, high, low)


def on_device(front, block_slots, rows_first, rows_second):
    if (lax.axis_size("row"), lax.axis_size("col")) != (4, 8):
        flags, cols, diag, panel = gather_summed(front, block_slots, rows_first, rows_second)
        one = PB * (PB + 1) // 2
        hooks = (lambda n, after: after), (lambda after: (diag[one:], after))
        factors = factor_both(diag[:one], [], hooks)
        cols = jnp.swapaxes(cols, 1, 2)
        none = jnp.zeros_like(cols[:PB])
        columns = solve_columns(flags, cols[:PB], none, cols[PB:], none, *factors[1:])
    else:
        flags, token, panel, parts = start(front, block_slots, rows_first, rows_second)
        keep_one, send_one, keep_two, send_two = parts
        panel = lax.psum(panel, "col")
        (own, *others), _ = spread("row", [keep_one, swap_core(send_one)], [])
        terms = [own] + across("row", others)
        run = functools.partial(work, front, flags, block_slots, terms, keep_two, swap_core(send_two))
        shapes = jax.eval_shape(run)
        *factors, col_high, col_low = lax.cond(
            token[0] == 0, run, lambda: tuple(jnp.zeros(x.shape, x.dtype) for x in shapes)
        )
        columns = col_high, col_low
    out = update_front(flags, local_blocks(front), panel, *factors, *columns)
    return out.reshape(front.shape)


def local_blocks(front):
    return front.reshape(front.shape[0], BS, front.shape[3], BS)


def solution(mesh):
    placed = (P(None, "row", None, None, "col", None), P(), P(), P())
    return jax.shard_map(
        on_device,
        mesh=mesh,
        in_specs=placed,
        out_specs=P(None, "row", None, None, "col", None),
        check_vma=False,
    )
```

```python
import functools

import jax
import jax.numpy as jnp
from jax import lax
from jax.experimental import pallas as pl
from jax.experimental.pallas import tpu as pltpu
from jax.sharding import PartitionSpec as P

BS = 128
PB = 4
NC = 2 * PB
STEP = 8
ALMOST_ALL = 63 * 2**20
HIGHEST = lax.Precision.HIGHEST
HBM = pl.BlockSpec(memory_space=pltpu.HBM)
VMEM = pl.BlockSpec(memory_space=pltpu.VMEM)
SMEM = pl.BlockSpec(memory_space=pltpu.SMEM)


def lane_copy(tile, lane):
    return jnp.broadcast_to(tile[:, lane : lane + 1], tile.shape)


def row_copy(tile, row):
    return jnp.broadcast_to(tile[row : row + 1, :], tile.shape)


def factor_block(block):
    tiles = BS // 8
    sub = lax.broadcasted_iota(jnp.int32, (8, BS), 0)
    lanes = lax.broadcasted_iota(jnp.int32, (8, BS), 1)
    left = [block[8 * i : 8 * i + 8, :] for i in range(tiles)]
    right = [jnp.where(lanes == sub + 8 * i, 1.0, 0.0).astype(jnp.float32) for i in range(tiles)]
    upper = []
    inverse = []
    for j in range(0, BS, STEP):
        g, o = divmod(j, 8)
        if o == 0:
            upper_tile = jnp.zeros((8, BS), jnp.float32)
            inverse_tile = jnp.zeros((8, BS), jnp.float32)
        rows = [row_copy(left[g], o + s) for s in range(STEP)]
        extra = [row_copy(right[g], o + s) for s in range(STEP)]
        first = g if o + STEP < 8 else g + 1
        cols = {i: [lane_copy(left[i], j + s) for s in range(STEP)] for i in range(first, tiles)}
        pivot = [[lane_copy(rows[s], j + t) if t >= s else None for t in range(STEP)] for s in range(STEP)]
        ratio = [[None] * STEP for _ in range(STEP)]
        recip = []
        for s in range(STEP):
            inv = 1.0 / pivot[s][s]
            recip.append(inv)
            for t in range(s + 1, STEP):
                ratio[s][t] = pivot[s][t] * inv
            for t in range(s + 1, STEP):
                for u in range(t, STEP):
                    pivot[t][u] = pivot[t][u] - ratio[s][t] * pivot[s][u]
                rows[t] = rows[t] - ratio[s][t] * rows[s]
                extra[t] = extra[t] - ratio[s][t] * extra[s]
        for s in range(STEP):
            scale = lax.rsqrt(pivot[s][s])
            scale = scale * (1.5 - 0.5 * pivot[s][s] * scale * scale)
            here = sub == o + s
            upper_tile = jnp.where(here, rows[s] * scale, upper_tile)
            inverse_tile = jnp.where(here, extra[s] * scale, inverse_tile)
        if o + STEP == 8:
            upper.append(jnp.where(lanes >= sub + 8 * g, upper_tile, 0.0))
            inverse.append(jnp.where(lanes <= sub + 8 * g, inverse_tile, 0.0))
        for s in reversed(range(STEP)):
            rows[s] = rows[s] * recip[s]
            extra[s] = extra[s] * recip[s]
            for t in range(s + 1, STEP):
                rows[s] = rows[s] - ratio[s][t] * rows[t]
                extra[s] = extra[s] - ratio[s][t] * extra[t]
        for i in range(first, tiles):
            less = cols[i][0] * rows[0]
            less_extra = cols[i][0] * extra[0]
            for s in range(1, STEP):
                less = less + cols[i][s] * rows[s]
                less_extra = less_extra + cols[i][s] * extra[s]
            if i == g:
                below = sub >= o + STEP
                left[i] = jnp.where(below, left[i] - less, left[i])
                right[i] = jnp.where(below, right[i] - less_extra, right[i])
            else:
                left[i] = left[i] - less
                right[i] = right[i] - less_extra
    return jnp.concatenate(upper, axis=0), jnp.concatenate(inverse, axis=0)


def lower_index(i, j):
    return i * (i + 1) // 2 + j


def dot_nt(a, b):
    return lax.dot_general(a, b, (((1,), (1,)), ((), ())), precision=HIGHEST, preferred_element_type=jnp.float32)


def dot_nn(a, b):
    return lax.dot_general(a, b, (((1,), (0,)), ((), ())), precision=HIGHEST, preferred_element_type=jnp.float32)


def split(x):
    high = x.astype(jnp.bfloat16)
    return high, (x - high.astype(jnp.float32)).astype(jnp.bfloat16)


def place(count, core, block):
    half = count // 2
    return (block // half) == core, block % half


def start_kernel(slots, first, second, front_ref, flags, token, panel, keep_one, send_one, keep_two, send_two,
                 zero, blocks, columns, sems, out_sems):
    row_blocks, _, col_blocks = front_ref.shape[:3]
    grid_rows, grid_cols = 4, 8
    own_row = lax.axis_index("row")
    own_col = lax.axis_index("col")
    core = own_col % 2
    slot = [slots[i] for i in range(NC)]
    one = PB * (PB + 1) // 2
    moves = []
    fills = []

    def move(condition, source, middle, targets):
        index = len(moves)

        @pl.when(condition)
        def _():
            pltpu.make_async_copy(source, middle, sems.at[index]).start()

        moves.append((condition, middle, targets, index))

    always = core >= 0
    group = zero.shape[0]
    for c in range(NC):
        owned = slot[c] % grid_cols == own_col
        for a in range(0, row_blocks, group):
            fills.append((jnp.logical_not(owned), zero, panel.at[c, a : a + group], len(moves)))
        move(owned, front_ref.at[:, :, slot[c] // grid_cols], columns.at[c], ((panel.at[c], always),))
    for i in range(NC):
        for j in range(i + 1):
            block = lower_index(i, j)
            if i < PB:
                half, at, keep, send = one // 2, block, keep_one, send_one
            else:
                half, at, keep, send = keep_two.shape[0], block - one, keep_two, send_two
            a = slot[i] // grid_rows
            b = slot[j] // grid_cols
            owned = jnp.logical_and(slot[i] % grid_rows == own_row, slot[j] % grid_cols == own_col)
            stay = core == at // half
            targets = ((keep.at[at % half], stay), (send.at[at % half], jnp.logical_not(stay)))
            for target, chosen in targets:
                fills.append((jnp.logical_and(chosen, jnp.logical_not(owned)), zero.at[0], target, len(moves)))
            move(owned, front_ref.at[a, :, b], blocks.at[block], targets)

    zero[...] = jnp.zeros_like(zero)
    for condition, source, target, index in fills:
        @pl.when(condition)
        def _(source=source, target=target, index=index):
            pltpu.make_async_copy(source, target, out_sems.at[index]).start()

    for a in range(row_blocks):
        for f in range(8):
            flags[a, f] = jnp.int32(-1 if f in (2, 5) else 0)
    for c in range(NC):
        @pl.when(slot[c] % grid_rows == own_row)
        def _(c=c):
            flags[slot[c] // grid_rows, 2] = jnp.int32(c)

        @pl.when(slot[c] % grid_cols == own_col)
        def _(c=c):
            flags[slot[c] // grid_cols, 5] = jnp.int32(c)

    for listed, f in ((first, 0), (second, 1)):
        @pl.loop(0, listed.shape[0])
        def _(i, listed=listed, f=f):
            s = slots[listed[i]]

            @pl.when(s % grid_rows == own_row)
            def _():
                flags[s // grid_rows, f] = jnp.int32(1)

            @pl.when(s % grid_cols == own_col)
            def _():
                flags[s // grid_cols, 3 + f] = jnp.int32(1)

    token[0] = jnp.int32(0)
    for condition, middle, targets, index in moves:
        @pl.when(condition)
        def _(middle=middle, targets=targets, index=index):
            pltpu.make_async_copy(middle, middle, sems.at[index]).wait()
            for target, chosen in targets:
                @pl.when(chosen)
                def _(target=target):
                    pltpu.make_async_copy(middle, target, out_sems.at[index]).start()
    for condition, middle, targets, index in moves:
        pltpu.make_async_copy(middle, middle, out_sems.at[index]).wait()


TOKEN = jax.ShapeDtypeStruct((1,), jnp.int32)


def start(front, block_slots, rows_first, rows_second):
    row_blocks, col_blocks = front.shape[0], front.shape[3]
    one = PB * (PB + 1) // 2
    count = NC * (NC + 1) // 2
    two = count - one
    f32 = lambda *shape: jax.ShapeDtypeStruct(shape, jnp.float32)
    flags, token, panel, *parts = pl.pallas_call(
        start_kernel,
        out_shape=(
            jax.ShapeDtypeStruct((row_blocks, 8), jnp.int32),
            TOKEN,
            f32(NC, row_blocks, BS, 1, BS),
            f32(one // 2, BS, 1, BS),
            f32(one // 2, BS, 1, BS),
            f32(two // 2, BS, 1, BS),
            f32(two // 2, BS, 1, BS),
        ),
        in_specs=[SMEM, SMEM, SMEM, HBM],
        out_specs=(SMEM, SMEM) + (HBM,) * 5,
        scratch_shapes=[
            pltpu.VMEM((row_blocks // 4, BS, 1, BS), jnp.float32),
            pltpu.VMEM((count, BS, 1, BS), jnp.float32),
            pltpu.VMEM((NC, row_blocks, BS, 1, BS), jnp.float32),
            pltpu.SemaphoreType.DMA((count + NC,)),
            pltpu.SemaphoreType.DMA((count + NC,)),
        ],
        compiler_params=pltpu.CompilerParams(vmem_limit_bytes=ALMOST_ALL),
        name="start",
    )(block_slots, rows_first, rows_second, front.reshape(row_blocks, BS, col_blocks, 1, BS))
    return flags, token, panel.reshape(NC, row_blocks, BS, BS), [x.reshape(-1, BS) for x in parts]


def lines_kernel(slots, after, wide_ref, one, two, token, zero, lines, sems, out_sems):
    own_row = lax.axis_index("row")
    col_blocks = wide_ref.shape[2]
    owned = [slots[c] % 4 == own_row for c in range(NC)]
    targets = [(one if c < PB else two).at[c % PB] for c in range(NC)]
    for c in range(NC):
        @pl.when(owned[c])
        def _(c=c):
            for b in range(col_blocks):
                pltpu.make_async_copy(wide_ref.at[slots[c] // 4, :, b], lines.at[c, b], sems.at[c]).start()
    zero[...] = jnp.zeros_like(zero)
    group = zero.shape[0]
    for c in range(NC):
        @pl.when(jnp.logical_not(owned[c]))
        def _(c=c):
            for b in range(0, col_blocks, group):
                pltpu.make_async_copy(zero, targets[c].at[b : b + group], out_sems.at[c]).start()
    for c in range(NC):
        @pl.when(owned[c])
        def _(c=c):
            pltpu.make_async_copy(lines.at[c], lines.at[c], sems.at[c]).wait()
            pltpu.make_async_copy(lines.at[c], targets[c], out_sems.at[c]).start()
    token[0] = jnp.int32(0)
    for c in range(NC):
        pltpu.make_async_copy(lines.at[c], targets[c], out_sems.at[c]).wait()


def lines(front, block_slots, after):
    row_blocks, col_blocks = front.shape[0], front.shape[3]
    part = jax.ShapeDtypeStruct((PB, col_blocks, BS, 1, BS), jnp.float32)
    one, two, token = pl.pallas_call(
        lines_kernel,
        out_shape=(part, part, TOKEN),
        in_specs=[SMEM, SMEM, HBM],
        out_specs=(HBM, HBM, SMEM),
        scratch_shapes=[
            pltpu.VMEM((2, BS, 1, BS), jnp.float32),
            pltpu.VMEM((NC, col_blocks, BS, 1, BS), jnp.float32),
            pltpu.SemaphoreType.DMA((NC,)),
            pltpu.SemaphoreType.DMA((NC,)),
        ],
        compiler_params=pltpu.CompilerParams(vmem_limit_bytes=ALMOST_ALL),
        name="lines",
    )(block_slots, after, front.reshape(row_blocks, BS, col_blocks, 1, BS))
    shape = (PB, col_blocks, BS, BS)
    return one.reshape(shape), two.reshape(shape), token


def add_kernel(after, a, b, c, d, first, second, token):
    first[...] = a[...] + b[...]
    second[...] = c[...] + d[...]

    @pl.when(pl.program_id(0) == 0)
    def _():
        token[0] = jnp.int32(0)


def add_pairs(a, b, c, d, after):
    block = pl.BlockSpec((1,) + a.shape[1:], lambda i: (i,) + (0,) * (a.ndim - 1))
    return pl.pallas_call(
        add_kernel,
        out_shape=(jax.ShapeDtypeStruct(a.shape, a.dtype),) * 2 + (TOKEN,),
        grid=(a.shape[0],),
        in_specs=[SMEM] + [block] * 4,
        out_specs=(block, block, SMEM),
        name="add_pairs",
    )(after, a, b, c, d)


def permute(value, flip):
    pairs = []
    for p in range(4):
        for q in range(8):
            to_p, to_q = flip(p, q)
            if 0 <= to_q < 8:
                pairs.append((p * 8 + q, to_p * 8 + to_q))
    return lax.ppermute(value, ("row", "col"), pairs)


def swap_core(value):
    return permute(value, lambda p, q: (p, q ^ 1))


def place(axis):
    return lax.axis_index("row") if axis == "row" else lax.axis_index("col") // 2


def spread_kernel(axis, count, *refs):
    token, total = refs[-2:]
    outs = refs[-6:-2]
    value = refs[0][...]
    for ref in refs[1:count]:
        value = value + ref[...]
    total[...] = value
    own = place(axis)
    for d in range(4):
        outs[d][...] = total[own ^ d]
    token[0] = jnp.int32(0)


def spread(axis, terms, after):
    rows = terms[0].shape[0] // 4
    shape = (4, rows, BS)
    *parts, token = pl.pallas_call(
        functools.partial(spread_kernel, axis, len(terms)),
        out_shape=(jax.ShapeDtypeStruct((rows, BS), jnp.float32),) * 4 + (TOKEN,),
        in_specs=[VMEM] * len(terms) + [SMEM] * len(after),
        out_specs=(VMEM,) * 4 + (SMEM,),
        scratch_shapes=[pltpu.VMEM(shape, jnp.float32)],
        name="spread",
    )(*[term.reshape(shape) for term in terms], *after)
    return parts, token


def total_kernel(*refs):
    out, token = refs[-2:]
    out[...] = refs[0][...] + refs[1][...] + refs[2][...] + refs[3][...]
    token[0] = jnp.int32(0)


def total(terms, after):
    return pl.pallas_call(
        total_kernel,
        out_shape=(jax.ShapeDtypeStruct(terms[0].shape, jnp.float32), TOKEN),
        in_specs=[VMEM] * 4 + [SMEM] * len(after),
        out_specs=(VMEM, SMEM),
        name="total",
    )(*terms, *after)


def collect_kernel(axis, own, one, two, three, *rest):
    out, token = rest[-2:]
    at = place(axis)
    for d, source in enumerate((own, one, two, three)):
        out[at ^ d] = source[...]
    token[0] = jnp.int32(0)


def collect(axis, own, others, after):
    rows = own.shape[0]
    out, token = pl.pallas_call(
        functools.partial(collect_kernel, axis),
        out_shape=(jax.ShapeDtypeStruct((4, rows, BS), jnp.float32), TOKEN),
        in_specs=[VMEM] * 4 + [SMEM] * len(after),
        out_specs=(VMEM, SMEM),
        name="collect",
    )(own, *others, *after)
    return out.reshape(4 * rows, BS), token


def join_kernel(own, other, out, token):
    core = lax.axis_index("col") % 2
    out[core] = own[...]
    out[1 - core] = other[...]
    token[0] = jnp.int32(0)


def join(own, other):
    out, token = pl.pallas_call(
        join_kernel,
        out_shape=(jax.ShapeDtypeStruct((2,) + own.shape, jnp.float32), TOKEN),
        in_specs=[VMEM] * 2,
        out_specs=(VMEM, SMEM),
        name="join",
    )(own, other)
    return out.reshape(-1, BS, BS), token


def across(axis, parts):
    if axis == "row":
        return [permute(parts[d - 1], lambda p, q, d=d: (p ^ d, q)) for d in range(1, 4)]
    return [permute(parts[d - 1], lambda p, q, d=d: (p, q ^ (2 * d))) for d in range(1, 4)]


def piece_kernel(n, diag, *rest):
    lowers = rest[:n]
    inverses = rest[n : 2 * n]
    lower_out, inverse_out, token = rest[-3:]
    token[0] = jnp.int32(0)

    def row(i):
        return jnp.concatenate([lowers[j][(i - j) * BS : (i - j + 1) * BS, :] for j in range(n)], axis=1)

    column = []
    for i in range(n, PB):
        value = diag[lower_index(i, n)]
        if n:
            value = value - dot_nt(row(i), row(n))
        column.append(value)
    upper, inverse = factor_block(column[0])
    lower_out[0:BS, :] = upper.T
    if n + 1 < PB:
        lower_out[BS:, :] = dot_nt(jnp.concatenate(column[1:], axis=0), inverse)
    inverse_out[:, n * BS :] = inverse
    if n:
        before = jnp.concatenate(
            [
                jnp.concatenate([inverses[j][...], jnp.zeros((BS, (n - 1 - j) * BS), jnp.float32)], axis=1)
                if j + 1 < n
                else inverses[j][...]
                for j in range(n)
            ],
            axis=0,
        )
        inverse_out[:, : n * BS] = -dot_nn(inverse, dot_nn(row(n), before))


def piece(n, diag, lowers, inverses, after):
    return pl.pallas_call(
        functools.partial(piece_kernel, n),
        out_shape=(
            jax.ShapeDtypeStruct(((PB - n) * BS, BS), jnp.float32),
            jax.ShapeDtypeStruct((BS, (n + 1) * BS), jnp.float32),
            TOKEN,
        ),
        in_specs=[VMEM] * (1 + 2 * n) + [SMEM] * len(after),
        out_specs=(VMEM, VMEM, SMEM),
        compiler_params=pltpu.CompilerParams(vmem_limit_bytes=32 * 2**20),
        cost_estimate=pl.CostEstimate(flops=10**8, bytes_accessed=10**5, transcendentals=0),
        name="factor_piece",
    )(diag, *lowers, *inverses, *after)


def inverse_rows(inverses):
    rows = []
    for j in range(PB):
        if j + 1 < PB:
            rows.append(jnp.concatenate([inverses[j][...], jnp.zeros((BS, (PB - 1 - j) * BS), jnp.float32)], axis=1))
        else:
            rows.append(inverses[j][...])
    return jnp.concatenate(rows, axis=0)


def between_kernel(diag, *rest):
    inverses = rest[:PB]
    cross_out, rest_out = rest[-2:]
    inverse = inverse_rows(inverses)
    one = PB * (PB + 1) // 2
    left = [
        jnp.concatenate([diag[lower_index(i, j) - one] for j in range(PB)], axis=1) for i in range(PB, NC)
    ]
    cross = dot_nt(jnp.concatenate(left, axis=0), inverse)
    cross_out[...] = cross
    for i in range(PB):
        here = cross[i * BS : (i + 1) * BS, :]
        product = dot_nt(here, cross[: (i + 1) * BS, :])
        for j in range(i + 1):
            block = diag[lower_index(i + PB, j + PB) - one]
            rest_out[lower_index(i, j)] = block - product[:, j * BS : (j + 1) * BS]


def between(diag, inverses, after):
    return pl.pallas_call(
        between_kernel,
        out_shape=(
            jax.ShapeDtypeStruct((PB * BS, PB * BS), jnp.float32),
            jax.ShapeDtypeStruct((PB * (PB + 1) // 2, BS, BS), jnp.float32),
        ),
        in_specs=[VMEM] * (1 + PB) + [SMEM] * len(after),
        out_specs=(VMEM, VMEM),
        compiler_params=pltpu.CompilerParams(vmem_limit_bytes=32 * 2**20),
        cost_estimate=pl.CostEstimate(flops=10**8, bytes_accessed=10**5, transcendentals=0),
        name="between",
    )(diag, *inverses, *after)


def finish_kernel(*refs):
    first = inverse_rows(refs[:PB])
    second = inverse_rows(refs[PB : 2 * PB])
    cross = refs[2 * PB][...]
    lowers = refs[2 * PB + 1 : 4 * PB + 1]
    lower_out, high_out, low_out = refs[-3:]
    size = PB * BS
    lower_out[...] = jnp.zeros_like(lower_out)
    for j in range(PB):
        for half in range(2):
            rows = slice(half * size + j * BS, (half + 1) * size)
            lower_out[rows, j * BS : (j + 1) * BS] = lowers[half * PB + j][...]
    high_out[:size, size:] = jnp.zeros((size, size), jnp.bfloat16)
    low_out[:size, size:] = jnp.zeros((size, size), jnp.bfloat16)
    inner = three(nn, *split(cross), *split(first))
    corner = -three(nn, *split(second), *split(inner))
    for value, rows, cols in (
        (first, slice(0, size), slice(0, size)),
        (corner, slice(size, 2 * size), slice(0, size)),
        (second, slice(size, 2 * size), slice(size, 2 * size)),
    ):
        high, low = split(value)
        high_out[rows, cols] = high
        low_out[rows, cols] = low


def finish(first, second, cross, lowers):
    size = NC * BS
    return pl.pallas_call(
        finish_kernel,
        out_shape=(jax.ShapeDtypeStruct((size, size // 2), jnp.float32),)
        + (jax.ShapeDtypeStruct((size, size), jnp.bfloat16),) * 2,
        in_specs=[VMEM] * (4 * PB + 1),
        out_specs=(VMEM,) * 3,
        compiler_params=pltpu.CompilerParams(vmem_limit_bytes=32 * 2**20),
        cost_estimate=pl.CostEstimate(flops=10**8, bytes_accessed=10**5, transcendentals=0),
        name="finish",
    )(*first, *second, cross, *lowers)


def three(dot, a_high, a_low, b_high, b_low):
    kwargs = dict(preferred_element_type=jnp.float32)
    return dot(a_high, b_high, **kwargs) + (dot(a_high, b_low, **kwargs) + dot(a_low, b_high, **kwargs))


def nt(a, b, **kwargs):
    return lax.dot_general(a, b, (((1,), (1,)), ((), ())), **kwargs)


def nn(a, b, **kwargs):
    return lax.dot_general(a, b, (((1,), (0,)), ((), ())), **kwargs)


def masked(tiles, axis, first, second):
    low_part = jnp.concatenate(tiles[:PB], axis=axis)
    high_part = jnp.concatenate(tiles[PB:], axis=axis)
    zero = jnp.zeros_like(low_part)
    return jnp.concatenate([jnp.where(first, low_part, zero), jnp.where(second, high_part, zero)], axis=axis)


def columns_kernel(flags, one, one_more, two, two_more, high_ref, low_ref, col_high, col_low, total):
    size = NC * BS
    half = PB * BS
    width = 2 * BS
    step = pl.program_id(0)
    col_blocks = one.shape[1]
    first_half = step < PB // 2
    for chosen, part, more, column in (
        (first_half, one, one_more, 3),
        (jnp.logical_not(first_half), two, two_more, 4),
    ):
        @pl.when(chosen)
        def _(part=part, more=more, column=column):
            for b in range(col_blocks):
                at = slice(b * BS, (b + 1) * BS)
                raw = jnp.concatenate([part[c, b] + more[c, b] for c in range(2)], axis=0)
                high, low = split(jnp.where(flags[b, column] != 0, raw, jnp.zeros_like(raw)))
                col_high[:width, at] = high
                col_low[:width, at] = low

    high, low = col_high[:width, :], col_low[:width, :]
    for m in range(0, size, width):
        rows = slice(m, m + width)

        @pl.when(step == 0)
        def _(rows=rows):
            total[rows, :] = three(nn, high_ref[rows, :], low_ref[rows, :], high, low)

        if m > 0:
            @pl.when(jnp.logical_and(step > 0, step * width <= m))
            def _(rows=rows):
                total[rows, :] = total[rows, :] + three(nn, high_ref[rows, :], low_ref[rows, :], high, low)

    @pl.when(step == pl.num_programs(0) - 1)
    def _():
        for b in range(col_blocks):
            at = slice(b * BS, (b + 1) * BS)
            for rows, f in ((slice(0, half), 3), (slice(half, size), 4)):
                value = total[rows, at]
                high, low = split(jnp.where(flags[b, f] != 0, value, jnp.zeros_like(value)))
                col_high[rows, at] = high
                col_low[rows, at] = low


def solve_columns(flags, one, one_more, two, two_more, high, low):
    size = NC * BS
    width = 2 * BS
    shape = (size, one.shape[1] * BS)
    first = pl.BlockSpec((2,) + one.shape[1:], lambda i: (jnp.minimum(i, PB // 2 - 1), 0, 0, 0))
    second = pl.BlockSpec((2,) + one.shape[1:], lambda i: (jnp.maximum(i - PB // 2, 0), 0, 0, 0))
    strip = pl.BlockSpec((size, width), lambda i: (0, i))
    whole = pl.BlockSpec(shape, lambda i: (0, 0))
    return pl.pallas_call(
        columns_kernel,
        out_shape=(jax.ShapeDtypeStruct(shape, jnp.bfloat16),) * 2,
        grid=(NC // 2,),
        in_specs=[SMEM, first, first, second, second, strip, strip],
        out_specs=(whole, whole),
        scratch_shapes=[pltpu.VMEM(shape, jnp.float32)],
        compiler_params=pltpu.CompilerParams(vmem_limit_bytes=48 * 2**20),
        name="solve_columns",
    )(flags, one, one_more, two, two_more, high, low)


def update_kernel(flags, front_ref, rows_ref, lower_hbm, high_hbm, low_hbm, col_high_hbm, col_low_hbm, out_ref,
                  solved, sol_high, sol_low, lower_ref, high_ref, low_ref, col_high, col_low, sems):
    size = NC * BS
    half = PB * BS
    width = 2 * BS
    step = pl.program_id(0)
    col_blocks = front_ref.shape[1]
    tall = rows_ref.shape[1]
    index = [step * tall + k for k in range(tall)]
    strips = []
    for m in range(0, size, width):
        rows = slice(m, m + width)
        cols = slice(0, m + width)
        strips.append(
            [
                pltpu.make_async_copy(source.at[rows, cols], target.at[rows, cols], sems.at[len(strips), i])
                for i, (source, target) in enumerate(((high_hbm, high_ref), (low_hbm, low_ref)))
            ]
        )
    last = [
        pltpu.make_async_copy(source, target, sems.at[len(strips) + i // 2, i % 2])
        for i, (source, target) in enumerate(
            ((col_high_hbm, col_high), (col_low_hbm, col_low), (lower_hbm, lower_ref))
        )
    ]

    @pl.when(step == 0)
    def _():
        for copy in sum(strips, []) + last:
            copy.start()

    def wait(copies):
        @pl.when(step == 0)
        def _():
            for copy in copies:
                copy.wait()

    for k, a in enumerate(index):
        raw = masked([rows_ref[c, k] for c in range(NC)], 1, flags[a, 0] != 0, flags[a, 1] != 0)
        high, low = split(raw)
        sol_high[k * BS : (k + 1) * BS, :] = high
        sol_low[k * BS : (k + 1) * BS, :] = low
    for m in range(0, size, width):
        wait(strips[m // width])
        deep = m + width
        value = three(nt, sol_high[:, :deep], sol_low[:, :deep], high_ref[m:deep, :deep], low_ref[m:deep, :deep])
        if m >= half:
            value = jnp.concatenate(
                [jnp.where(flags[a, 1] != 0, value[k * BS : (k + 1) * BS, :], 0.0) for k, a in enumerate(index)],
                axis=0,
            )
        solved[:, m:deep] = value
    high, low = split(solved[...])
    sol_high[...] = high
    sol_low[...] = low
    wait(last)
    for k in range(tall):
        rows = slice(k * BS, (k + 1) * BS)
        value = three(nn, sol_high[rows, :], sol_low[rows, :], col_high[...], col_low[...])
        out_ref[rows] = front_ref[rows] - value.reshape(BS, col_blocks, BS)
    for b in range(col_blocks):
        j = flags[b, 5]

        @pl.when(j >= 0)
        def _(b=b, j=j):
            at = pl.ds(pl.multiple_of(j * BS, BS), BS)
            for k, a in enumerate(index):
                rows = slice(k * BS, (k + 1) * BS)
                listed = jnp.where(j < PB, flags[a, 0], flags[a, 1])
                own = flags[a, 2]

                @pl.when(listed != 0)
                def _(rows=rows):
                    out_ref[rows, b, :] = solved[rows, at]

                @pl.when(jnp.logical_and(own >= 0, own // PB == j // PB))
                def _(rows=rows, own=own):
                    source = pl.ds(pl.multiple_of(own * BS, BS), BS)
                    inside = pl.ds(pl.multiple_of(j % PB * BS, BS), BS)
                    out_ref[rows, b, :] = lower_ref[source, inside]


def update_front(flags, front, rows, lower, high, low, col_high, col_low):
    row_blocks, _, col_blocks = front.shape[:3]
    size = NC * BS
    tall = 2
    block = pl.BlockSpec((tall * BS, col_blocks, BS), lambda i: (i, 0, 0))
    return pl.pallas_call(
        update_kernel,
        out_shape=jax.ShapeDtypeStruct((row_blocks * BS, col_blocks, BS), jnp.float32),
        grid=(row_blocks // tall,),
        in_specs=[SMEM, block, pl.BlockSpec((NC, tall, BS, BS), lambda i: (0, i, 0, 0))] + [HBM] * 5,
        out_specs=block,
        scratch_shapes=[
            pltpu.VMEM((tall * BS, size), jnp.float32),
            pltpu.VMEM((tall * BS, size), jnp.bfloat16),
            pltpu.VMEM((tall * BS, size), jnp.bfloat16),
            pltpu.VMEM(lower.shape, lower.dtype),
            pltpu.VMEM(high.shape, high.dtype),
            pltpu.VMEM(low.shape, low.dtype),
            pltpu.VMEM(col_high.shape, col_high.dtype),
            pltpu.VMEM(col_low.shape, col_low.dtype),
            pltpu.SemaphoreType.DMA((size // (2 * BS) + 2, 2)),
        ],
        compiler_params=pltpu.CompilerParams(vmem_limit_bytes=ALMOST_ALL),
        cost_estimate=pl.CostEstimate(flops=10**9, bytes_accessed=10**6, transcendentals=0),
        name="update_front",
    )(flags, front.reshape(row_blocks * BS, col_blocks, BS), rows, lower, high, low, col_high, col_low)


def block_flags(slots, listed_one, listed_two, diag_slots):
    one = jnp.any(slots[:, None] == listed_one[None, :], axis=1).astype(jnp.int32)
    two = jnp.any(slots[:, None] == listed_two[None, :], axis=1).astype(jnp.int32)
    order = jnp.arange(1, NC + 1, dtype=jnp.int32)
    where = jnp.sum(jnp.where(slots[:, None] == diag_slots[None, :], order[None, :], 0), axis=1) - 1
    return jnp.stack([one, two, where], axis=1)


def gather_summed(front, block_slots, rows_first, rows_second):
    grid_rows, grid_cols = lax.axis_size("row"), lax.axis_size("col")
    own_row, own_col = lax.axis_index("row"), lax.axis_index("col")
    row_blocks, col_blocks = front.shape[0], front.shape[3]
    diag_slots = block_slots[:NC]
    listed_one = block_slots[rows_first]
    listed_two = block_slots[rows_second]
    row_slots = jnp.arange(row_blocks, dtype=jnp.int32) * grid_rows + own_row
    col_slots = jnp.arange(row_blocks, dtype=jnp.int32) * grid_cols + own_col
    flags = jnp.concatenate(
        [block_flags(slots, listed_one, listed_two, diag_slots) for slots in (row_slots, col_slots)], axis=1
    )
    flags = jnp.pad(flags, ((0, 0), (0, 2)))
    local = front.reshape(row_blocks, BS, col_blocks, BS)
    pieces = []
    rows = []
    for c in range(NC):
        piece = lax.dynamic_index_in_dim(local, diag_slots[c] // grid_cols, 2, keepdims=False)
        pieces.append(jnp.where(diag_slots[c] % grid_cols == own_col, piece, jnp.zeros_like(piece)))
        piece = lax.dynamic_index_in_dim(local, diag_slots[c] // grid_rows, 0, keepdims=False)
        rows.append(jnp.where(diag_slots[c] % grid_rows == own_row, piece, jnp.zeros_like(piece)))
    pieces = jnp.stack(pieces, axis=0)
    blocks = []
    for i in range(NC):
        part = lax.dynamic_index_in_dim(pieces, diag_slots[i] // grid_rows, 1, keepdims=False)[: i + 1]
        blocks.append(jnp.where(diag_slots[i] % grid_rows == own_row, part, jnp.zeros_like(part)))
    diag = lax.psum(jnp.concatenate(blocks, axis=0), ("row", "col"))
    return flags, lax.psum(jnp.stack(rows, axis=0), "row"), diag, lax.psum(pieces, "col")


def factor_panel(diag, after, hooks):
    lowers, inverses = [], []
    for n in range(PB):
        lower, inverse, token = piece(n, diag, lowers, inverses, hooks(n, after))
        lowers.append(lower)
        inverses.append(inverse)
        after = [token]
    return lowers, inverses, after


def factor_both(diag, after, hooks):
    lowers, inverses, after = factor_panel(diag, after, hooks[0])
    second, after = hooks[1](after)
    cross, corner = between(second, inverses, after)
    more_lowers, more_inverses, _ = factor_panel(corner, [], lambda n, after: after)
    return finish(inverses, more_inverses, cross, lowers + more_lowers)


def work(front, flags, block_slots, terms, keep, got):
    (own, *parts), token = spread("col", terms, [])
    (own_two, *parts_two), token = spread("row", [keep, got], [token])
    state = {"two": [own_two] + across("row", parts_two)}
    value = [own] + across("col", parts)
    value, _ = total(value, [token])
    value, token = collect("col", value, across("col", [value] * 3), [])
    around = across("row", [value] * 3)
    (own_two, *parts_two), token = spread("col", state["two"], [token])
    state["two"] = [own_two] + across("col", parts_two)
    value, token = collect("row", value, around, [token])
    other = swap_core(value)
    one, two, token = lines(front, block_slots, token)
    got_one = permute(one, lambda p, q: (p ^ 1, q))
    got_two = permute(two, lambda p, q: (p ^ 2, q))
    diag, ready = join(value, other)

    def beside(n, after):
        terms = state["two"]
        if n == 0:
            return [ready, token_lines]
        if n == 1:
            value, token = total(terms, after)
            state["two"] = [value] + across("col", [value] * 3)
        elif n == 2:
            value, token = collect("col", terms[0], terms[1:], after)
            state["two"] = [value] + across("row", [value] * 3)
        else:
            value, token = collect("row", terms[0], terms[1:], after)
            state["two"] = [value, swap_core(value)]
        return [token]

    token_lines = token

    def second(after):
        *sums, token = add_pairs(one, got_one, two, got_two, after[0])
        state["sums"] = sums
        state["more"] = [permute(sums[0], lambda p, q: (p ^ 2, q)), permute(sums[1], lambda p, q: (p ^ 1, q))]
        blocks, _ = join(*state["two"])
        return blocks, [token]

    lower, high, low = factor_both(diag, [], (beside, second))
    (one, two), (more_one, more_two) = state["sums"], state["more"]
    return lower, high, low, *solve_columns(flags, one, more_one, two, more_two, high, low)


def on_device(front, block_slots, rows_first, rows_second):
    if (lax.axis_size("row"), lax.axis_size("col")) != (4, 8):
        flags, cols, diag, panel = gather_summed(front, block_slots, rows_first, rows_second)
        one = PB * (PB + 1) // 2
        hooks = (lambda n, after: after), (lambda after: (diag[one:], after))
        factors = factor_both(diag[:one], [], hooks)
        cols = jnp.swapaxes(cols, 1, 2)
        none = jnp.zeros_like(cols[:PB])
        columns = solve_columns(flags, cols[:PB], none, cols[PB:], none, *factors[1:])
    else:
        flags, token, panel, parts = start(front, block_slots, rows_first, rows_second)
        keep_one, send_one, keep_two, send_two = parts
        panel = lax.psum(panel, "col")
        (own, *others), _ = spread("row", [keep_one, swap_core(send_one)], [])
        terms = [own] + across("row", others)
        run = functools.partial(work, front, flags, block_slots, terms, keep_two, swap_core(send_two))
        shapes = jax.eval_shape(run)
        *factors, col_high, col_low = lax.cond(
            token[0] == 0, run, lambda: tuple(jnp.zeros(x.shape, x.dtype) for x in shapes)
        )
        columns = col_high, col_low
    out = update_front(flags, local_blocks(front), panel, *factors, *columns)
    return out.reshape(front.shape)


def local_blocks(front):
    return front.reshape(front.shape[0], BS, front.shape[3], BS)


def solution(mesh):
    placed = (P(None, "row", None, None, "col", None), P(), P(), P())
    return jax.shard_map(
        on_device,
        mesh=mesh,
        in_specs=placed,
        out_specs=P(None, "row", None, None, "col", None),
        check_vma=False,
    )
```

```python
import functools

import jax
import jax.numpy as jnp
from jax import lax
from jax.experimental import pallas as pl
from jax.experimental.pallas import tpu as pltpu
from jax.sharding import PartitionSpec as P

BS = 128
PB = 4
NC = 2 * PB
STEP = 8
ALMOST_ALL = 63 * 2**20
HIGHEST = lax.Precision.HIGHEST
HBM = pl.BlockSpec(memory_space=pltpu.HBM)
VMEM = pl.BlockSpec(memory_space=pltpu.VMEM)
SMEM = pl.BlockSpec(memory_space=pltpu.SMEM)


def lane_copy(tile, lane):
    return jnp.broadcast_to(tile[:, lane : lane + 1], tile.shape)


def row_copy(tile, row):
    return jnp.broadcast_to(tile[row : row + 1, :], tile.shape)


def factor_block(block):
    tiles = BS // 8
    sub = lax.broadcasted_iota(jnp.int32, (8, BS), 0)
    lanes = lax.broadcasted_iota(jnp.int32, (8, BS), 1)
    left = [block[8 * i : 8 * i + 8, :] for i in range(tiles)]
    right = [jnp.where(lanes == sub + 8 * i, 1.0, 0.0).astype(jnp.float32) for i in range(tiles)]
    upper = []
    inverse = []
    for j in range(0, BS, STEP):
        g, o = divmod(j, 8)
        if o == 0:
            upper_tile = jnp.zeros((8, BS), jnp.float32)
            inverse_tile = jnp.zeros((8, BS), jnp.float32)
        rows = [row_copy(left[g], o + s) for s in range(STEP)]
        extra = [row_copy(right[g], o + s) for s in range(STEP)]
        first = g if o + STEP < 8 else g + 1
        cols = {i: [lane_copy(left[i], j + s) for s in range(STEP)] for i in range(first, tiles)}
        pivot = [[lane_copy(rows[s], j + t) if t >= s else None for t in range(STEP)] for s in range(STEP)]
        ratio = [[None] * STEP for _ in range(STEP)]
        recip = []
        for s in range(STEP):
            inv = 1.0 / pivot[s][s]
            recip.append(inv)
            for t in range(s + 1, STEP):
                ratio[s][t] = pivot[s][t] * inv
            for t in range(s + 1, STEP):
                for u in range(t, STEP):
                    pivot[t][u] = pivot[t][u] - ratio[s][t] * pivot[s][u]
                rows[t] = rows[t] - ratio[s][t] * rows[s]
                extra[t] = extra[t] - ratio[s][t] * extra[s]
        for s in range(STEP):
            scale = lax.rsqrt(pivot[s][s])
            scale = scale * (1.5 - 0.5 * pivot[s][s] * scale * scale)
            here = sub == o + s
            upper_tile = jnp.where(here, rows[s] * scale, upper_tile)
            inverse_tile = jnp.where(here, extra[s] * scale, inverse_tile)
        if o + STEP == 8:
            upper.append(jnp.where(lanes >= sub + 8 * g, upper_tile, 0.0))
            inverse.append(jnp.where(lanes <= sub + 8 * g, inverse_tile, 0.0))
        for s in reversed(range(STEP)):
            rows[s] = rows[s] * recip[s]
            extra[s] = extra[s] * recip[s]
            for t in range(s + 1, STEP):
                rows[s] = rows[s] - ratio[s][t] * rows[t]
                extra[s] = extra[s] - ratio[s][t] * extra[t]
        for i in range(first, tiles):
            less = cols[i][0] * rows[0]
            less_extra = cols[i][0] * extra[0]
            for s in range(1, STEP):
                less = less + cols[i][s] * rows[s]
                less_extra = less_extra + cols[i][s] * extra[s]
            if i == g:
                below = sub >= o + STEP
                left[i] = jnp.where(below, left[i] - less, left[i])
                right[i] = jnp.where(below, right[i] - less_extra, right[i])
            else:
                left[i] = left[i] - less
                right[i] = right[i] - less_extra
    return jnp.concatenate(upper, axis=0), jnp.concatenate(inverse, axis=0)


def lower_index(i, j):
    return i * (i + 1) // 2 + j


def dot_nt(a, b):
    return lax.dot_general(a, b, (((1,), (1,)), ((), ())), precision=HIGHEST, preferred_element_type=jnp.float32)


def dot_nn(a, b):
    return lax.dot_general(a, b, (((1,), (0,)), ((), ())), precision=HIGHEST, preferred_element_type=jnp.float32)


def split(x):
    high = x.astype(jnp.bfloat16)
    return high, (x - high.astype(jnp.float32)).astype(jnp.bfloat16)


def place(count, core, block):
    half = count // 2
    return (block // half) == core, block % half


def start_kernel(slots, first, second, front_ref, flags, token, panel, keep_one, send_one, keep_two, send_two,
                 zero, blocks, columns, sems, out_sems):
    row_blocks, _, col_blocks = front_ref.shape[:3]
    grid_rows, grid_cols = 4, 8
    own_row = lax.axis_index("row")
    own_col = lax.axis_index("col")
    core = own_col % 2
    slot = [slots[i] for i in range(NC)]
    one = PB * (PB + 1) // 2
    moves = []
    fills = []

    def move(condition, source, middle, targets):
        index = len(moves)

        @pl.when(condition)
        def _():
            pltpu.make_async_copy(source, middle, sems.at[index]).start()

        moves.append((condition, middle, targets, index))

    always = core >= 0
    group = zero.shape[0]
    for c in range(NC):
        owned = slot[c] % grid_cols == own_col
        for a in range(0, row_blocks, group):
            fills.append((jnp.logical_not(owned), zero, panel.at[c, a : a + group], len(moves)))
        move(owned, front_ref.at[:, :, slot[c] // grid_cols], columns.at[c], ((panel.at[c], always),))
    for i in range(NC):
        for j in range(i + 1):
            block = lower_index(i, j)
            if i < PB:
                half, at, keep, send = one // 2, block, keep_one, send_one
            else:
                half, at, keep, send = keep_two.shape[0], block - one, keep_two, send_two
            a = slot[i] // grid_rows
            b = slot[j] // grid_cols
            owned = jnp.logical_and(slot[i] % grid_rows == own_row, slot[j] % grid_cols == own_col)
            stay = core == at // half
            targets = ((keep.at[at % half], stay), (send.at[at % half], jnp.logical_not(stay)))
            for target, chosen in targets:
                fills.append((jnp.logical_and(chosen, jnp.logical_not(owned)), zero.at[0], target, len(moves)))
            move(owned, front_ref.at[a, :, b], blocks.at[block], targets)

    zero[...] = jnp.zeros_like(zero)
    for condition, source, target, index in fills:
        @pl.when(condition)
        def _(source=source, target=target, index=index):
            pltpu.make_async_copy(source, target, out_sems.at[index]).start()

    for a in range(row_blocks):
        for f in range(8):
            flags[a, f] = jnp.int32(-1 if f in (2, 5) else 0)
    for c in range(NC):
        @pl.when(slot[c] % grid_rows == own_row)
        def _(c=c):
            flags[slot[c] // grid_rows, 2] = jnp.int32(c)

        @pl.when(slot[c] % grid_cols == own_col)
        def _(c=c):
            flags[slot[c] // grid_cols, 5] = jnp.int32(c)

    for listed, f in ((first, 0), (second, 1)):
        @pl.loop(0, listed.shape[0])
        def _(i, listed=listed, f=f):
            s = slots[listed[i]]

            @pl.when(s % grid_rows == own_row)
            def _():
                flags[s // grid_rows, f] = jnp.int32(1)

            @pl.when(s % grid_cols == own_col)
            def _():
                flags[s // grid_cols, 3 + f] = jnp.int32(1)

    token[0] = jnp.int32(0)
    for condition, middle, targets, index in moves:
        @pl.when(condition)
        def _(middle=middle, targets=targets, index=index):
            pltpu.make_async_copy(middle, middle, sems.at[index]).wait()
            for target, chosen in targets:
                @pl.when(chosen)
                def _(target=target):
                    pltpu.make_async_copy(middle, target, out_sems.at[index]).start()
    for condition, middle, targets, index in moves:
        pltpu.make_async_copy(middle, middle, out_sems.at[index]).wait()


TOKEN = jax.ShapeDtypeStruct((1,), jnp.int32)


def start(front, block_slots, rows_first, rows_second):
    row_blocks, col_blocks = front.shape[0], front.shape[3]
    one = PB * (PB + 1) // 2
    count = NC * (NC + 1) // 2
    two = count - one
    f32 = lambda *shape: jax.ShapeDtypeStruct(shape, jnp.float32)
    flags, token, panel, *parts = pl.pallas_call(
        start_kernel,
        out_shape=(
            jax.ShapeDtypeStruct((row_blocks, 8), jnp.int32),
            TOKEN,
            f32(NC, row_blocks, BS, 1, BS),
            f32(one // 2, BS, 1, BS),
            f32(one // 2, BS, 1, BS),
            f32(two // 2, BS, 1, BS),
            f32(two // 2, BS, 1, BS),
        ),
        in_specs=[SMEM, SMEM, SMEM, HBM],
        out_specs=(SMEM, SMEM) + (HBM,) * 5,
        scratch_shapes=[
            pltpu.VMEM((row_blocks // 4, BS, 1, BS), jnp.float32),
            pltpu.VMEM((count, BS, 1, BS), jnp.float32),
            pltpu.VMEM((NC, row_blocks, BS, 1, BS), jnp.float32),
            pltpu.SemaphoreType.DMA((count + NC,)),
            pltpu.SemaphoreType.DMA((count + NC,)),
        ],
        compiler_params=pltpu.CompilerParams(vmem_limit_bytes=ALMOST_ALL),
        name="start",
    )(block_slots, rows_first, rows_second, front.reshape(row_blocks, BS, col_blocks, 1, BS))
    return flags, token, panel.reshape(NC, row_blocks, BS, BS), [x.reshape(-1, BS) for x in parts]


def lines_kernel(slots, after, wide_ref, one, two, token, zero, lines, sems, out_sems):
    own_row = lax.axis_index("row")
    col_blocks = wide_ref.shape[2]
    owned = [slots[c] % 4 == own_row for c in range(NC)]
    targets = [(one if c < PB else two).at[c % PB] for c in range(NC)]
    for c in range(NC):
        @pl.when(owned[c])
        def _(c=c):
            for b in range(col_blocks):
                pltpu.make_async_copy(wide_ref.at[slots[c] // 4, :, b], lines.at[c, b], sems.at[c]).start()
    zero[...] = jnp.zeros_like(zero)
    group = zero.shape[0]
    for c in range(NC):
        @pl.when(jnp.logical_not(owned[c]))
        def _(c=c):
            for b in range(0, col_blocks, group):
                pltpu.make_async_copy(zero, targets[c].at[b : b + group], out_sems.at[c]).start()
    for c in range(NC):
        @pl.when(owned[c])
        def _(c=c):
            pltpu.make_async_copy(lines.at[c], lines.at[c], sems.at[c]).wait()
            pltpu.make_async_copy(lines.at[c], targets[c], out_sems.at[c]).start()
    token[0] = jnp.int32(0)
    for c in range(NC):
        pltpu.make_async_copy(lines.at[c], targets[c], out_sems.at[c]).wait()


def lines(front, block_slots, after):
    row_blocks, col_blocks = front.shape[0], front.shape[3]
    part = jax.ShapeDtypeStruct((PB, col_blocks, BS, 1, BS), jnp.float32)
    one, two, token = pl.pallas_call(
        lines_kernel,
        out_shape=(part, part, TOKEN),
        in_specs=[SMEM, SMEM, HBM],
        out_specs=(HBM, HBM, SMEM),
        scratch_shapes=[
            pltpu.VMEM((2, BS, 1, BS), jnp.float32),
            pltpu.VMEM((NC, col_blocks, BS, 1, BS), jnp.float32),
            pltpu.SemaphoreType.DMA((NC,)),
            pltpu.SemaphoreType.DMA((NC,)),
        ],
        compiler_params=pltpu.CompilerParams(vmem_limit_bytes=ALMOST_ALL),
        name="lines",
    )(block_slots, after, front.reshape(row_blocks, BS, col_blocks, 1, BS))
    shape = (PB, col_blocks, BS, BS)
    return one.reshape(shape), two.reshape(shape), token


def add_kernel(after, a, b, c, d, first, second, token):
    first[...] = a[...] + b[...]
    second[...] = c[...] + d[...]

    @pl.when(pl.program_id(0) == 0)
    def _():
        token[0] = jnp.int32(0)


def add_pairs(a, b, c, d, after):
    block = pl.BlockSpec((1,) + a.shape[1:], lambda i: (i,) + (0,) * (a.ndim - 1))
    return pl.pallas_call(
        add_kernel,
        out_shape=(jax.ShapeDtypeStruct(a.shape, a.dtype),) * 2 + (TOKEN,),
        grid=(a.shape[0],),
        in_specs=[SMEM] + [block] * 4,
        out_specs=(block, block, SMEM),
        name="add_pairs",
    )(after, a, b, c, d)


def permute(value, flip):
    pairs = []
    for p in range(4):
        for q in range(8):
            to_p, to_q = flip(p, q)
            if 0 <= to_q < 8:
                pairs.append((p * 8 + q, to_p * 8 + to_q))
    return lax.ppermute(value, ("row", "col"), pairs)


def swap_core(value):
    return permute(value, lambda p, q: (p, q ^ 1))


def place(axis):
    return lax.axis_index("row") if axis == "row" else lax.axis_index("col") // 2


def spread_kernel(axis, count, *refs):
    token, total = refs[-2:]
    outs = refs[-6:-2]
    value = refs[0][...]
    for ref in refs[1:count]:
        value = value + ref[...]
    total[...] = value
    own = place(axis)
    for d in range(4):
        outs[d][...] = total[own ^ d]
    token[0] = jnp.int32(0)


def spread(axis, terms, after):
    rows = terms[0].shape[0] // 4
    shape = (4, rows, BS)
    *parts, token = pl.pallas_call(
        functools.partial(spread_kernel, axis, len(terms)),
        out_shape=(jax.ShapeDtypeStruct((rows, BS), jnp.float32),) * 4 + (TOKEN,),
        in_specs=[VMEM] * len(terms) + [SMEM] * len(after),
        out_specs=(VMEM,) * 4 + (SMEM,),
        scratch_shapes=[pltpu.VMEM(shape, jnp.float32)],
        name="spread",
    )(*[term.reshape(shape) for term in terms], *after)
    return parts, token


def total_kernel(*refs):
    out, token = refs[-2:]
    out[...] = refs[0][...] + refs[1][...] + refs[2][...] + refs[3][...]
    token[0] = jnp.int32(0)


def total(terms, after):
    return pl.pallas_call(
        total_kernel,
        out_shape=(jax.ShapeDtypeStruct(terms[0].shape, jnp.float32), TOKEN),
        in_specs=[VMEM] * 4 + [SMEM] * len(after),
        out_specs=(VMEM, SMEM),
        name="total",
    )(*terms, *after)


def collect_kernel(axis, own, one, two, three, *rest):
    out, token = rest[-2:]
    at = place(axis)
    for d, source in enumerate((own, one, two, three)):
        out[at ^ d] = source[...]
    token[0] = jnp.int32(0)


def collect(axis, own, others, after):
    rows = own.shape[0]
    out, token = pl.pallas_call(
        functools.partial(collect_kernel, axis),
        out_shape=(jax.ShapeDtypeStruct((4, rows, BS), jnp.float32), TOKEN),
        in_specs=[VMEM] * 4 + [SMEM] * len(after),
        out_specs=(VMEM, SMEM),
        name="collect",
    )(own, *others, *after)
    return out.reshape(4 * rows, BS), token


def join_kernel(own, other, out, token):
    core = lax.axis_index("col") % 2
    out[core] = own[...]
    out[1 - core] = other[...]
    token[0] = jnp.int32(0)


def join(own, other):
    out, token = pl.pallas_call(
        join_kernel,
        out_shape=(jax.ShapeDtypeStruct((2,) + own.shape, jnp.float32), TOKEN),
        in_specs=[VMEM] * 2,
        out_specs=(VMEM, SMEM),
        name="join",
    )(own, other)
    return out.reshape(-1, BS, BS), token


def across(axis, parts):
    if axis == "row":
        return [permute(parts[d - 1], lambda p, q, d=d: (p ^ d, q)) for d in range(1, 4)]
    return [permute(parts[d - 1], lambda p, q, d=d: (p, q ^ (2 * d))) for d in range(1, 4)]


def piece_kernel(n, diag, *rest):
    lowers = rest[:n]
    inverses = rest[n : 2 * n]
    lower_out, inverse_out, token = rest[-3:]
    token[0] = jnp.int32(0)

    def row(i):
        return jnp.concatenate([lowers[j][(i - j) * BS : (i - j + 1) * BS, :] for j in range(n)], axis=1)

    column = []
    for i in range(n, PB):
        value = diag[lower_index(i, n)]
        if n:
            value = value - dot_nt(row(i), row(n))
        column.append(value)
    upper, inverse = factor_block(column[0])
    lower_out[0:BS, :] = upper.T
    if n + 1 < PB:
        lower_out[BS:, :] = dot_nt(jnp.concatenate(column[1:], axis=0), inverse)
    inverse_out[:, n * BS :] = inverse
    if n:
        before = jnp.concatenate(
            [
                jnp.concatenate([inverses[j][...], jnp.zeros((BS, (n - 1 - j) * BS), jnp.float32)], axis=1)
                if j + 1 < n
                else inverses[j][...]
                for j in range(n)
            ],
            axis=0,
        )
        inverse_out[:, : n * BS] = -dot_nn(inverse, dot_nn(row(n), before))


def piece(n, diag, lowers, inverses, after):
    return pl.pallas_call(
        functools.partial(piece_kernel, n),
        out_shape=(
            jax.ShapeDtypeStruct(((PB - n) * BS, BS), jnp.float32),
            jax.ShapeDtypeStruct((BS, (n + 1) * BS), jnp.float32),
            TOKEN,
        ),
        in_specs=[VMEM] * (1 + 2 * n) + [SMEM] * len(after),
        out_specs=(VMEM, VMEM, SMEM),
        compiler_params=pltpu.CompilerParams(vmem_limit_bytes=32 * 2**20),
        cost_estimate=pl.CostEstimate(flops=10**8, bytes_accessed=10**5, transcendentals=0),
        name="factor_piece",
    )(diag, *lowers, *inverses, *after)


def inverse_rows(inverses):
    rows = []
    for j in range(PB):
        if j + 1 < PB:
            rows.append(jnp.concatenate([inverses[j][...], jnp.zeros((BS, (PB - 1 - j) * BS), jnp.float32)], axis=1))
        else:
            rows.append(inverses[j][...])
    return jnp.concatenate(rows, axis=0)


def between_kernel(diag, *rest):
    inverses = rest[:PB]
    cross_out, rest_out = rest[-2:]
    inverse = inverse_rows(inverses)
    one = PB * (PB + 1) // 2
    left = [
        jnp.concatenate([diag[lower_index(i, j) - one] for j in range(PB)], axis=1) for i in range(PB, NC)
    ]
    cross = dot_nt(jnp.concatenate(left, axis=0), inverse)
    cross_out[...] = cross
    for i in range(PB):
        here = cross[i * BS : (i + 1) * BS, :]
        product = dot_nt(here, cross[: (i + 1) * BS, :])
        for j in range(i + 1):
            block = diag[lower_index(i + PB, j + PB) - one]
            rest_out[lower_index(i, j)] = block - product[:, j * BS : (j + 1) * BS]


def between(diag, inverses, after):
    return pl.pallas_call(
        between_kernel,
        out_shape=(
            jax.ShapeDtypeStruct((PB * BS, PB * BS), jnp.float32),
            jax.ShapeDtypeStruct((PB * (PB + 1) // 2, BS, BS), jnp.float32),
        ),
        in_specs=[VMEM] * (1 + PB) + [SMEM] * len(after),
        out_specs=(VMEM, VMEM),
        compiler_params=pltpu.CompilerParams(vmem_limit_bytes=32 * 2**20),
        cost_estimate=pl.CostEstimate(flops=10**8, bytes_accessed=10**5, transcendentals=0),
        name="between",
    )(diag, *inverses, *after)


def finish_kernel(*refs):
    first = inverse_rows(refs[:PB])
    second = inverse_rows(refs[PB : 2 * PB])
    cross = refs[2 * PB][...]
    lowers = refs[2 * PB + 1 : 4 * PB + 1]
    lower_out, high_out, low_out = refs[-3:]
    size = PB * BS
    lower_out[...] = jnp.zeros_like(lower_out)
    for j in range(PB):
        for half in range(2):
            rows = slice(half * size + j * BS, (half + 1) * size)
            lower_out[rows, j * BS : (j + 1) * BS] = lowers[half * PB + j][...]
    high_out[:size, size:] = jnp.zeros((size, size), jnp.bfloat16)
    low_out[:size, size:] = jnp.zeros((size, size), jnp.bfloat16)
    inner = three(nn, *split(cross), *split(first))
    corner = -three(nn, *split(second), *split(inner))
    for value, rows, cols in (
        (first, slice(0, size), slice(0, size)),
        (corner, slice(size, 2 * size), slice(0, size)),
        (second, slice(size, 2 * size), slice(size, 2 * size)),
    ):
        high, low = split(value)
        high_out[rows, cols] = high
        low_out[rows, cols] = low


def finish(first, second, cross, lowers):
    size = NC * BS
    return pl.pallas_call(
        finish_kernel,
        out_shape=(jax.ShapeDtypeStruct((size, size // 2), jnp.float32),)
        + (jax.ShapeDtypeStruct((size, size), jnp.bfloat16),) * 2,
        in_specs=[VMEM] * (4 * PB + 1),
        out_specs=(VMEM,) * 3,
        compiler_params=pltpu.CompilerParams(vmem_limit_bytes=32 * 2**20),
        cost_estimate=pl.CostEstimate(flops=10**8, bytes_accessed=10**5, transcendentals=0),
        name="finish",
    )(*first, *second, cross, *lowers)


def three(dot, a_high, a_low, b_high, b_low):
    kwargs = dict(preferred_element_type=jnp.float32)
    return dot(a_high, b_high, **kwargs) + (dot(a_high, b_low, **kwargs) + dot(a_low, b_high, **kwargs))


def nt(a, b, **kwargs):
    return lax.dot_general(a, b, (((1,), (1,)), ((), ())), **kwargs)


def nn(a, b, **kwargs):
    return lax.dot_general(a, b, (((1,), (0,)), ((), ())), **kwargs)


def masked(tiles, axis, first, second):
    low_part = jnp.concatenate(tiles[:PB], axis=axis)
    high_part = jnp.concatenate(tiles[PB:], axis=axis)
    zero = jnp.zeros_like(low_part)
    return jnp.concatenate([jnp.where(first, low_part, zero), jnp.where(second, high_part, zero)], axis=axis)


def columns_kernel(flags, one, one_more, two, two_more, high_ref, low_ref, col_high, col_low, raw_high, raw_low):
    size = NC * BS
    half = PB * BS
    width = 2 * BS
    col_blocks = one.shape[1]
    for b in range(col_blocks):
        at = slice(b * BS, (b + 1) * BS)
        tiles = [one[c, b] + one_more[c, b] for c in range(PB)] + [two[c, b] + two_more[c, b] for c in range(PB)]
        high, low = split(masked(tiles, 0, flags[b, 3] != 0, flags[b, 4] != 0))
        raw_high[:, at] = high
        raw_low[:, at] = low
    for m in range(0, size, width):
        deep = m + width
        both = jnp.concatenate([high_ref[m:deep, :deep], low_ref[m:deep, :deep]], axis=0)
        value = stacked(nn, both, raw_high[:deep, :], raw_low[:deep, :])
        if m >= half:
            value = jnp.concatenate(
                [jnp.where(flags[b, 4] != 0, value[:, b * BS : (b + 1) * BS], 0.0) for b in range(col_blocks)],
                axis=1,
            )
        high, low = split(value)
        col_high[m:deep, :] = high
        col_low[m:deep, :] = low


def solve_columns(flags, one, one_more, two, two_more, high, low):
    size = NC * BS
    shape = (size, one.shape[1] * BS)
    return pl.pallas_call(
        columns_kernel,
        out_shape=(jax.ShapeDtypeStruct(shape, jnp.bfloat16),) * 2,
        in_specs=[SMEM] + [VMEM] * 6,
        out_specs=(VMEM, VMEM),
        scratch_shapes=[pltpu.VMEM(shape, jnp.bfloat16), pltpu.VMEM(shape, jnp.bfloat16)],
        compiler_params=pltpu.CompilerParams(vmem_limit_bytes=ALMOST_ALL),
        name="solve_columns",
    )(flags, one, one_more, two, two_more, high, low)


def stacked(dot, both, high, low):
    rows = both.shape[0] // 2
    first = dot(both, high, preferred_element_type=jnp.float32)
    return first[:rows] + (first[rows:] + dot(both[:rows], low, preferred_element_type=jnp.float32))


def update_kernel(flags, front_ref, rows_ref, lower_ref, high_ref, low_ref, col_high, col_low, out_ref,
                  solved, stack):
    size = NC * BS
    half = PB * BS
    width = 2 * BS
    step = pl.program_id(0)
    col_blocks = front_ref.shape[1]
    tall = rows_ref.shape[1]
    index = [step * tall + k for k in range(tall)]
    for k, a in enumerate(index):
        raw = masked([rows_ref[c, k] for c in range(NC)], 1, flags[a, 0] != 0, flags[a, 1] != 0)
        high, low = split(raw)
        stack[k * BS : (k + 1) * BS, :] = high
        stack[(tall + k) * BS : (tall + k + 1) * BS, :] = low
    for m in range(0, size, width):
        deep = m + width
        value = stacked(nt, stack[:, :deep], high_ref[m:deep, :deep], low_ref[m:deep, :deep])
        if m >= half:
            value = jnp.concatenate(
                [jnp.where(flags[a, 1] != 0, value[k * BS : (k + 1) * BS, :], 0.0) for k, a in enumerate(index)],
                axis=0,
            )
        solved[:, m:deep] = value
    high, low = split(solved[...])
    stack[: tall * BS, :] = high
    stack[tall * BS :, :] = low
    value = stacked(nn, stack[...], col_high[...], col_low[...])
    out_ref[...] = front_ref[...] - value.reshape(tall * BS, col_blocks, BS)
    for b in range(col_blocks):
        j = flags[b, 5]

        @pl.when(j >= 0)
        def _(b=b, j=j):
            at = pl.ds(pl.multiple_of(j * BS, BS), BS)
            for k, a in enumerate(index):
                rows = slice(k * BS, (k + 1) * BS)
                listed = jnp.where(j < PB, flags[a, 0], flags[a, 1])
                own = flags[a, 2]

                @pl.when(listed != 0)
                def _(rows=rows):
                    out_ref[rows, b, :] = solved[rows, at]

                @pl.when(jnp.logical_and(own >= 0, own // PB == j // PB))
                def _(rows=rows, own=own):
                    source = pl.ds(pl.multiple_of(own * BS, BS), BS)
                    inside = pl.ds(pl.multiple_of(j % PB * BS, BS), BS)
                    out_ref[rows, b, :] = lower_ref[source, inside]


def update_front(flags, front, rows, lower, high, low, col_high, col_low):
    row_blocks, _, col_blocks = front.shape[:3]
    size = NC * BS
    tall = 2
    block = pl.BlockSpec((tall * BS, col_blocks, BS), lambda i: (i, 0, 0))
    return pl.pallas_call(
        update_kernel,
        out_shape=jax.ShapeDtypeStruct((row_blocks * BS, col_blocks, BS), jnp.float32),
        grid=(row_blocks // tall,),
        in_specs=[SMEM, block, pl.BlockSpec((NC, tall, BS, BS), lambda i: (0, i, 0, 0))] + [VMEM] * 5,
        out_specs=block,
        scratch_shapes=[
            pltpu.VMEM((tall * BS, size), jnp.float32),
            pltpu.VMEM((2 * tall * BS, size), jnp.bfloat16),
        ],
        compiler_params=pltpu.CompilerParams(vmem_limit_bytes=ALMOST_ALL),
        cost_estimate=pl.CostEstimate(flops=10**9, bytes_accessed=10**6, transcendentals=0),
        name="update_front",
    )(flags, front.reshape(row_blocks * BS, col_blocks, BS), rows, lower, high, low, col_high, col_low)


def block_flags(slots, listed_one, listed_two, diag_slots):
    one = jnp.any(slots[:, None] == listed_one[None, :], axis=1).astype(jnp.int32)
    two = jnp.any(slots[:, None] == listed_two[None, :], axis=1).astype(jnp.int32)
    order = jnp.arange(1, NC + 1, dtype=jnp.int32)
    where = jnp.sum(jnp.where(slots[:, None] == diag_slots[None, :], order[None, :], 0), axis=1) - 1
    return jnp.stack([one, two, where], axis=1)


def gather_summed(front, block_slots, rows_first, rows_second):
    grid_rows, grid_cols = lax.axis_size("row"), lax.axis_size("col")
    own_row, own_col = lax.axis_index("row"), lax.axis_index("col")
    row_blocks, col_blocks = front.shape[0], front.shape[3]
    diag_slots = block_slots[:NC]
    listed_one = block_slots[rows_first]
    listed_two = block_slots[rows_second]
    row_slots = jnp.arange(row_blocks, dtype=jnp.int32) * grid_rows + own_row
    col_slots = jnp.arange(row_blocks, dtype=jnp.int32) * grid_cols + own_col
    flags = jnp.concatenate(
        [block_flags(slots, listed_one, listed_two, diag_slots) for slots in (row_slots, col_slots)], axis=1
    )
    flags = jnp.pad(flags, ((0, 0), (0, 2)))
    local = front.reshape(row_blocks, BS, col_blocks, BS)
    pieces = []
    rows = []
    for c in range(NC):
        piece = lax.dynamic_index_in_dim(local, diag_slots[c] // grid_cols, 2, keepdims=False)
        pieces.append(jnp.where(diag_slots[c] % grid_cols == own_col, piece, jnp.zeros_like(piece)))
        piece = lax.dynamic_index_in_dim(local, diag_slots[c] // grid_rows, 0, keepdims=False)
        rows.append(jnp.where(diag_slots[c] % grid_rows == own_row, piece, jnp.zeros_like(piece)))
    pieces = jnp.stack(pieces, axis=0)
    blocks = []
    for i in range(NC):
        part = lax.dynamic_index_in_dim(pieces, diag_slots[i] // grid_rows, 1, keepdims=False)[: i + 1]
        blocks.append(jnp.where(diag_slots[i] % grid_rows == own_row, part, jnp.zeros_like(part)))
    diag = lax.psum(jnp.concatenate(blocks, axis=0), ("row", "col"))
    return flags, lax.psum(jnp.stack(rows, axis=0), "row"), diag, lax.psum(pieces, "col")


def factor_panel(diag, after, hooks):
    lowers, inverses = [], []
    for n in range(PB):
        lower, inverse, token = piece(n, diag, lowers, inverses, hooks(n, after))
        lowers.append(lower)
        inverses.append(inverse)
        after = [token]
    return lowers, inverses, after


def factor_both(diag, after, hooks):
    lowers, inverses, after = factor_panel(diag, after, hooks[0])
    second, after = hooks[1](after)
    cross, corner = between(second, inverses, after)
    more_lowers, more_inverses, _ = factor_panel(corner, [], lambda n, after: after)
    return finish(inverses, more_inverses, cross, lowers + more_lowers)


def work(front, flags, block_slots, terms, keep, got):
    (own, *parts), token = spread("col", terms, [])
    (own_two, *parts_two), token = spread("row", [keep, got], [token])
    state = {"two": [own_two] + across("row", parts_two)}
    value = [own] + across("col", parts)
    value, _ = total(value, [token])
    value, token = collect("col", value, across("col", [value] * 3), [])
    around = across("row", [value] * 3)
    (own_two, *parts_two), token = spread("col", state["two"], [token])
    state["two"] = [own_two] + across("col", parts_two)
    value, token = collect("row", value, around, [token])
    other = swap_core(value)
    one, two, token = lines(front, block_slots, token)
    got_one = permute(one, lambda p, q: (p ^ 1, q))
    got_two = permute(two, lambda p, q: (p ^ 2, q))
    diag, ready = join(value, other)

    def beside(n, after):
        terms = state["two"]
        if n == 0:
            return [ready, token_lines]
        if n == 1:
            value, token = total(terms, after)
            state["two"] = [value] + across("col", [value] * 3)
        elif n == 2:
            value, token = collect("col", terms[0], terms[1:], after)
            state["two"] = [value] + across("row", [value] * 3)
        else:
            value, token = collect("row", terms[0], terms[1:], after)
            state["two"] = [value, swap_core(value)]
        return [token]

    token_lines = token

    def second(after):
        *sums, token = add_pairs(one, got_one, two, got_two, after[0])
        state["sums"] = sums
        state["more"] = [permute(sums[0], lambda p, q: (p ^ 2, q)), permute(sums[1], lambda p, q: (p ^ 1, q))]
        blocks, _ = join(*state["two"])
        return blocks, [token]

    lower, high, low = factor_both(diag, [], (beside, second))
    (one, two), (more_one, more_two) = state["sums"], state["more"]
    return lower, high, low, *solve_columns(flags, one, more_one, two, more_two, high, low)


def on_device(front, block_slots, rows_first, rows_second):
    if (lax.axis_size("row"), lax.axis_size("col")) != (4, 8):
        flags, cols, diag, panel = gather_summed(front, block_slots, rows_first, rows_second)
        one = PB * (PB + 1) // 2
        hooks = (lambda n, after: after), (lambda after: (diag[one:], after))
        factors = factor_both(diag[:one], [], hooks)
        cols = jnp.swapaxes(cols, 1, 2)
        none = jnp.zeros_like(cols[:PB])
        columns = solve_columns(flags, cols[:PB], none, cols[PB:], none, *factors[1:])
    else:
        flags, token, panel, parts = start(front, block_slots, rows_first, rows_second)
        keep_one, send_one, keep_two, send_two = parts
        panel = lax.psum(panel, "col")
        (own, *others), _ = spread("row", [keep_one, swap_core(send_one)], [])
        terms = [own] + across("row", others)
        run = functools.partial(work, front, flags, block_slots, terms, keep_two, swap_core(send_two))
        shapes = jax.eval_shape(run)
        *factors, col_high, col_low = lax.cond(
            token[0] == 0, run, lambda: tuple(jnp.zeros(x.shape, x.dtype) for x in shapes)
        )
        columns = col_high, col_low
    out = update_front(flags, local_blocks(front), panel, *factors, *columns)
    return out.reshape(front.shape)


def local_blocks(front):
    return front.reshape(front.shape[0], BS, front.shape[3], BS)


def solution(mesh):
    placed = (P(None, "row", None, None, "col", None), P(), P(), P())
    return jax.shard_map(
        on_device,
        mesh=mesh,
        in_specs=placed,
        out_specs=P(None, "row", None, None, "col", None),
        check_vma=False,
    )
```

```python
import functools

import jax
import jax.numpy as jnp
from jax import lax
from jax.experimental import pallas as pl
from jax.experimental.pallas import tpu as pltpu
from jax.sharding import PartitionSpec as P

BS = 128
PB = 4
NC = 2 * PB
STEP = 8
ALMOST_ALL = 63 * 2**20
HIGHEST = lax.Precision.HIGHEST
HBM = pl.BlockSpec(memory_space=pltpu.HBM)
VMEM = pl.BlockSpec(memory_space=pltpu.VMEM)
SMEM = pl.BlockSpec(memory_space=pltpu.SMEM)


def lane_copy(tile, lane):
    return jnp.broadcast_to(tile[:, lane : lane + 1], tile.shape)


def row_copy(tile, row):
    return jnp.broadcast_to(tile[row : row + 1, :], tile.shape)


def factor_block(block):
    tiles = BS // 8
    sub = lax.broadcasted_iota(jnp.int32, (8, BS), 0)
    lanes = lax.broadcasted_iota(jnp.int32, (8, BS), 1)
    left = [block[8 * i : 8 * i + 8, :] for i in range(tiles)]
    right = [jnp.where(lanes == sub + 8 * i, 1.0, 0.0).astype(jnp.float32) for i in range(tiles)]
    upper = []
    inverse = []
    for j in range(0, BS, STEP):
        g, o = divmod(j, 8)
        if o == 0:
            upper_tile = jnp.zeros((8, BS), jnp.float32)
            inverse_tile = jnp.zeros((8, BS), jnp.float32)
        rows = [row_copy(left[g], o + s) for s in range(STEP)]
        extra = [row_copy(right[g], o + s) for s in range(STEP)]
        first = g if o + STEP < 8 else g + 1
        cols = {i: [lane_copy(left[i], j + s) for s in range(STEP)] for i in range(first, tiles)}
        pivot = [[lane_copy(rows[s], j + t) if t >= s else None for t in range(STEP)] for s in range(STEP)]
        ratio = [[None] * STEP for _ in range(STEP)]
        recip = []
        for s in range(STEP):
            inv = 1.0 / pivot[s][s]
            recip.append(inv)
            for t in range(s + 1, STEP):
                ratio[s][t] = pivot[s][t] * inv
            for t in range(s + 1, STEP):
                for u in range(t, STEP):
                    pivot[t][u] = pivot[t][u] - ratio[s][t] * pivot[s][u]
                rows[t] = rows[t] - ratio[s][t] * rows[s]
                extra[t] = extra[t] - ratio[s][t] * extra[s]
        for s in range(STEP):
            scale = lax.rsqrt(pivot[s][s])
            scale = scale * (1.5 - 0.5 * pivot[s][s] * scale * scale)
            here = sub == o + s
            upper_tile = jnp.where(here, rows[s] * scale, upper_tile)
            inverse_tile = jnp.where(here, extra[s] * scale, inverse_tile)
        if o + STEP == 8:
            upper.append(jnp.where(lanes >= sub + 8 * g, upper_tile, 0.0))
            inverse.append(jnp.where(lanes <= sub + 8 * g, inverse_tile, 0.0))
        for s in reversed(range(STEP)):
            rows[s] = rows[s] * recip[s]
            extra[s] = extra[s] * recip[s]
            for t in range(s + 1, STEP):
                rows[s] = rows[s] - ratio[s][t] * rows[t]
                extra[s] = extra[s] - ratio[s][t] * extra[t]
        for i in range(first, tiles):
            less = cols[i][0] * rows[0]
            less_extra = cols[i][0] * extra[0]
            for s in range(1, STEP):
                less = less + cols[i][s] * rows[s]
                less_extra = less_extra + cols[i][s] * extra[s]
            if i == g:
                below = sub >= o + STEP
                left[i] = jnp.where(below, left[i] - less, left[i])
                right[i] = jnp.where(below, right[i] - less_extra, right[i])
            else:
                left[i] = left[i] - less
                right[i] = right[i] - less_extra
    return jnp.concatenate(upper, axis=0), jnp.concatenate(inverse, axis=0)


def lower_index(i, j):
    return i * (i + 1) // 2 + j


def dot_nt(a, b):
    return lax.dot_general(a, b, (((1,), (1,)), ((), ())), precision=HIGHEST, preferred_element_type=jnp.float32)


def dot_nn(a, b):
    return lax.dot_general(a, b, (((1,), (0,)), ((), ())), precision=HIGHEST, preferred_element_type=jnp.float32)


def split(x):
    high = x.astype(jnp.bfloat16)
    return high, (x - high.astype(jnp.float32)).astype(jnp.bfloat16)


def place(count, core, block):
    half = count // 2
    return (block // half) == core, block % half


def start_kernel(slots, first, second, front_ref, flags, token, panel, keep_one, send_one, keep_two, send_two,
                 zero, blocks, columns, sems, out_sems):
    row_blocks, _, col_blocks = front_ref.shape[:3]
    grid_rows, grid_cols = 4, 8
    own_row = lax.axis_index("row")
    own_col = lax.axis_index("col")
    core = own_col % 2
    slot = [slots[i] for i in range(NC)]
    one = PB * (PB + 1) // 2
    moves = []
    fills = []

    def move(condition, source, middle, targets):
        index = len(moves)

        @pl.when(condition)
        def _():
            pltpu.make_async_copy(source, middle, sems.at[index]).start()

        moves.append((condition, middle, targets, index))

    always = core >= 0
    group = zero.shape[0]
    for c in range(NC):
        owned = slot[c] % grid_cols == own_col
        for a in range(0, row_blocks, group):
            fills.append((jnp.logical_not(owned), zero, panel.at[c, a : a + group], len(moves)))
        move(owned, front_ref.at[:, :, slot[c] // grid_cols], columns.at[c], ((panel.at[c], always),))
    for i in range(NC):
        for j in range(i + 1):
            block = lower_index(i, j)
            if i < PB:
                half, at, keep, send = one // 2, block, keep_one, send_one
            else:
                half, at, keep, send = keep_two.shape[0], block - one, keep_two, send_two
            a = slot[i] // grid_rows
            b = slot[j] // grid_cols
            owned = jnp.logical_and(slot[i] % grid_rows == own_row, slot[j] % grid_cols == own_col)
            stay = core == at // half
            targets = ((keep.at[at % half], stay), (send.at[at % half], jnp.logical_not(stay)))
            for target, chosen in targets:
                fills.append((jnp.logical_and(chosen, jnp.logical_not(owned)), zero.at[0], target, len(moves)))
            move(owned, front_ref.at[a, :, b], blocks.at[block], targets)

    zero[...] = jnp.zeros_like(zero)
    for condition, source, target, index in fills:
        @pl.when(condition)
        def _(source=source, target=target, index=index):
            pltpu.make_async_copy(source, target, out_sems.at[index]).start()

    for a in range(row_blocks):
        for f in range(8):
            flags[a, f] = jnp.int32(-1 if f in (2, 5) else 0)
    for c in range(NC):
        @pl.when(slot[c] % grid_rows == own_row)
        def _(c=c):
            flags[slot[c] // grid_rows, 2] = jnp.int32(c)

        @pl.when(slot[c] % grid_cols == own_col)
        def _(c=c):
            flags[slot[c] // grid_cols, 5] = jnp.int32(c)

    for listed, f in ((first, 0), (second, 1)):
        @pl.loop(0, listed.shape[0])
        def _(i, listed=listed, f=f):
            s = slots[listed[i]]

            @pl.when(s % grid_rows == own_row)
            def _():
                flags[s // grid_rows, f] = jnp.int32(1)

            @pl.when(s % grid_cols == own_col)
            def _():
                flags[s // grid_cols, 3 + f] = jnp.int32(1)

    token[0] = jnp.int32(0)
    for condition, middle, targets, index in moves:
        @pl.when(condition)
        def _(middle=middle, targets=targets, index=index):
            pltpu.make_async_copy(middle, middle, sems.at[index]).wait()
            for target, chosen in targets:
                @pl.when(chosen)
                def _(target=target):
                    pltpu.make_async_copy(middle, target, out_sems.at[index]).start()
    for condition, middle, targets, index in moves:
        pltpu.make_async_copy(middle, middle, out_sems.at[index]).wait()


TOKEN = jax.ShapeDtypeStruct((1,), jnp.int32)


def start(front, block_slots, rows_first, rows_second):
    row_blocks, col_blocks = front.shape[0], front.shape[3]
    one = PB * (PB + 1) // 2
    count = NC * (NC + 1) // 2
    two = count - one
    f32 = lambda *shape: jax.ShapeDtypeStruct(shape, jnp.float32)
    flags, token, panel, *parts = pl.pallas_call(
        start_kernel,
        out_shape=(
            jax.ShapeDtypeStruct((row_blocks, 8), jnp.int32),
            TOKEN,
            f32(NC, row_blocks, BS, 1, BS),
            f32(one // 2, BS, 1, BS),
            f32(one // 2, BS, 1, BS),
            f32(two // 2, BS, 1, BS),
            f32(two // 2, BS, 1, BS),
        ),
        in_specs=[SMEM, SMEM, SMEM, HBM],
        out_specs=(SMEM, SMEM) + (HBM,) * 5,
        scratch_shapes=[
            pltpu.VMEM((row_blocks // 4, BS, 1, BS), jnp.float32),
            pltpu.VMEM((count, BS, 1, BS), jnp.float32),
            pltpu.VMEM((NC, row_blocks, BS, 1, BS), jnp.float32),
            pltpu.SemaphoreType.DMA((count + NC,)),
            pltpu.SemaphoreType.DMA((count + NC,)),
        ],
        compiler_params=pltpu.CompilerParams(vmem_limit_bytes=ALMOST_ALL),
        name="start",
    )(block_slots, rows_first, rows_second, front.reshape(row_blocks, BS, col_blocks, 1, BS))
    return flags, token, panel.reshape(NC, row_blocks, BS, BS), [x.reshape(-1, BS) for x in parts]


def lines_kernel(slots, after, wide_ref, one, two, token, zero, lines, sems, out_sems):
    own_row = lax.axis_index("row")
    col_blocks = wide_ref.shape[2]
    owned = [slots[c] % 4 == own_row for c in range(NC)]
    targets = [(one if c < PB else two).at[c % PB] for c in range(NC)]
    for c in range(NC):
        @pl.when(owned[c])
        def _(c=c):
            for b in range(col_blocks):
                pltpu.make_async_copy(wide_ref.at[slots[c] // 4, :, b], lines.at[c, b], sems.at[c]).start()
    zero[...] = jnp.zeros_like(zero)
    group = zero.shape[0]
    for c in range(NC):
        @pl.when(jnp.logical_not(owned[c]))
        def _(c=c):
            for b in range(0, col_blocks, group):
                pltpu.make_async_copy(zero, targets[c].at[b : b + group], out_sems.at[c]).start()
    for c in range(NC):
        @pl.when(owned[c])
        def _(c=c):
            pltpu.make_async_copy(lines.at[c], lines.at[c], sems.at[c]).wait()
            pltpu.make_async_copy(lines.at[c], targets[c], out_sems.at[c]).start()
    token[0] = jnp.int32(0)
    for c in range(NC):
        pltpu.make_async_copy(lines.at[c], targets[c], out_sems.at[c]).wait()


def lines(front, block_slots, after):
    row_blocks, col_blocks = front.shape[0], front.shape[3]
    part = jax.ShapeDtypeStruct((PB, col_blocks, BS, 1, BS), jnp.float32)
    one, two, token = pl.pallas_call(
        lines_kernel,
        out_shape=(part, part, TOKEN),
        in_specs=[SMEM, SMEM, HBM],
        out_specs=(HBM, HBM, SMEM),
        scratch_shapes=[
            pltpu.VMEM((2, BS, 1, BS), jnp.float32),
            pltpu.VMEM((NC, col_blocks, BS, 1, BS), jnp.float32),
            pltpu.SemaphoreType.DMA((NC,)),
            pltpu.SemaphoreType.DMA((NC,)),
        ],
        compiler_params=pltpu.CompilerParams(vmem_limit_bytes=ALMOST_ALL),
        name="lines",
    )(block_slots, after, front.reshape(row_blocks, BS, col_blocks, 1, BS))
    shape = (PB, col_blocks, BS, BS)
    return one.reshape(shape), two.reshape(shape), token


def add_kernel(after, a, b, c, d, first, second, token):
    first[...] = a[...] + b[...]
    second[...] = c[...] + d[...]

    @pl.when(pl.program_id(0) == 0)
    def _():
        token[0] = jnp.int32(0)


def add_pairs(a, b, c, d, after):
    block = pl.BlockSpec((1,) + a.shape[1:], lambda i: (i,) + (0,) * (a.ndim - 1))
    return pl.pallas_call(
        add_kernel,
        out_shape=(jax.ShapeDtypeStruct(a.shape, a.dtype),) * 2 + (TOKEN,),
        grid=(a.shape[0],),
        in_specs=[SMEM] + [block] * 4,
        out_specs=(block, block, SMEM),
        name="add_pairs",
    )(after, a, b, c, d)


def permute(value, flip):
    pairs = []
    for p in range(4):
        for q in range(8):
            to_p, to_q = flip(p, q)
            if 0 <= to_q < 8:
                pairs.append((p * 8 + q, to_p * 8 + to_q))
    return lax.ppermute(value, ("row", "col"), pairs)


def swap_core(value):
    return permute(value, lambda p, q: (p, q ^ 1))


def place(axis):
    return lax.axis_index("row") if axis == "row" else lax.axis_index("col") // 2


def spread_kernel(axis, count, *refs):
    token, total = refs[-2:]
    outs = refs[-6:-2]
    value = refs[0][...]
    for ref in refs[1:count]:
        value = value + ref[...]
    total[...] = value
    own = place(axis)
    for d in range(4):
        outs[d][...] = total[own ^ d]
    token[0] = jnp.int32(0)


def spread(axis, terms, after):
    rows = terms[0].shape[0] // 4
    shape = (4, rows, BS)
    *parts, token = pl.pallas_call(
        functools.partial(spread_kernel, axis, len(terms)),
        out_shape=(jax.ShapeDtypeStruct((rows, BS), jnp.float32),) * 4 + (TOKEN,),
        in_specs=[VMEM] * len(terms) + [SMEM] * len(after),
        out_specs=(VMEM,) * 4 + (SMEM,),
        scratch_shapes=[pltpu.VMEM(shape, jnp.float32)],
        name="spread",
    )(*[term.reshape(shape) for term in terms], *after)
    return parts, token


def total_kernel(*refs):
    out, token = refs[-2:]
    out[...] = refs[0][...] + refs[1][...] + refs[2][...] + refs[3][...]
    token[0] = jnp.int32(0)


def total(terms, after):
    return pl.pallas_call(
        total_kernel,
        out_shape=(jax.ShapeDtypeStruct(terms[0].shape, jnp.float32), TOKEN),
        in_specs=[VMEM] * 4 + [SMEM] * len(after),
        out_specs=(VMEM, SMEM),
        name="total",
    )(*terms, *after)


def collect_kernel(axis, own, one, two, three, *rest):
    out, token = rest[-2:]
    at = place(axis)
    for d, source in enumerate((own, one, two, three)):
        out[at ^ d] = source[...]
    token[0] = jnp.int32(0)


def collect(axis, own, others, after):
    rows = own.shape[0]
    out, token = pl.pallas_call(
        functools.partial(collect_kernel, axis),
        out_shape=(jax.ShapeDtypeStruct((4, rows, BS), jnp.float32), TOKEN),
        in_specs=[VMEM] * 4 + [SMEM] * len(after),
        out_specs=(VMEM, SMEM),
        name="collect",
    )(own, *others, *after)
    return out.reshape(4 * rows, BS), token


def join_kernel(own, other, out, token):
    core = lax.axis_index("col") % 2
    out[core] = own[...]
    out[1 - core] = other[...]
    token[0] = jnp.int32(0)


def join(own, other):
    out, token = pl.pallas_call(
        join_kernel,
        out_shape=(jax.ShapeDtypeStruct((2,) + own.shape, jnp.float32), TOKEN),
        in_specs=[VMEM] * 2,
        out_specs=(VMEM, SMEM),
        name="join",
    )(own, other)
    return out.reshape(-1, BS, BS), token


def across(axis, parts):
    if axis == "row":
        return [permute(parts[d - 1], lambda p, q, d=d: (p ^ d, q)) for d in range(1, 4)]
    return [permute(parts[d - 1], lambda p, q, d=d: (p, q ^ (2 * d))) for d in range(1, 4)]


def piece_kernel(n, diag, *rest):
    lowers = rest[:n]
    inverses = rest[n : 2 * n]
    lower_out, inverse_out, token = rest[-3:]
    token[0] = jnp.int32(0)

    def row(i):
        return jnp.concatenate([lowers[j][(i - j) * BS : (i - j + 1) * BS, :] for j in range(n)], axis=1)

    column = []
    for i in range(n, PB):
        value = diag[lower_index(i, n)]
        if n:
            value = value - dot_nt(row(i), row(n))
        column.append(value)
    upper, inverse = factor_block(column[0])
    lower_out[0:BS, :] = upper.T
    if n + 1 < PB:
        lower_out[BS:, :] = dot_nt(jnp.concatenate(column[1:], axis=0), inverse)
    inverse_out[:, n * BS :] = inverse
    if n:
        before = jnp.concatenate(
            [
                jnp.concatenate([inverses[j][...], jnp.zeros((BS, (n - 1 - j) * BS), jnp.float32)], axis=1)
                if j + 1 < n
                else inverses[j][...]
                for j in range(n)
            ],
            axis=0,
        )
        inverse_out[:, : n * BS] = -dot_nn(inverse, dot_nn(row(n), before))


def piece(n, diag, lowers, inverses, after):
    return pl.pallas_call(
        functools.partial(piece_kernel, n),
        out_shape=(
            jax.ShapeDtypeStruct(((PB - n) * BS, BS), jnp.float32),
            jax.ShapeDtypeStruct((BS, (n + 1) * BS), jnp.float32),
            TOKEN,
        ),
        in_specs=[VMEM] * (1 + 2 * n) + [SMEM] * len(after),
        out_specs=(VMEM, VMEM, SMEM),
        compiler_params=pltpu.CompilerParams(vmem_limit_bytes=32 * 2**20),
        cost_estimate=pl.CostEstimate(flops=10**8, bytes_accessed=10**5, transcendentals=0),
        name="factor_piece",
    )(diag, *lowers, *inverses, *after)


def inverse_rows(inverses):
    rows = []
    for j in range(PB):
        if j + 1 < PB:
            rows.append(jnp.concatenate([inverses[j][...], jnp.zeros((BS, (PB - 1 - j) * BS), jnp.float32)], axis=1))
        else:
            rows.append(inverses[j][...])
    return jnp.concatenate(rows, axis=0)


def between_kernel(diag, *rest):
    inverses = rest[:PB]
    cross_out, rest_out = rest[-2:]
    inverse = inverse_rows(inverses)
    one = PB * (PB + 1) // 2
    left = [
        jnp.concatenate([diag[lower_index(i, j) - one] for j in range(PB)], axis=1) for i in range(PB, NC)
    ]
    cross = dot_nt(jnp.concatenate(left, axis=0), inverse)
    cross_out[...] = cross
    for i in range(PB):
        here = cross[i * BS : (i + 1) * BS, :]
        product = dot_nt(here, cross[: (i + 1) * BS, :])
        for j in range(i + 1):
            block = diag[lower_index(i + PB, j + PB) - one]
            rest_out[lower_index(i, j)] = block - product[:, j * BS : (j + 1) * BS]


def between(diag, inverses, after):
    return pl.pallas_call(
        between_kernel,
        out_shape=(
            jax.ShapeDtypeStruct((PB * BS, PB * BS), jnp.float32),
            jax.ShapeDtypeStruct((PB * (PB + 1) // 2, BS, BS), jnp.float32),
        ),
        in_specs=[VMEM] * (1 + PB) + [SMEM] * len(after),
        out_specs=(VMEM, VMEM),
        compiler_params=pltpu.CompilerParams(vmem_limit_bytes=32 * 2**20),
        cost_estimate=pl.CostEstimate(flops=10**8, bytes_accessed=10**5, transcendentals=0),
        name="between",
    )(diag, *inverses, *after)


def finish_kernel(*refs):
    first = inverse_rows(refs[:PB])
    second = inverse_rows(refs[PB : 2 * PB])
    cross = refs[2 * PB][...]
    lowers = refs[2 * PB + 1 : 4 * PB + 1]
    lower_out, high_out, low_out = refs[-3:]
    size = PB * BS
    lower_out[...] = jnp.zeros_like(lower_out)
    for j in range(PB):
        for half in range(2):
            rows = slice(half * size + j * BS, (half + 1) * size)
            lower_out[rows, j * BS : (j + 1) * BS] = lowers[half * PB + j][...]
    high_out[:size, size:] = jnp.zeros((size, size), jnp.bfloat16)
    low_out[:size, size:] = jnp.zeros((size, size), jnp.bfloat16)
    inner = three(nn, *split(cross), *split(first))
    corner = -three(nn, *split(second), *split(inner))
    for value, rows, cols in (
        (first, slice(0, size), slice(0, size)),
        (corner, slice(size, 2 * size), slice(0, size)),
        (second, slice(size, 2 * size), slice(size, 2 * size)),
    ):
        high, low = split(value)
        high_out[rows, cols] = high
        low_out[rows, cols] = low


def finish(first, second, cross, lowers):
    size = NC * BS
    return pl.pallas_call(
        finish_kernel,
        out_shape=(jax.ShapeDtypeStruct((size, size // 2), jnp.float32),)
        + (jax.ShapeDtypeStruct((size, size), jnp.bfloat16),) * 2,
        in_specs=[VMEM] * (4 * PB + 1),
        out_specs=(VMEM,) * 3,
        compiler_params=pltpu.CompilerParams(vmem_limit_bytes=32 * 2**20),
        cost_estimate=pl.CostEstimate(flops=10**8, bytes_accessed=10**5, transcendentals=0),
        name="finish",
    )(*first, *second, cross, *lowers)


def three(dot, a_high, a_low, b_high, b_low):
    kwargs = dict(preferred_element_type=jnp.float32)
    return dot(a_high, b_high, **kwargs) + (dot(a_high, b_low, **kwargs) + dot(a_low, b_high, **kwargs))


def nt(a, b, **kwargs):
    return lax.dot_general(a, b, (((1,), (1,)), ((), ())), **kwargs)


def nn(a, b, **kwargs):
    return lax.dot_general(a, b, (((1,), (0,)), ((), ())), **kwargs)


def masked(tiles, axis, first, second):
    low_part = jnp.concatenate(tiles[:PB], axis=axis)
    high_part = jnp.concatenate(tiles[PB:], axis=axis)
    zero = jnp.zeros_like(low_part)
    return jnp.concatenate([jnp.where(first, low_part, zero), jnp.where(second, high_part, zero)], axis=axis)


def columns_kernel(flags, one, one_more, two, two_more, high_ref, low_ref, col_high, col_low, raw_high, raw_low):
    size = NC * BS
    half = PB * BS
    width = 2 * BS
    col_blocks = one.shape[1]
    for b in range(col_blocks):
        at = slice(b * BS, (b + 1) * BS)
        tiles = [one[c, b] + one_more[c, b] for c in range(PB)] + [two[c, b] + two_more[c, b] for c in range(PB)]
        high, low = split(masked(tiles, 0, flags[b, 3] != 0, flags[b, 4] != 0))
        raw_high[:, at] = high
        raw_low[:, at] = low
    for m in range(0, size, width):
        deep = m + width
        both = jnp.concatenate([high_ref[m:deep, :deep], low_ref[m:deep, :deep]], axis=0)
        value = stacked(nn, both, raw_high[:deep, :], raw_low[:deep, :])
        if m >= half:
            value = jnp.concatenate(
                [jnp.where(flags[b, 4] != 0, value[:, b * BS : (b + 1) * BS], 0.0) for b in range(col_blocks)],
                axis=1,
            )
        high, low = split(value)
        col_high[m:deep, :] = high
        col_low[m:deep, :] = low


def solve_columns(flags, one, one_more, two, two_more, high, low):
    size = NC * BS
    shape = (size, one.shape[1] * BS)
    return pl.pallas_call(
        columns_kernel,
        out_shape=(jax.ShapeDtypeStruct(shape, jnp.bfloat16),) * 2,
        in_specs=[SMEM] + [VMEM] * 6,
        out_specs=(VMEM, VMEM),
        scratch_shapes=[pltpu.VMEM(shape, jnp.bfloat16), pltpu.VMEM(shape, jnp.bfloat16)],
        compiler_params=pltpu.CompilerParams(vmem_limit_bytes=ALMOST_ALL),
        name="solve_columns",
    )(flags, one, one_more, two, two_more, high, low)


def stacked(dot, both, high, low):
    rows = both.shape[0] // 2
    first = dot(both, high, preferred_element_type=jnp.float32)
    return first[:rows] + (first[rows:] + dot(both[:rows], low, preferred_element_type=jnp.float32))


def update_kernel(flags, front_ref, rows_ref, lower_ref, high_ref, low_ref, col_high, col_low, out_ref,
                  solved, stack):
    size = NC * BS
    half = PB * BS
    width = 2 * BS
    step = pl.program_id(0)
    col_blocks = front_ref.shape[1]
    tall = rows_ref.shape[1]
    index = [step * tall + k for k in range(tall)]
    for k, a in enumerate(index):
        rows = slice(k * BS, (k + 1) * BS)
        first = flags[a, 0] != 0
        second = flags[a, 1] != 0

        def solve_and_subtract(begin, k=k, rows=rows, second=second):
            tiles = [rows_ref[c, k] for c in range(begin // BS, NC)]
            if begin == 0:
                raw = masked(tiles, 1, True, second)
            else:
                raw = jnp.concatenate(tiles, axis=1)
            depth = size - begin
            high, low = split(raw)
            stack[:BS, :depth] = high
            stack[BS:, :depth] = low
            for m in range(begin, size, width):
                deep = m + width
                value = stacked(
                    nt, stack[:, : deep - begin], high_ref[m:deep, begin:deep], low_ref[m:deep, begin:deep]
                )
                if begin < half <= m:
                    value = jnp.where(second, value, jnp.zeros_like(value))
                solved[rows, m:deep] = value
            high, low = split(solved[rows, begin:])
            stack[:BS, :depth] = high
            stack[BS:, :depth] = low
            value = stacked(nn, stack[:, :depth], col_high[begin:, :], col_low[begin:, :])
            out_ref[rows] = front_ref[rows] - value.reshape(BS, col_blocks, BS)

        @pl.when(first)
        def _():
            solve_and_subtract(0)

        @pl.when(jnp.logical_and(jnp.logical_not(first), second))
        def _():
            solve_and_subtract(half)

        @pl.when(jnp.logical_not(jnp.logical_or(first, second)))
        def _(rows=rows):
            out_ref[rows] = front_ref[rows]

    for b in range(col_blocks):
        j = flags[b, 5]

        @pl.when(j >= 0)
        def _(b=b, j=j):
            at = pl.ds(pl.multiple_of(j * BS, BS), BS)
            for k, a in enumerate(index):
                rows = slice(k * BS, (k + 1) * BS)
                listed = jnp.where(j < PB, flags[a, 0], flags[a, 1])
                own = flags[a, 2]

                @pl.when(listed != 0)
                def _(rows=rows):
                    out_ref[rows, b, :] = solved[rows, at]

                @pl.when(jnp.logical_and(own >= 0, own // PB == j // PB))
                def _(rows=rows, own=own):
                    source = pl.ds(pl.multiple_of(own * BS, BS), BS)
                    inside = pl.ds(pl.multiple_of(j % PB * BS, BS), BS)
                    out_ref[rows, b, :] = lower_ref[source, inside]


def update_front(flags, front, rows, lower, high, low, col_high, col_low):
    row_blocks, _, col_blocks = front.shape[:3]
    size = NC * BS
    tall = 2
    block = pl.BlockSpec((tall * BS, col_blocks, BS), lambda i: (i, 0, 0))
    return pl.pallas_call(
        update_kernel,
        out_shape=jax.ShapeDtypeStruct((row_blocks * BS, col_blocks, BS), jnp.float32),
        grid=(row_blocks // tall,),
        in_specs=[SMEM, block, pl.BlockSpec((NC, tall, BS, BS), lambda i: (0, i, 0, 0))] + [VMEM] * 5,
        out_specs=block,
        scratch_shapes=[
            pltpu.VMEM((tall * BS, size), jnp.float32),
            pltpu.VMEM((2 * BS, size), jnp.bfloat16),
        ],
        compiler_params=pltpu.CompilerParams(vmem_limit_bytes=ALMOST_ALL),
        cost_estimate=pl.CostEstimate(flops=10**9, bytes_accessed=10**6, transcendentals=0),
        name="update_front",
    )(flags, front.reshape(row_blocks * BS, col_blocks, BS), rows, lower, high, low, col_high, col_low)


def block_flags(slots, listed_one, listed_two, diag_slots):
    one = jnp.any(slots[:, None] == listed_one[None, :], axis=1).astype(jnp.int32)
    two = jnp.any(slots[:, None] == listed_two[None, :], axis=1).astype(jnp.int32)
    order = jnp.arange(1, NC + 1, dtype=jnp.int32)
    where = jnp.sum(jnp.where(slots[:, None] == diag_slots[None, :], order[None, :], 0), axis=1) - 1
    return jnp.stack([one, two, where], axis=1)


def gather_summed(front, block_slots, rows_first, rows_second):
    grid_rows, grid_cols = lax.axis_size("row"), lax.axis_size("col")
    own_row, own_col = lax.axis_index("row"), lax.axis_index("col")
    row_blocks, col_blocks = front.shape[0], front.shape[3]
    diag_slots = block_slots[:NC]
    listed_one = block_slots[rows_first]
    listed_two = block_slots[rows_second]
    row_slots = jnp.arange(row_blocks, dtype=jnp.int32) * grid_rows + own_row
    col_slots = jnp.arange(row_blocks, dtype=jnp.int32) * grid_cols + own_col
    flags = jnp.concatenate(
        [block_flags(slots, listed_one, listed_two, diag_slots) for slots in (row_slots, col_slots)], axis=1
    )
    flags = jnp.pad(flags, ((0, 0), (0, 2)))
    local = front.reshape(row_blocks, BS, col_blocks, BS)
    pieces = []
    rows = []
    for c in range(NC):
        piece = lax.dynamic_index_in_dim(local, diag_slots[c] // grid_cols, 2, keepdims=False)
        pieces.append(jnp.where(diag_slots[c] % grid_cols == own_col, piece, jnp.zeros_like(piece)))
        piece = lax.dynamic_index_in_dim(local, diag_slots[c] // grid_rows, 0, keepdims=False)
        rows.append(jnp.where(diag_slots[c] % grid_rows == own_row, piece, jnp.zeros_like(piece)))
    pieces = jnp.stack(pieces, axis=0)
    blocks = []
    for i in range(NC):
        part = lax.dynamic_index_in_dim(pieces, diag_slots[i] // grid_rows, 1, keepdims=False)[: i + 1]
        blocks.append(jnp.where(diag_slots[i] % grid_rows == own_row, part, jnp.zeros_like(part)))
    diag = lax.psum(jnp.concatenate(blocks, axis=0), ("row", "col"))
    return flags, lax.psum(jnp.stack(rows, axis=0), "row"), diag, lax.psum(pieces, "col")


def factor_panel(diag, after, hooks):
    lowers, inverses = [], []
    for n in range(PB):
        lower, inverse, token = piece(n, diag, lowers, inverses, hooks(n, after))
        lowers.append(lower)
        inverses.append(inverse)
        after = [token]
    return lowers, inverses, after


def factor_both(diag, after, hooks):
    lowers, inverses, after = factor_panel(diag, after, hooks[0])
    second, after = hooks[1](after)
    cross, corner = between(second, inverses, after)
    more_lowers, more_inverses, _ = factor_panel(corner, [], lambda n, after: after)
    return finish(inverses, more_inverses, cross, lowers + more_lowers)


def work(front, flags, block_slots, terms, keep, got):
    (own, *parts), token = spread("col", terms, [])
    (own_two, *parts_two), token = spread("row", [keep, got], [token])
    state = {"two": [own_two] + across("row", parts_two)}
    value = [own] + across("col", parts)
    value, _ = total(value, [token])
    value, token = collect("col", value, across("col", [value] * 3), [])
    around = across("row", [value] * 3)
    (own_two, *parts_two), token = spread("col", state["two"], [token])
    state["two"] = [own_two] + across("col", parts_two)
    value, token = collect("row", value, around, [token])
    other = swap_core(value)
    one, two, token = lines(front, block_slots, token)
    got_one = permute(one, lambda p, q: (p ^ 1, q))
    got_two = permute(two, lambda p, q: (p ^ 2, q))
    diag, ready = join(value, other)

    def beside(n, after):
        terms = state["two"]
        if n == 0:
            return [ready, token_lines]
        if n == 1:
            value, token = total(terms, after)
            state["two"] = [value] + across("col", [value] * 3)
        elif n == 2:
            value, token = collect("col", terms[0], terms[1:], after)
            state["two"] = [value] + across("row", [value] * 3)
        else:
            value, token = collect("row", terms[0], terms[1:], after)
            state["two"] = [value, swap_core(value)]
        return [token]

    token_lines = token

    def second(after):
        *sums, token = add_pairs(one, got_one, two, got_two, after[0])
        state["sums"] = sums
        state["more"] = [permute(sums[0], lambda p, q: (p ^ 2, q)), permute(sums[1], lambda p, q: (p ^ 1, q))]
        blocks, _ = join(*state["two"])
        return blocks, [token]

    lower, high, low = factor_both(diag, [], (beside, second))
    (one, two), (more_one, more_two) = state["sums"], state["more"]
    return lower, high, low, *solve_columns(flags, one, more_one, two, more_two, high, low)


def on_device(front, block_slots, rows_first, rows_second):
    if (lax.axis_size("row"), lax.axis_size("col")) != (4, 8):
        flags, cols, diag, panel = gather_summed(front, block_slots, rows_first, rows_second)
        one = PB * (PB + 1) // 2
        hooks = (lambda n, after: after), (lambda after: (diag[one:], after))
        factors = factor_both(diag[:one], [], hooks)
        cols = jnp.swapaxes(cols, 1, 2)
        none = jnp.zeros_like(cols[:PB])
        columns = solve_columns(flags, cols[:PB], none, cols[PB:], none, *factors[1:])
    else:
        flags, token, panel, parts = start(front, block_slots, rows_first, rows_second)
        keep_one, send_one, keep_two, send_two = parts
        panel = lax.psum(panel, "col")
        (own, *others), _ = spread("row", [keep_one, swap_core(send_one)], [])
        terms = [own] + across("row", others)
        run = functools.partial(work, front, flags, block_slots, terms, keep_two, swap_core(send_two))
        shapes = jax.eval_shape(run)
        *factors, col_high, col_low = lax.cond(
            token[0] == 0, run, lambda: tuple(jnp.zeros(x.shape, x.dtype) for x in shapes)
        )
        columns = col_high, col_low
    out = update_front(flags, local_blocks(front), panel, *factors, *columns)
    return out.reshape(front.shape)


def local_blocks(front):
    return front.reshape(front.shape[0], BS, front.shape[3], BS)


def solution(mesh):
    placed = (P(None, "row", None, None, "col", None), P(), P(), P())
    return jax.shard_map(
        on_device,
        mesh=mesh,
        in_specs=placed,
        out_specs=P(None, "row", None, None, "col", None),
        check_vma=False,
    )
```
